256 devices in a mesh: gx: 16 (over y, x_hi, core), gy: 8 (over z), ga: 2 (over x_lo).
Axes of the slice: x: 4 (x_hi: 2, x_lo: 2; x = x_hi * 2 + x_lo), y: 4, z: 8, core: 2. Of those that a mesh axis runs over, the one named last changes fastest.
Arguments:
- velocity: float32 [2, 256, 1024], P(None, 'gx', 'gy'), may hold values from -6 to 6
- density: float32 [256, 1024], P('gx', 'gy'), may hold values from 0.25 to 2
- grain_stress: float32 [6, 128, 256, 1024], P(None, 'ga', 'gx', 'gy'), may hold values from -4 to 4
- grain_angles: float32 [3, 128, 256, 1024], P(None, 'ga', 'gx', 'gy'), may hold values from -3.140625 to 3.140625
- hardness: float32 [128, 256, 1024], P('ga', 'gx', 'gy'), may hold values from 0.1 to 1
- active: int32 [2, 128, 256, 1024], P(None, 'ga', 'gx', 'gy'), may hold values from 0 to 4095
- donor_faces: int32 [2, 256, 1024], P(None, 'gx', 'gy'), may hold values 0 or 1
Outputs:
- velocity_out: float32 [2, 256, 1024], P(None, 'gx', 'gy')
- stress_out: float32 [6, 128, 256, 1024], P(None, 'ga', 'gx', 'gy')
- zone_stress: float32 [3, 256, 1024], P(None, 'gx', 'gy')
The draws below stay inside these ranges and needn't reach their ends.
Inputs may be any that keep to these rules, and one draw needn't show every extreme that they name: Bit b of word w, for b below 12, is 1 when slip system 12 * w + b of that grain is active; higher bits are zero. `donor_faces`: 1 when the face takes its value from the zone itself, 0 when from the next zone along that direction.
All inputs are finite; a program needn't handle non-finite values. No bound on the sum of `donor_faces` on one device may be relied on, other than what follows from the above.
Results may differ from the reference program's by a relative error of at most 0.0001.
Values sent between devices are 32-bit elements; how exact they have to be, the bound alone decides.
No kernel may reach another device: no remote copies, remote signals or barrier semaphores. Data moves between devices by JAX's collectives and lax.ppermute only.
A program may use at most 128 MiB of HBM per device.

```python
import math
import jax
import jax.numpy as jnp
from jax import lax

G = 128
ITERS = 4
NX = 256
NY = 1024


def plant(drawn, key, least, high):
    place = [jax.random.randint(jax.random.fold_in(key, axis), (), 0, length) for axis, length in enumerate(drawn.shape)]
    widest = drawn.shape.index(max(drawn.shape))
    next_to = place[:widest] + [(place[widest] + 1) % drawn.shape[widest]] + place[widest + 1:]
    return drawn.at[tuple(place)].set(least).at[tuple(next_to)].set(high)


def level_of(own_key, dims, cuts, low, largest):
    gain = 1.0
    for axis_at, shards_of in cuts:
        steps = jax.random.uniform(jax.random.fold_in(jax.random.fold_in(own_key, 6), axis_at), (shards_of,), jnp.float32, low / len(cuts), largest / len(cuts))
        gain = gain * jnp.repeat(jnp.exp(steps), dims[axis_at] // shards_of).reshape((-1,) + (1,) * (len(dims) - 1 - axis_at))
    return gain


def centred(own_key, dims, spread, limit, split=(), kind=jnp.bfloat16):
    drawn = spread * jax.random.normal(own_key, dims, jnp.float32)
    if split:
        drawn = drawn * level_of(own_key, dims, split, -0.22, 0.18)
    return jnp.clip(drawn, -limit, limit).astype(kind)


def setup_inputs(seed: int = 0) -> dict:
    arg_keys = jax.random.split(jax.random.key(seed), 8)
    return {
        "velocity": centred(arg_keys[0], (2, NX, NY), 1.0, 6.0, ((1, 16), (2, 8)), jnp.float32),
        "density": jnp.clip(jnp.exp(math.log(2.0) - 2.0794415 * jax.random.uniform(arg_keys[1], (NX, NY), jnp.float32) ** level_of(arg_keys[1], (NX, NY), ((0, 16), (1, 8)), -0.2, 0.2)), 0.25, 2.0),
        "grain_stress": centred(arg_keys[2], (6, G, NX, NY), 0.5, 4.0, ((1, 2), (2, 16), (3, 8)), jnp.float32),
        "grain_angles": jnp.clip(jax.random.uniform(arg_keys[3], (3, G, NX, NY), jnp.float32, -3.140625, 3.140625), -3.140625, 3.140625),
        "hardness": jnp.clip(jnp.exp(math.log(1.0) - 2.3025851 * jax.random.uniform(arg_keys[4], (G, NX, NY), jnp.float32) ** level_of(arg_keys[4], (G, NX, NY), ((0, 2), (1, 16), (2, 8)), -0.2, 0.2)), 0.1, 1.0),
        "active": plant(jax.random.randint(arg_keys[5], (2, G, NX, NY), 0, 4096), jax.random.fold_in(arg_keys[5], 1), 0, 4095).astype(jnp.int32),
        "donor_faces": plant((jax.random.randint(arg_keys[6], (2, NX, NY), 0, 2) < 1).astype(jnp.int32), jax.random.fold_in(arg_keys[6], 1), 0, 1),
    }


shear_modulus = 1.0
lame_first = 1.5
time_step = 0.1
grain_block = 8
voigt_pairs = ((0, 0), (1, 1), (2, 2), (1, 2), (0, 2), (0, 1))
system_list = (((0, 1, 1), (1, 1, -1)), ((0, 1, 1), (1, -1, 1)), ((1, 0, 1), (1, 1, -1)), ((1, 0, 1), (-1, 1, 1)), ((1, 1, 0), (1, -1, 1)), ((1, 1, 0), (-1, 1, 1)), ((0, 1, -1), (1, 1, 1)), ((0, 1, -1), (1, -1, -1)), ((1, 0, -1), (1, 1, 1)), ((1, 0, -1), (1, -1, 1)), ((1, -1, 0), (1, 1, 1)), ((1, -1, 0), (1, 1, -1)), ((1, 1, 2), (1, 1, -1)), ((1, 1, -2), (1, 1, 1)), ((1, -1, 2), (1, -1, -1)), ((-1, 1, 2), (-1, 1, -1)), ((1, 2, 1), (1, -1, 1)), ((1, -2, 1), (1, 1, 1)), ((-1, 2, 1), (1, 1, -1)), ((1, 2, -1), (-1, 1, 1)), ((2, 1, 1), (-1, 1, 1)), ((-2, 1, 1), (1, 1, 1)), ((2, -1, 1), (1, 1, -1)), ((2, 1, -1), (1, -1, 1)))

def slip_tables():
    plain_rows = []
    weighted_rows = []
    for entry in system_list:
        normal_len = math.sqrt(sum((value * value for value in entry[0])))
        direction_len = math.sqrt(sum((value * value for value in entry[1])))
        normal = [value / normal_len for value in entry[0]]
        direction = [value / direction_len for value in entry[1]]
        plain_row = []
        weighted_row = []
        for column, pair in enumerate(voigt_pairs):
            first_axis, second_axis = pair
            entry_value = 0.5 * (direction[first_axis] * normal[second_axis] + normal[first_axis] * direction[second_axis])
            plain_row.append(entry_value)
            weighted_row.append(entry_value * (1.0 if column < 3 else 2.0))
        plain_rows.append(plain_row)
        weighted_rows.append(weighted_row)
    return (jnp.asarray(plain_rows, dtype=jnp.float32), jnp.asarray(weighted_rows, dtype=jnp.float32))

def rotation_rows(angles):
    cos_one, sin_one = (jnp.cos(angles[0]), jnp.sin(angles[0]))
    cos_mid, sin_mid = (jnp.cos(angles[1]), jnp.sin(angles[1]))
    cos_two, sin_two = (jnp.cos(angles[2]), jnp.sin(angles[2]))
    first_row = (cos_one * cos_two - sin_one * sin_two * cos_mid, -cos_one * sin_two - sin_one * cos_two * cos_mid, sin_one * sin_mid)
    second_row = (sin_one * cos_two + cos_one * sin_two * cos_mid, -sin_one * sin_two + cos_one * cos_two * cos_mid, -cos_one * sin_mid)
    return (first_row, second_row)

def sample_sum(relaxed, row_left, row_right):
    total = None
    for first_axis in range(3):
        for second_axis in range(3):
            pair = (min(first_axis, second_axis), max(first_axis, second_axis))
            column = voigt_pairs.index(pair)
            term = row_left[first_axis] * row_right[second_axis] * relaxed[column]
            total = term if total is None else total + term
    return total

def grain_update(stress, angles, hardness, active, strain_xx, strain_yy, strain_xy):
    plain_table, weighted_table = slip_tables()
    first_row, second_row = rotation_rows(angles)
    crystal = []
    for pair in voigt_pairs:
        first_axis, second_axis = pair
        crystal.append(first_row[first_axis] * first_row[second_axis] * strain_xx + second_row[first_axis] * second_row[second_axis] * strain_yy + (first_row[first_axis] * second_row[second_axis] + second_row[first_axis] * first_row[second_axis]) * strain_xy)
    volume_rate = crystal[0] + crystal[1] + crystal[2]
    trial_parts = []
    for column in range(6):
        if column < 3:
            trial_parts.append(stress[column] + time_step * (2.0 * shear_modulus * crystal[column] + lame_first * volume_rate))
        else:
            trial_parts.append(stress[column] + time_step * (2.0 * shear_modulus * crystal[column]))
    trial_stress = jnp.stack(trial_parts)
    shifts = jnp.arange(12, dtype=jnp.int32).reshape(12, 1, 1, 1)
    low_bits = jnp.bitwise_and(jnp.right_shift(active[0][None], shifts), 1)
    high_bits = jnp.bitwise_and(jnp.right_shift(active[1][None], shifts), 1)
    switches = jnp.concatenate([low_bits, high_bits], 0).astype(jnp.float32)
    step_size = 1.0 / (shear_modulus * (lax.optimization_barrier(jnp.sum(switches, 0)) + 1.0))
    increments = jnp.zeros(switches.shape, jnp.float32)
    for iteration in range(ITERS):
        current = trial_stress - 2.0 * shear_modulus * jnp.einsum('sc,sbxy->cbxy', plain_table, increments, precision=lax.Precision.HIGHEST)
        resolved = jnp.einsum('sc,cbxy->sbxy', weighted_table, current, precision=lax.Precision.HIGHEST)
        increments = increments + switches * (resolved - hardness[None]) * step_size[None]
    relaxed = trial_stress - 2.0 * shear_modulus * jnp.einsum('sc,sbxy->cbxy', plain_table, increments, precision=lax.Precision.HIGHEST)
    sample = jnp.stack([sample_sum(relaxed, first_row, first_row), sample_sum(relaxed, second_row, second_row), sample_sum(relaxed, first_row, second_row)])
    return (relaxed, lax.optimization_barrier(jnp.sum(sample, axis=1)))

def solve_grains(stress, angles, hardness, active, strain_xx, strain_yy, strain_xy):
    grains, rows_x, rows_y = hardness.shape
    blocks = grains // grain_block
    stress_blocks = jnp.moveaxis(stress.reshape(6, blocks, grain_block, rows_x, rows_y), 1, 0)
    angle_blocks = jnp.moveaxis(angles.reshape(3, blocks, grain_block, rows_x, rows_y), 1, 0)
    hard_blocks = hardness.reshape(blocks, grain_block, rows_x, rows_y)
    active_blocks = jnp.moveaxis(active.reshape(2, blocks, grain_block, rows_x, rows_y), 1, 0)

    def one_block(pieces):
        return grain_update(pieces[0], pieces[1], pieces[2], pieces[3], strain_xx, strain_yy, strain_xy)
    relaxed_blocks, sums = lax.map(one_block, (stress_blocks, angle_blocks, hard_blocks, active_blocks))
    relaxed = jnp.moveaxis(relaxed_blocks, 0, 1).reshape(stress.shape)
    return (relaxed, lax.optimization_barrier(jnp.sum(sums, axis=0)))

def pad_cells(field):
    widths = [(0, 0)] * (field.ndim - 2) + [(1, 1), (1, 1)]
    return jnp.pad(field, widths)

def strain_rates(padded):
    ux_x = (padded[0, 2:, 1:-1] - padded[0, :-2, 1:-1]) * 0.5
    ux_y = (padded[0, 1:-1, 2:] - padded[0, 1:-1, :-2]) * 0.5
    uy_x = (padded[1, 2:, 1:-1] - padded[1, :-2, 1:-1]) * 0.5
    uy_y = (padded[1, 1:-1, 2:] - padded[1, 1:-1, :-2]) * 0.5
    return (ux_x, uy_y, 0.5 * (ux_y + uy_x))

def stress_force(padded):
    force_x = (padded[0, 2:, 1:-1] - padded[0, :-2, 1:-1]) * 0.5 + (padded[2, 1:-1, 2:] - padded[2, 1:-1, :-2]) * 0.5
    force_y = (padded[2, 2:, 1:-1] - padded[2, :-2, 1:-1]) * 0.5 + (padded[1, 1:-1, 2:] - padded[1, 1:-1, :-2]) * 0.5
    return jnp.stack([force_x, force_y])

def donor_remap(padded, moving, flag_pad):
    frac_x = time_step * 0.5 * (moving[0, :-1, 1:-1] + moving[0, 1:, 1:-1])
    pick_x = flag_pad[0, :-1, 1:-1]
    flux_x = frac_x * (pick_x * padded[..., :-1, 1:-1] + (1.0 - pick_x) * padded[..., 1:, 1:-1])
    frac_y = time_step * 0.5 * (moving[1, 1:-1, :-1] + moving[1, 1:-1, 1:])
    pick_y = flag_pad[1, 1:-1, :-1]
    flux_y = frac_y * (pick_y * padded[..., 1:-1, :-1] + (1.0 - pick_y) * padded[..., 1:-1, 1:])
    return padded[..., 1:-1, 1:-1] - (flux_x[..., 1:, :] - flux_x[..., :-1, :]) - (flux_y[..., :, 1:] - flux_y[..., :, :-1])

def reference(velocity, density, grain_stress, grain_angles, hardness, active, donor_faces):
    strain_xx, strain_yy, strain_xy = strain_rates(pad_cells(velocity))
    relaxed, summed = solve_grains(grain_stress, grain_angles, hardness, active, strain_xx, strain_yy, strain_xy)
    zone_stress = summed / G
    force_field = stress_force(pad_cells(zone_stress))
    inverse = 1.0 / density
    updated = velocity + time_step * inverse * force_field
    flag_pad = pad_cells(donor_faces.astype(jnp.float32))
    moving = pad_cells(updated)
    velocity_out = donor_remap(moving, moving, flag_pad)
    stress_out = donor_remap(pad_cells(relaxed), moving, flag_pad)
    return (velocity_out, stress_out, zone_stress)
```

```python
import functools
import math

import jax
import jax.numpy as jnp
import ml_dtypes
import numpy as np
from jax import lax
from jax.experimental import pallas as pl
from jax.experimental.pallas import tpu as pltpu
from jax.sharding import PartitionSpec as P

G = 128
ITERS = 4

time_step = 0.1
lame_first = 1.5
grain_block = 8
system_list = (
    ((0, 1, 1), (1, 1, -1)),
    ((0, 1, 1), (1, -1, 1)),
    ((1, 0, 1), (1, 1, -1)),
    ((1, 0, 1), (-1, 1, 1)),
    ((1, 1, 0), (1, -1, 1)),
    ((1, 1, 0), (-1, 1, 1)),
    ((0, 1, -1), (1, 1, 1)),
    ((0, 1, -1), (1, -1, -1)),
    ((1, 0, -1), (1, 1, 1)),
    ((1, 0, -1), (1, -1, 1)),
    ((1, -1, 0), (1, 1, 1)),
    ((1, -1, 0), (1, 1, -1)),
    ((1, 1, 2), (1, 1, -1)),
    ((1, 1, -2), (1, 1, 1)),
    ((1, -1, 2), (1, -1, -1)),
    ((-1, 1, 2), (-1, 1, -1)),
    ((1, 2, 1), (1, -1, 1)),
    ((1, -2, 1), (1, 1, 1)),
    ((-1, 2, 1), (1, 1, -1)),
    ((1, 2, -1), (-1, 1, 1)),
    ((2, 1, 1), (-1, 1, 1)),
    ((-2, 1, 1), (1, 1, 1)),
    ((2, -1, 1), (1, 1, -1)),
    ((2, 1, -1), (1, -1, 1)),
)
upper_pairs = [(i, j) for i in range(5) for j in range(i, 5)]
n_sums = 26


def slip_sums_table():
    table = np.zeros((n_sums, 24))
    for s, (normal, direction) in enumerate(system_list):
        q = np.outer(direction, normal) + np.outer(normal, direction)
        k = np.array([(q[0, 0] - q[1, 1]) / 2, -q[2, 2] / 2, q[1, 2], q[0, 2], q[0, 1]])
        weight = 3 if s < 12 else 1
        for e, (i, j) in enumerate(upper_pairs):
            table[e, s] = weight * k[i] * k[j] * (3 if i == j == 1 else 1)
        first = 15 if s < 12 else 20
        table[first : first + 5, s] = k
        table[25, s] = 1
    columns = np.zeros((n_sums, 24))
    for s in range(24):
        word, bit = divmod(s, 12)
        columns[:, 2 * bit + word] = table[:, s] / 2.0**bit
    return np.kron(columns, np.eye(8)).astype(ml_dtypes.bfloat16)


def fitted(function, degree, top):
    series = np.polynomial.chebyshev.Chebyshev.interpolate(function, degree, domain=[0.0, top])
    return [float(c) for c in series.convert(kind=np.polynomial.Polynomial).coef]


angle_top = 3.1416**2
sin_half = fitted(lambda t: math.sqrt(2) * np.sin(np.sqrt(t) / 2) / np.sqrt(t), 4, angle_top)
cos_half = fitted(lambda t: math.sqrt(2) * np.cos(np.sqrt(t) / 2), 4, angle_top)


def polynomial(t, coefs):
    total = coefs[-1] * t + coefs[-2]
    for c in coefs[-3::-1]:
        total = total * t + c
    return total


def sin_cos(x):
    t = x * x
    s = x * polynomial(t, sin_half)
    c = polynomial(t, cos_half)
    return s * c, 1.0 - s * s


def grain_math(stress, angles, hardness, sums, strain):
    exx, eyy, exy, trace, hydro = strain
    s1, c1 = sin_cos(angles[0])
    sq, cq = sin_cos(angles[1])
    s2, c2 = sin_cos(angles[2])
    c1c2, s1s2, c1s2, s1c2 = c1 * c2, s1 * s2, c1 * s2, s1 * c2
    r00 = c1c2 - s1s2 * cq
    r01 = -(c1s2 + s1c2 * cq)
    r02 = s1 * sq
    r10 = s1c2 + c1s2 * cq
    r11 = c1c2 * cq - s1s2
    r12 = -(c1 * sq)
    a0, b0 = r00 * exx + r10 * exy, r10 * eyy + r00 * exy
    a1, b1 = r01 * exx + r11 * exy, r11 * eyy + r01 * exy
    d00 = r00 * a0 + r10 * b0
    d11 = r01 * a1 + r11 * b1
    t00, t11 = stress[0] + d00, stress[1] + d11
    t22 = stress[2] + (trace - (d00 + d11))
    t_sum = t00 + t11
    v = [
        (t00 - t11) * 0.5,
        t_sum * (1 / math.sqrt(12)) - t22 * (2 / math.sqrt(12)),
        stress[3] + (r02 * a1 + r12 * b1),
        stress[4] + (r02 * a0 + r12 * b0),
        stress[5] + (r01 * a0 + r11 * b0),
    ]
    pressure = (t_sum + t22) * (1.0 / 3.0) + hydro
    step = 1.0 / (1.0 + sums(25))
    h0 = hardness * step * (1 / math.sqrt(2))
    h1 = h0 * (1 / math.sqrt(3))
    h2 = h0 * (1.0 / 3.0)
    bias = []
    for i in range(5):
        first, second = (h0, h1) if i == 1 else (h1, h2)
        bias.append(sums(15 + i) * first + sums(20 + i) * second)
    plain, mixed = step * (1 / 18.0), step * (math.sqrt(3) / 18.0)
    m = {}
    for e, (i, j) in enumerate(upper_pairs):
        entry = sums(e) * (mixed if (i == 1) != (j == 1) else plain)
        m[i, j] = m[j, i] = (1.0 - entry) if i == j else entry
    for _ in range(ITERS):
        fresh = []
        for i in range(5):
            off = None
            for j in range(5):
                if j != i:
                    term = m[i, j] * v[j]
                    off = term if off is None else off + term
            fresh.append((m[i, i] * v[i] + bias[i]) - off)
        v = fresh
    w = v[1] * (1 / math.sqrt(3))
    mid = pressure + w
    x = [mid + v[0], mid - v[0], pressure - 2.0 * w, v[2], v[3], v[4]]
    f0 = x[0] * r00 + x[5] * r01 + x[4] * r02
    f1 = x[5] * r00 + x[1] * r01 + x[3] * r02
    f2 = x[4] * r00 + x[3] * r01 + x[2] * r02
    g0 = x[0] * r10 + x[5] * r11 + x[4] * r12
    g1 = x[5] * r10 + x[1] * r11 + x[3] * r12
    g2 = x[4] * r10 + x[3] * r11 + x[2] * r12
    sample = (
        r00 * f0 + r01 * f1 + r02 * f2,
        r10 * g0 + r11 * g1 + r12 * g2,
        r00 * g0 + r01 * g1 + r02 * g2,
    )
    return x, sample


def bit_rows(words):
    pieces = [jnp.concatenate([w[:8], w[8:]], axis=1) for w in words]
    both = jnp.concatenate(pieces, axis=0).astype(jnp.int16)
    rows = [both & jnp.int16(1 << bit) for bit in range(12)]
    return jnp.concatenate(rows, axis=0).astype(jnp.bfloat16)


def solve_kernel(
    parity, table, strain, stress, angles, hardness, active,
    relaxed, zone_sum, rows_even, rows_odd, cols_even, cols_odd,
    sums_a, sums_b, rows, cols,
):
    block = pl.program_id(0)
    size = hardness.shape[0]
    grains = rows.shape[2]
    last_row, first_row = parity[0], 1 - parity[0]
    last_col, first_col = parity[1], 1 - parity[1]
    lane = lax.broadcasted_iota(jnp.int32, (16, 128), 1)

    @pl.when(block == 0)
    def _():
        zone_sum[...] = jnp.zeros_like(zone_sum)

    zone_strain = [strain[i] for i in range(5)]

    def count(g, sums):
        sums[...] = jnp.dot(
            table[...], bit_rows([active[0, g], active[1, g]]), preferred_element_type=jnp.float32
        )

    def update(g, sums):
        def entry(e):
            piece = sums[e * 8 : (e + 1) * 8]
            return jnp.concatenate([piece[:, :128], piece[:, 128:]], axis=0)

        x, sample = grain_math(
            [stress[c, g] for c in range(6)],
            [angles[c, g] for c in range(3)],
            hardness[g],
            entry,
            zone_strain,
        )
        place = block * size + g
        for c in range(6):
            relaxed[c, g] = x[c]
            rows[last_row, c, pl.ds(place, 1), :] = x[c][15:16]
            rows[first_row, c, pl.ds(place, 1), :] = x[c][0:1]
            spot = place + (c // 3) * 64
            here = lane == spot
            at_last = pltpu.roll(x[c], spot + 1, 1)
            at_first = pltpu.roll(x[c], spot, 1)
            cols[last_col, c % 3] = jnp.where(here, at_last, cols[last_col, c % 3])
            cols[first_col, c % 3] = jnp.where(here, at_first, cols[first_col, c % 3])
        for k in range(3):
            zone_sum[k] += sample[k]

    count(0, sums_a)

    def pair(i, carry):
        g = i * 2
        count(g + 1, sums_b)
        update(g, sums_a)
        count(jnp.minimum(g + 2, size - 1), sums_a)
        update(g + 1, sums_b)
        return carry

    lax.fori_loop(0, size // 2, pair, 0)

    @pl.when(block == pl.num_programs(0) - 1)
    def _():
        rows_even[...] = rows[0]
        rows_odd[...] = rows[1]
        cols_even[...] = cols[0]
        cols_odd[...] = cols[1]


def solve_grains(parity, strain, stress, angles, hardness, active):
    n = hardness.shape[0]
    size = grain_block
    table = jnp.asarray(slip_sums_table())
    whole = lambda *shape: pl.BlockSpec(shape, lambda i: (0,) * len(shape))
    f32 = lambda *shape: jax.ShapeDtypeStruct(shape, jnp.float32)
    return pl.pallas_call(
        solve_kernel,
        grid=(n // size,),
        in_specs=[
            pl.BlockSpec(memory_space=pltpu.SMEM),
            whole(*table.shape),
            whole(5, 16, 128),
            pl.BlockSpec((6, size, 16, 128), lambda i: (0, i, 0, 0)),
            pl.BlockSpec((3, size, 16, 128), lambda i: (0, i, 0, 0)),
            pl.BlockSpec((size, 16, 128), lambda i: (i, 0, 0)),
            pl.BlockSpec((2, size, 16, 128), lambda i: (0, i, 0, 0)),
        ],
        out_specs=[
            pl.BlockSpec((6, size, 16, 128), lambda i: (0, i, 0, 0)),
            whole(3, 16, 128),
            whole(6, n, 128),
            whole(6, n, 128),
            whole(3, 16, 128),
            whole(3, 16, 128),
        ],
        out_shape=[
            f32(6, n, 16, 128),
            f32(3, 16, 128),
            f32(6, n, 128),
            f32(6, n, 128),
            f32(3, 16, 128),
            f32(3, 16, 128),
        ],
        scratch_shapes=[
            pltpu.VMEM((table.shape[0], 256), jnp.float32),
            pltpu.VMEM((table.shape[0], 256), jnp.float32),
            pltpu.VMEM((2, 6, n, 128), jnp.float32),
            pltpu.VMEM((2, 3, 16, 128), jnp.float32),
        ],
        compiler_params=pltpu.CompilerParams(vmem_limit_bytes=40 * 2**20),
        cost_estimate=pl.CostEstimate(flops=10**8, bytes_accessed=10**7, transcendentals=0),
    )(parity, table, strain, stress, angles, hardness, active)


def remap_kernel(parity, coefs, relaxed, rows_even, rows_odd, cols_even, cols_odd, out, rows, cols):
    block = pl.program_id(0)
    size = relaxed.shape[1]
    odd_x, odd_y = parity[0] == 1, parity[1] == 1
    rows[0] = jnp.where(odd_x, rows_odd[...], rows_even[...])
    rows[1] = jnp.where(odd_x, rows_even[...], rows_odd[...])

    @pl.when(block == 0)
    def _():
        cols[0] = jnp.where(odd_y, cols_odd[...], cols_even[...])
        cols[1] = jnp.where(odd_y, cols_even[...], cols_odd[...])

    lane = lax.broadcasted_iota(jnp.int32, (16, 128), 1)
    row = lax.broadcasted_iota(jnp.int32, (16, 128), 0)
    centre, east, west, north, south = [coefs[i] for i in range(5)]

    def one(g, carry):
        for c in range(6):
            q = relaxed[c, g]
            spot = block * size + g + (c // 3) * 64
            q_east = jnp.where(row == 15, rows[0, c, pl.ds(g, 1), :], pltpu.roll(q, 15, 0))
            q_west = jnp.where(row == 0, rows[1, c, pl.ds(g, 1), :], pltpu.roll(q, 1, 0))
            q_north = jnp.where(lane == 127, pltpu.roll(cols[0, c % 3], 127 - spot, 1), pltpu.roll(q, 127, 1))
            q_south = jnp.where(lane == 0, pltpu.roll(cols[1, c % 3], 128 - spot, 1), pltpu.roll(q, 1, 1))
            out[c, g] = centre * q + east * q_east + west * q_west + north * q_north + south * q_south
        return carry

    lax.fori_loop(0, size, one, 0)


def remap_grains(parity, coefs, relaxed, rows_even, rows_odd, cols_even, cols_odd):
    n = relaxed.shape[1]
    size = grain_block
    whole = lambda *shape: pl.BlockSpec(shape, lambda i: (0,) * len(shape))
    return pl.pallas_call(
        remap_kernel,
        grid=(n // size,),
        in_specs=[
            pl.BlockSpec(memory_space=pltpu.SMEM),
            whole(5, 16, 128),
            pl.BlockSpec((6, size, 16, 128), lambda i: (0, i, 0, 0)),
            pl.BlockSpec((6, size, 128), lambda i: (0, i, 0)),
            pl.BlockSpec((6, size, 128), lambda i: (0, i, 0)),
            whole(3, 16, 128),
            whole(3, 16, 128),
        ],
        out_specs=pl.BlockSpec((6, size, 16, 128), lambda i: (0, i, 0, 0)),
        out_shape=jax.ShapeDtypeStruct(relaxed.shape, jnp.float32),
        scratch_shapes=[
            pltpu.VMEM((2, 6, size, 128), jnp.float32),
            pltpu.VMEM((2, 3, 16, 128), jnp.float32),
        ],
        compiler_params=pltpu.CompilerParams(vmem_limit_bytes=40 * 2**20),
        cost_estimate=pl.CostEstimate(flops=10**7, bytes_accessed=10**7, transcendentals=0),
    )(parity, coefs, relaxed, rows_even, rows_odd, cols_even, cols_odd)


def swap_even(block, axis):
    count = lax.axis_size(axis)
    pairs = [(i, i ^ 1) for i in range(count)]
    return lax.ppermute(block, axis, pairs)


def swap_odd(block, axis):
    count = lax.axis_size(axis)
    pairs = []
    for i in range(1, count - 1, 2):
        pairs += [(i, i + 1), (i + 1, i)]
    return lax.ppermute(block, axis, pairs)


def swap_odd_crossed(block):
    count = lax.axis_size("gx")
    pairs = []
    for i in range(1, count - 1, 2):
        for a in range(2):
            left, right = i * 2 + a, (i + 1) * 2 + 1 - a
            pairs += [(left, right), (right, left)]
    return lax.ppermute(block, ("gx", "ga"), pairs)


def zone_swap_x(first, last, odd):
    got_even = swap_even(jnp.where(odd, first, last), "gx")
    got_odd = swap_odd_crossed(jnp.where(odd, last, first))
    return jnp.where(odd, got_even, got_odd), jnp.where(odd, got_odd, got_even)


def zone_swap_y(first, last, odd):
    got_even = swap_even(jnp.where(odd, first, last), "gy")
    got_odd = swap_odd(jnp.where(odd, last, first), "gy")
    return jnp.where(odd, got_even, got_odd), jnp.where(odd, got_odd, got_even)


def strain_rates(padded):
    ux_x = (padded[0, 2:, 1:-1] - padded[0, :-2, 1:-1]) * 0.5
    ux_y = (padded[0, 1:-1, 2:] - padded[0, 1:-1, :-2]) * 0.5
    uy_x = (padded[1, 2:, 1:-1] - padded[1, :-2, 1:-1]) * 0.5
    uy_y = (padded[1, 1:-1, 2:] - padded[1, 1:-1, :-2]) * 0.5
    return (ux_x, uy_y, 0.5 * (ux_y + uy_x))


def stress_force(padded):
    force_x = (padded[0, 2:, 1:-1] - padded[0, :-2, 1:-1]) * 0.5 + (
        padded[2, 1:-1, 2:] - padded[2, 1:-1, :-2]
    ) * 0.5
    force_y = (padded[2, 2:, 1:-1] - padded[2, :-2, 1:-1]) * 0.5 + (
        padded[1, 1:-1, 2:] - padded[1, 1:-1, :-2]
    ) * 0.5
    return jnp.stack([force_x, force_y])


def face_shares(moving, flag_pad):
    frac_x = time_step * 0.5 * (moving[0, :-1, 1:-1] + moving[0, 1:, 1:-1])
    frac_y = time_step * 0.5 * (moving[1, 1:-1, :-1] + moving[1, 1:-1, 1:])
    pick_x, pick_y = flag_pad[0, :-1, 1:-1], flag_pad[1, 1:-1, :-1]
    return frac_x * pick_x, frac_x * (1.0 - pick_x), frac_y * pick_y, frac_y * (1.0 - pick_y)


def per_device(velocity, density, grain_stress, grain_angles, hardness, active, donor_faces):
    index_x, index_y = lax.axis_index("gx"), lax.axis_index("gy")
    odd_x, odd_y = index_x % 2 == 1, index_y % 2 == 1
    parity = jnp.stack([index_x % 2, index_y % 2]).astype(jnp.int32)

    fields = jnp.concatenate(
        [velocity, (1.0 / density)[None], donor_faces.astype(jnp.float32)], axis=0
    )
    west, east = zone_swap_x(fields[:, :1], fields[:, -1:], odd_x)
    south, north = zone_swap_y(fields[:, :, :1], fields[:, :, -1:], odd_y)
    tall = jnp.concatenate([west, fields, east], axis=1)
    rim = ((0, 0), (1, 1), (0, 0))
    field_pad = jnp.concatenate([jnp.pad(south, rim), tall, jnp.pad(north, rim)], axis=2)
    exx, eyy, exy = strain_rates(field_pad[:2])
    strain = jnp.stack(
        [
            2.0 * time_step * exx,
            2.0 * time_step * eyy,
            2.0 * time_step * exy,
            2.0 * time_step * (exx + eyy),
            lame_first * time_step * (exx + eyy),
        ]
    )
    relaxed, part, rows_even, rows_odd, cols_even, cols_odd = solve_grains(
        parity, strain, grain_stress, grain_angles, hardness, active
    )
    far_rows_odd = swap_odd(rows_odd, "gx")
    far_rows_even = swap_even(rows_even, "gx")
    zone_stress = (part + swap_even(part, "ga")) * (1.0 / G)
    stress_west, stress_east = zone_swap_x(zone_stress[:, :2], zone_stress[:, -2:], odd_x)
    stress_tall = jnp.concatenate([stress_west, zone_stress, stress_east], axis=1)
    edge = jnp.pad(stress_tall[:, 1:-1], ((0, 0), (0, 6), (0, 0)))
    first = jnp.pad(edge[:, :, :2], ((0, 0), (0, 0), (0, 126)))
    last = jnp.pad(edge[:, :, -2:], ((0, 0), (0, 0), (0, 126)))
    sent_even = jnp.concatenate([cols_even, jnp.where(odd_y, first, last)], axis=1)
    sent_odd = jnp.concatenate([cols_odd, jnp.where(odd_y, last, first)], axis=1)
    got_even, got_odd = swap_even(sent_even, "gy"), swap_odd(sent_odd, "gy")
    far_cols_even, far_cols_odd = got_even[:, :16], got_odd[:, :16]
    stress_even, stress_odd = got_even[:, 16:34, :2], got_odd[:, 16:34, :2]
    stress_south = jnp.where(odd_y, stress_even, stress_odd)
    stress_north = jnp.where(odd_y, stress_odd, stress_even)
    stress_pad = jnp.concatenate(
        [jnp.pad(stress_south, rim), stress_tall, jnp.pad(stress_north, rim)], axis=2
    )
    moving = field_pad[:2] + time_step * field_pad[2] * stress_force(stress_pad)
    x_self, x_next, y_self, y_next = face_shares(moving, field_pad[3:])
    coefs = jnp.stack(
        [
            1.0 - x_self[1:] + x_next[:-1] - y_self[:, 1:] + y_next[:, :-1],
            -x_next[1:],
            x_self[:-1],
            -y_next[:, 1:],
            y_self[:, :-1],
        ]
    )
    velocity_out = (
        coefs[0] * moving[:, 1:-1, 1:-1]
        + coefs[1] * moving[:, 2:, 1:-1]
        + coefs[2] * moving[:, :-2, 1:-1]
        + coefs[3] * moving[:, 1:-1, 2:]
        + coefs[4] * moving[:, 1:-1, :-2]
    )
    stress_out = remap_grains(
        parity, coefs, relaxed, far_rows_even, far_rows_odd, far_cols_even, far_cols_odd
    )
    return (velocity_out, stress_out, zone_stress)


def solution(mesh):
    return jax.shard_map(
        per_device,
        mesh=mesh,
        in_specs=(
            P(None, "gx", "gy"),
            P("gx", "gy"),
            P(None, "ga", "gx", "gy"),
            P(None, "ga", "gx", "gy"),
            P("ga", "gx", "gy"),
            P(None, "ga", "gx", "gy"),
            P(None, "gx", "gy"),
        ),
        out_specs=(P(None, "gx", "gy"), P(None, "ga", "gx", "gy"), P(None, "gx", "gy")),
        check_vma=False,
    )
```

```python
import functools
import math

import jax
import jax.numpy as jnp
import ml_dtypes
import numpy as np
from jax import lax
from jax.experimental import pallas as pl
from jax.experimental.pallas import tpu as pltpu
from jax.sharding import PartitionSpec as P

G = 128
ITERS = 4

time_step = 0.1
lame_first = 1.5
grain_block = 8
batch = 4
system_list = (
    ((0, 1, 1), (1, 1, -1)),
    ((0, 1, 1), (1, -1, 1)),
    ((1, 0, 1), (1, 1, -1)),
    ((1, 0, 1), (-1, 1, 1)),
    ((1, 1, 0), (1, -1, 1)),
    ((1, 1, 0), (-1, 1, 1)),
    ((0, 1, -1), (1, 1, 1)),
    ((0, 1, -1), (1, -1, -1)),
    ((1, 0, -1), (1, 1, 1)),
    ((1, 0, -1), (1, -1, 1)),
    ((1, -1, 0), (1, 1, 1)),
    ((1, -1, 0), (1, 1, -1)),
    ((1, 1, 2), (1, 1, -1)),
    ((1, 1, -2), (1, 1, 1)),
    ((1, -1, 2), (1, -1, -1)),
    ((-1, 1, 2), (-1, 1, -1)),
    ((1, 2, 1), (1, -1, 1)),
    ((1, -2, 1), (1, 1, 1)),
    ((-1, 2, 1), (1, 1, -1)),
    ((1, 2, -1), (-1, 1, 1)),
    ((2, 1, 1), (-1, 1, 1)),
    ((-2, 1, 1), (1, 1, 1)),
    ((2, -1, 1), (1, 1, -1)),
    ((2, 1, -1), (1, -1, 1)),
)
upper_pairs = [(i, j) for i in range(5) for j in range(i, 5)]
n_sums = 26


def slip_sums_table():
    table = np.zeros((n_sums, 24))
    for s, (normal, direction) in enumerate(system_list):
        q = np.outer(direction, normal) + np.outer(normal, direction)
        k = np.array([(q[0, 0] - q[1, 1]) / 2, -q[2, 2] / 2, q[1, 2], q[0, 2], q[0, 1]])
        weight = 3 if s < 12 else 1
        for e, (i, j) in enumerate(upper_pairs):
            table[e, s] = weight * k[i] * k[j] * (3 if i == j == 1 else 1)
        first = 15 if s < 12 else 20
        table[first : first + 5, s] = k
        table[25, s] = 1
    columns = np.zeros((n_sums, 24))
    for s in range(24):
        word, bit = divmod(s, 12)
        columns[:, 2 * bit + word] = table[:, s] / 2.0**bit
    return np.kron(columns, np.eye(8)).astype(ml_dtypes.bfloat16)


def fitted(function, degree, top):
    series = np.polynomial.chebyshev.Chebyshev.interpolate(function, degree, domain=[0.0, top])
    return [float(c) for c in series.convert(kind=np.polynomial.Polynomial).coef]


angle_top = 3.1416**2
sin_half = fitted(lambda t: math.sqrt(2) * np.sin(np.sqrt(t) / 2) / np.sqrt(t), 4, angle_top)
cos_half = fitted(lambda t: math.sqrt(2) * np.cos(np.sqrt(t) / 2), 4, angle_top)


def polynomial(t, coefs):
    total = coefs[-1] * t + coefs[-2]
    for c in coefs[-3::-1]:
        total = total * t + c
    return total


def sin_cos(x):
    t = x * x
    s = x * polynomial(t, sin_half)
    c = polynomial(t, cos_half)
    return s * c, 1.0 - s * s


def grain_math(stress, angles, hardness, sums, strain):
    exx, eyy, exy, trace, hydro = strain
    s1, c1 = sin_cos(angles[0])
    sq, cq = sin_cos(angles[1])
    s2, c2 = sin_cos(angles[2])
    c1c2, s1s2, c1s2, s1c2 = c1 * c2, s1 * s2, c1 * s2, s1 * c2
    r00 = c1c2 - s1s2 * cq
    r01 = -(c1s2 + s1c2 * cq)
    r02 = s1 * sq
    r10 = s1c2 + c1s2 * cq
    r11 = c1c2 * cq - s1s2
    r12 = -(c1 * sq)
    a0, b0 = r00 * exx + r10 * exy, r10 * eyy + r00 * exy
    a1, b1 = r01 * exx + r11 * exy, r11 * eyy + r01 * exy
    d00 = r00 * a0 + r10 * b0
    d11 = r01 * a1 + r11 * b1
    t00, t11 = stress[0] + d00, stress[1] + d11
    t22 = stress[2] + (trace - (d00 + d11))
    t_sum = t00 + t11
    v = [
        (t00 - t11) * 0.5,
        t_sum * (1 / math.sqrt(12)) - t22 * (2 / math.sqrt(12)),
        stress[3] + (r02 * a1 + r12 * b1),
        stress[4] + (r02 * a0 + r12 * b0),
        stress[5] + (r01 * a0 + r11 * b0),
    ]
    pressure = (t_sum + t22) * (1.0 / 3.0) + hydro
    step = 1.0 / (1.0 + sums(25))
    h0 = hardness * step * (1 / math.sqrt(2))
    h1 = h0 * (1 / math.sqrt(3))
    h2 = h0 * (1.0 / 3.0)
    bias = []
    for i in range(5):
        first, second = (h0, h1) if i == 1 else (h1, h2)
        bias.append(sums(15 + i) * first + sums(20 + i) * second)
    plain, mixed = step * (1 / 18.0), step * (math.sqrt(3) / 18.0)
    m = {}
    for e, (i, j) in enumerate(upper_pairs):
        entry = sums(e) * (mixed if (i == 1) != (j == 1) else plain)
        m[i, j] = m[j, i] = (1.0 - entry) if i == j else entry
    for _ in range(ITERS):
        fresh = []
        for i in range(5):
            off = None
            for j in range(5):
                if j != i:
                    term = m[i, j] * v[j]
                    off = term if off is None else off + term
            fresh.append((m[i, i] * v[i] + bias[i]) - off)
        v = fresh
    w = v[1] * (1 / math.sqrt(3))
    mid = pressure + w
    x = [mid + v[0], mid - v[0], pressure - 2.0 * w, v[2], v[3], v[4]]
    f0 = x[0] * r00 + x[5] * r01 + x[4] * r02
    f1 = x[5] * r00 + x[1] * r01 + x[3] * r02
    f2 = x[4] * r00 + x[3] * r01 + x[2] * r02
    g0 = x[0] * r10 + x[5] * r11 + x[4] * r12
    g1 = x[5] * r10 + x[1] * r11 + x[3] * r12
    g2 = x[4] * r10 + x[3] * r11 + x[2] * r12
    sample = (
        r00 * f0 + r01 * f1 + r02 * f2,
        r10 * g0 + r11 * g1 + r12 * g2,
        r00 * g0 + r01 * g1 + r02 * g2,
    )
    return x, sample


def bit_rows(words):
    pieces = [jnp.concatenate([w[:8], w[8:]], axis=1) for w in words]
    both = jnp.concatenate(pieces, axis=0).astype(jnp.int16)
    rows = [both & jnp.int16(1 << bit) for bit in range(12)]
    return jnp.concatenate(rows, axis=0).astype(jnp.bfloat16)


def places():
    return lax.axis_index("gx"), lax.axis_index("gy")


def whole(*shape):
    return pl.BlockSpec(shape, lambda *i: (0,) * len(shape))


def f32(*shape):
    return jax.ShapeDtypeStruct(shape, jnp.float32)


def lane_ids(rows):
    return lax.broadcasted_iota(jnp.int32, (rows, 128), 1)


def row_ids():
    return lax.broadcasted_iota(jnp.int32, (16, 128), 0)


def edges_kernel(velocity, density, donor_faces, fields, x_even, x_odd, y_sent):
    gx, _ = places()
    odd_x = gx % 2 == 1
    fields[0:2] = velocity[...]
    fields[2] = 1.0 / density[...]
    fields[3:5] = donor_faces[...].astype(jnp.float32)
    lane = lane_ids(16)
    x_even[...] = jnp.zeros_like(x_even)
    x_odd[...] = jnp.zeros_like(x_odd)
    edge = jnp.zeros((16, 128), jnp.float32)
    for k in range(5):
        field = fields[k]
        first, last = field[0:1], field[15:16]
        x_even[k : k + 1] = jnp.where(odd_x, first, last)
        x_odd[k : k + 1] = jnp.where(odd_x, last, first)
        edge = jnp.where((lane == 2 * k) | (lane == 2 * k + 1), pltpu.roll(field, 2 * k + 1, 1), edge)
    y_sent[...] = edge


def edge_fields(velocity, density, donor_faces):
    return pl.pallas_call(
        edges_kernel,
        out_shape=[f32(5, 16, 128), f32(8, 128), f32(8, 128), f32(16, 128)],
    )(velocity, density, donor_faces)


def from_sides(got_even, got_odd, index, count):
    odd = index % 2 == 1
    after = jnp.where(odd, got_odd, got_even)
    before = jnp.where(odd, got_even, got_odd)
    return jnp.where(index == count - 1, 0.0, after), jnp.where(index == 0, 0.0, before)


def shifts_x(field, east, west):
    row = row_ids()
    return (
        jnp.where(row == 15, east, pltpu.roll(field, 15, 0)),
        jnp.where(row == 0, west, pltpu.roll(field, 1, 0)),
    )


def shifts_y(field, halo):
    lane = lane_ids(field.shape[0])
    return (
        jnp.where(lane == 127, halo, pltpu.roll(field, 127, 1)),
        jnp.where(lane == 0, halo, pltpu.roll(field, 1, 1)),
    )


def side_columns(after, before, first, last):
    lane = lane_ids(after.shape[0])
    return jnp.where(
        lane == 127,
        pltpu.roll(after, 127 - first, 1),
        jnp.where(lane == 0, pltpu.roll(before, (128 - last) % 128, 1), 0.0),
    )


def solve_kernel(
    counts, table, fields, x_even, x_odd, y_even, y_odd, stress_in, angles_in, hardness_in, active_in,
    relaxed, zone_sum, rows_even, rows_odd, cols_sent,
    stress, angles, hardness, active, sums_a, sums_b, strain, rows, sems,
):
    block = pl.program_id(0)
    blocks = hardness.shape[0] // grain_block
    gx, gy = places()

    def copies(i, kinds):
        part = pl.ds(i * grain_block, grain_block)
        every = (
            lambda: (active_in.at[:, part], active.at[:, part]),
            lambda: (stress_in.at[:, part], stress.at[:, part]),
            lambda: (angles_in.at[:, part], angles.at[:, part]),
            lambda: (hardness_in.at[part], hardness.at[part]),
        )
        return [pltpu.make_async_copy(*every[k](), sems.at[k, i]) for k in kinds]

    def count(group, sums):
        first = group * batch
        bits = [bit_rows([active[0, first + k], active[1, first + k]]) for k in range(batch)]
        sums[...] = jnp.dot(
            table[...], jnp.concatenate(bits, axis=1), preferred_element_type=jnp.float32
        )

    def update(group, sums):
        for half in range(2):
            part = pl.ds(8 * half, 8)
            zone_strain = [strain[i, part] for i in range(5)]
            totals = [0.0, 0.0, 0.0]
            for k in range(batch):
                g = group * batch + k
                lanes = slice(256 * k + 128 * half, 256 * k + 128 * half + 128)
                x, sample = grain_math(
                    [stress[c, g, part] for c in range(6)],
                    [angles[c, g, part] for c in range(3)],
                    hardness[g, part],
                    lambda e: sums[e * 8 : (e + 1) * 8, lanes],
                    zone_strain,
                )
                lane = lane_ids(8)
                here = (lane == 2 * g) | (lane == 2 * g + 1)
                for c in range(6):
                    relaxed[c, g - block * grain_block, part] = x[c]
                    if half:
                        rows[gx % 2, c, pl.ds(g, 1), :] = x[c][7:8]
                    else:
                        rows[1 - gx % 2, c, pl.ds(g, 1), :] = x[c][0:1]
                    cols_sent[c, part] = jnp.where(
                        here, pltpu.roll(x[c], 2 * g + 1, 1), cols_sent[c, part]
                    )
                totals = [t + s for t, s in zip(totals, sample)]
            for k in range(3):
                zone_sum[k, part] += totals[k]

    @pl.when(block == 0)
    def _():
        for i in range(blocks):
            for copy in copies(i, range(4)):
                copy.start()
        zone_sum[...] = jnp.zeros_like(zone_sum)
        cols_sent[...] = jnp.zeros_like(cols_sent)
        east, west = from_sides(x_even[...], x_odd[...], gx, counts[0])
        north, south = from_sides(y_even[...], y_odd[...], gy, counts[1])
        grads = []
        for k in range(2):
            u = fields[k]
            u_east, u_west = shifts_x(u, east[k : k + 1], west[k : k + 1])
            u_north, u_south = shifts_y(u, side_columns(north, south, 2 * k + 1, 2 * k))
            grads.append(((u_east - u_west) * 0.5, (u_north - u_south) * 0.5))
        exx, eyy = grads[0][0], grads[1][1]
        exy = 0.5 * (grads[0][1] + grads[1][0])
        strain[0] = 2.0 * time_step * exx
        strain[1] = 2.0 * time_step * eyy
        strain[2] = 2.0 * time_step * exy
        strain[3] = 2.0 * time_step * (exx + eyy)
        strain[4] = lame_first * time_step * (exx + eyy)
        copies(0, [0])[0].wait()
        count(0, sums_a)

    for copy in copies(block, [1, 2, 3]):
        copy.wait()

    @pl.when(block < blocks - 1)
    def _():
        copies(block + 1, [0])[0].wait()

    count(block * 2 + 1, sums_b)
    update(block * 2, sums_a)
    count(jnp.minimum(block * 2 + 2, blocks * 2 - 1), sums_a)
    update(block * 2 + 1, sums_b)

    @pl.when(block == blocks - 1)
    def _():
        rows_even[...] = rows[0]
        rows_odd[...] = rows[1]


def solve_grains(counts, fields, got, stress, angles, hardness, active):
    n = hardness.shape[0]
    table = jnp.asarray(slip_sums_table())
    in_hbm = pl.BlockSpec(memory_space=pltpu.HBM)
    return pl.pallas_call(
        solve_kernel,
        grid=(n // grain_block,),
        in_specs=[
            pl.BlockSpec(memory_space=pltpu.SMEM),
            whole(*table.shape),
            whole(*fields.shape),
            *[whole(*g.shape) for g in got],
            *[in_hbm] * 4,
        ],
        out_specs=[
            pl.BlockSpec((6, grain_block, 16, 128), lambda i: (0, i, 0, 0)),
            whole(3, 16, 128),
            whole(6, n, 128),
            whole(6, n, 128),
            whole(6, 16, 128),
        ],
        out_shape=[f32(6, n, 16, 128), f32(3, 16, 128), f32(6, n, 128), f32(6, n, 128), f32(6, 16, 128)],
        scratch_shapes=[
            pltpu.VMEM(stress.shape, jnp.float32),
            pltpu.VMEM(angles.shape, jnp.float32),
            pltpu.VMEM(hardness.shape, jnp.float32),
            pltpu.VMEM(active.shape, jnp.int32),
            pltpu.VMEM((table.shape[0], 256 * batch), jnp.float32),
            pltpu.VMEM((table.shape[0], 256 * batch), jnp.float32),
            pltpu.VMEM((5, 16, 128), jnp.float32),
            pltpu.VMEM((2, 6, n, 128), jnp.float32),
            pltpu.SemaphoreType.DMA((4, n // grain_block)),
        ],
        compiler_params=pltpu.CompilerParams(vmem_limit_bytes=40 * 2**20),
        cost_estimate=pl.CostEstimate(flops=10**8, bytes_accessed=10**7, transcendentals=0),
    )(counts, table, fields, *got, stress, angles, hardness, active)


def zone_update(counts, fields, f_got, stress, s_got, tall, moved, velocity_out):
    gx, gy = places()
    fx_even, fx_odd, fy_even, fy_odd = f_got
    sx_even, sx_odd, sy_even, sy_odd = s_got
    f_east, f_west = from_sides(fx_even, fx_odd, gx, counts[0])
    f_north, f_south = from_sides(fy_even, fy_odd, gy, counts[1])
    s_east, s_west = from_sides(sx_even, sx_odd, gx, counts[0])
    s_north, s_south = from_sides(sy_even, sy_odd, gy, counts[1])
    for c in range(3):
        tall[c, 0:2] = s_west[2 * c : 2 * c + 2]
        tall[c, 2:18] = stress[c]
        tall[c, 18:20] = s_east[2 * c : 2 * c + 2]
    near = [side_columns(s_north, s_south, 4 * c, 4 * c + 3) for c in range(3)]
    far = [side_columns(s_north, s_south, 4 * c + 1, 4 * c + 2) for c in range(3)]
    lane = lane_ids(16)
    sign = jnp.where(lane == 127, 0.5, -0.5)

    def x_diff(c):
        return (tall[c, 2:20] - tall[c, 0:18]) * 0.5

    def y_diff(c):
        after, before = shifts_y(tall[c, 1:19], near[c][:18])
        return (after - before) * 0.5

    def rim_x(c):
        return (near[c][2:18] - near[c][0:16]) * 0.5

    def rim_y(c):
        return (far[c][1:17] - stress[c]) * sign

    force = [x_diff(0) + y_diff(2), x_diff(2) + y_diff(1)]
    rim_force = [rim_x(0) + rim_y(2), rim_x(2) + rim_y(1)]
    field_rim = [side_columns(f_north, f_south, 2 * k + 1, 2 * k) for k in range(5)]

    def high(k):
        return jnp.concatenate([f_west[k : k + 1], fields[k], f_east[k : k + 1]], axis=0)

    mass = time_step * high(2)
    rim = []
    for k in range(2):
        moved[k, 0:18] = high(k) + mass * force[k]
        rim.append(field_rim[k] + time_step * field_rim[2] * rim_force[k])
    frac_x = time_step * 0.5 * (moved[0, 0:17] + moved[0, 1:18])
    x_self = frac_x * high(3)[:17]
    x_next = frac_x - x_self
    own = [moved[k, 1:17] for k in range(2)]
    y_sides = [shifts_y(own[k], rim[k]) for k in range(2)]
    frac_y = time_step * 0.5 * (own[1] + y_sides[1][0])
    frac_before = time_step * 0.5 * (own[1] + y_sides[1][1])
    flag = fields[4]
    flag_before = jnp.where(lane == 0, field_rim[4], pltpu.roll(flag, 1, 1))
    y_self, before_self = frac_y * flag, frac_before * flag_before
    y_next, before_next = frac_y - y_self, frac_before - before_self
    centre = 1.0 - x_self[1:17] + x_next[0:16] - y_self + before_next
    coefs = (centre, -x_next[1:17], x_self[0:16], -y_next, before_self)
    for k in range(2):
        velocity_out[k] = (
            centre * own[k]
            + coefs[1] * moved[k, 2:18]
            + coefs[2] * moved[k, 0:16]
            + coefs[3] * y_sides[k][0]
            + coefs[4] * y_sides[k][1]
        )
    return coefs


def remap_kernel(
    counts, fields, fx_even, fx_odd, fy_even, fy_odd, stress, sx_even, sx_odd, y_even, y_odd,
    relaxed, rows_even, rows_odd, out, velocity_out, tall, moved, coefs, rows, cols,
):
    block = pl.program_id(0)
    size = relaxed.shape[1]
    gx, gy = places()
    odd_x = gx % 2 == 1
    rows[0] = jnp.where(odd_x, rows_odd[...], rows_even[...])
    rows[1] = jnp.where(odd_x, rows_even[...], rows_odd[...])
    lane, row = lane_ids(16), row_ids()

    @pl.when(block == 0)
    def _():
        fresh = zone_update(
            counts,
            fields,
            (fx_even[...], fx_odd[...], fy_even[...], fy_odd[...]),
            stress,
            (sx_even[...], sx_odd[...], y_even[96:120], y_odd[96:120]),
            tall,
            moved,
            velocity_out,
        )
        centre, east, west, north, south = fresh
        coefs[0] = centre
        coefs[1] = jnp.where(row == 15, 0.0, east)
        coefs[2] = jnp.where(row == 0, 0.0, west)
        coefs[3] = jnp.where(lane == 127, 0.0, north)
        coefs[4] = jnp.where(lane == 0, 0.0, south)
        coefs[5] = jnp.where((row == 15) & (gx < counts[0] - 1), east, 0.0)
        coefs[6] = jnp.where((row == 0) & (gx > 0), west, 0.0)
        rim = jnp.where((lane == 127) & (gy < counts[1] - 1), north, 0.0)
        coefs[7] = jnp.where((lane == 0) & (gy > 0), south, rim)
        odd_y = gy % 2 == 1
        for c in range(6):
            got_even, got_odd = y_even[16 * c : 16 * c + 16], y_odd[16 * c : 16 * c + 16]
            after = pltpu.roll(jnp.where(odd_y, got_odd, got_even), 127, 1)
            before = pltpu.roll(jnp.where(odd_y, got_even, got_odd), 1, 1)
            cols[c] = jnp.where(lane % 2 == 0, after, before)

    centre, east, west, north, south, _, _, rim = [coefs[i] for i in range(8)]
    high_east, low_west = coefs[5, 8:16], coefs[6, 0:8]

    def one(g):
        for c in range(6):
            q = relaxed[c, g]
            halo = pltpu.roll(cols[c], 127 - 2 * (block * size + g), 1)
            total = centre * q + north * pltpu.roll(q, 127, 1) + south * pltpu.roll(q, 1, 1)
            total = total + rim * halo
            total = total + east * pltpu.roll(q, 15, 0) + west * pltpu.roll(q, 1, 0)
            out[c, g, 0:8] = total[:8] + low_west * rows[1, c, pl.ds(g, 1), :]
            out[c, g, 8:16] = total[8:] + high_east * rows[0, c, pl.ds(g, 1), :]

    def some(i, carry):
        for k in range(8):
            one(i * 8 + k)
        return carry

    lax.fori_loop(0, size // 8, some, 0)


def remap_grains(counts, fields, f_got, stress, s_got, y_got, relaxed, rows_even, rows_odd):
    n = relaxed.shape[1]
    size = 16
    small = (fields, *f_got, stress, *s_got, *y_got)
    return pl.pallas_call(
        remap_kernel,
        grid=(n // size,),
        in_specs=[
            pl.BlockSpec(memory_space=pltpu.SMEM),
            *[whole(*a.shape) for a in small],
            pl.BlockSpec((6, size, 16, 128), lambda i: (0, i, 0, 0)),
            pl.BlockSpec((6, size, 128), lambda i: (0, i, 0)),
            pl.BlockSpec((6, size, 128), lambda i: (0, i, 0)),
        ],
        out_specs=[
            pl.BlockSpec((6, size, 16, 128), lambda i: (0, i, 0, 0)),
            whole(2, 16, 128),
        ],
        out_shape=[f32(*relaxed.shape), f32(2, 16, 128)],
        scratch_shapes=[
            pltpu.VMEM((3, 24, 128), jnp.float32),
            pltpu.VMEM((2, 24, 128), jnp.float32),
            pltpu.VMEM((8, 16, 128), jnp.float32),
            pltpu.VMEM((2, 6, size, 128), jnp.float32),
            pltpu.VMEM((6, 16, 128), jnp.float32),
        ],
        compiler_params=pltpu.CompilerParams(vmem_limit_bytes=40 * 2**20),
        cost_estimate=pl.CostEstimate(flops=10**7, bytes_accessed=10**7, transcendentals=0),
    )(counts, *small, relaxed, rows_even, rows_odd)


def swap_even(block, axis):
    return lax.ppermute(block, axis, [(i, i ^ 1) for i in range(lax.axis_size(axis))])


def swap_odd(block, axis):
    count = lax.axis_size(axis)
    pairs = []
    for i in range(1, count, 2):
        pairs += [(i, (i + 1) % count), ((i + 1) % count, i)]
    return lax.ppermute(block, axis, pairs)


def swap_odd_crossed(block):
    count = lax.axis_size("gx")
    pairs = []
    for i in range(1, count, 2):
        for a in range(2):
            left, right = i * 2 + a, ((i + 1) % count) * 2 + 1 - a
            pairs += [(left, right), (right, left)]
    return lax.ppermute(block, ("gx", "ga"), pairs)


def per_device(velocity, density, grain_stress, grain_angles, hardness, active, donor_faces):
    gx = lax.axis_index("gx")
    odd_x = gx % 2 == 1
    counts = jnp.array([lax.axis_size("gx"), lax.axis_size("gy")], jnp.int32)

    fields, x_even, x_odd, y_sent = edge_fields(velocity, density, donor_faces)
    f_got = (
        swap_even(x_even, "gx"),
        swap_odd_crossed(x_odd),
        swap_even(y_sent, "gy"),
        swap_odd(y_sent, "gy"),
    )
    relaxed, part, rows_even, rows_odd, cols = solve_grains(
        counts, fields, f_got, grain_stress, grain_angles, hardness, active
    )
    far_rows_odd = swap_odd(rows_odd, "gx")
    far_rows_even = swap_even(rows_even, "gx")
    zone_stress = (part + swap_even(part, "ga")) * (1.0 / G)
    first, last = zone_stress[:, :2], zone_stress[:, -2:]
    got_even = swap_even(jnp.where(odd_x, first, last).reshape(6, 128), "gx")
    got_odd = swap_odd_crossed(jnp.where(odd_x, last, first).reshape(6, 128))
    east, west = from_sides(got_even, got_odd, gx, lax.axis_size("gx"))
    east, west = east.reshape(3, 2, 128), west.reshape(3, 2, 128)
    tall = jnp.concatenate([west[:, 1:], zone_stress, east[:, :1]], axis=1)
    sides = jnp.concatenate([tall[:, :, :2], tall[:, :, -2:]], axis=2)
    sides = jnp.moveaxis(sides, 0, 1).reshape(18, 12)
    sent = jnp.concatenate(
        [cols.reshape(96, 128), jnp.pad(sides, ((0, 6), (0, 116)))], axis=0
    )
    y_got = (swap_even(sent, "gy"), swap_odd(sent, "gy"))
    stress_out, velocity_out = remap_grains(
        counts, fields, f_got, zone_stress, (got_even, got_odd), y_got, relaxed, far_rows_even, far_rows_odd
    )
    return (velocity_out, stress_out, zone_stress)


def solution(mesh):
    return jax.shard_map(
        per_device,
        mesh=mesh,
        in_specs=(
            P(None, "gx", "gy"),
            P("gx", "gy"),
            P(None, "ga", "gx", "gy"),
            P(None, "ga", "gx", "gy"),
            P("ga", "gx", "gy"),
            P(None, "ga", "gx", "gy"),
            P(None, "gx", "gy"),
        ),
        out_specs=(P(None, "gx", "gy"), P(None, "ga", "gx", "gy"), P(None, "gx", "gy")),
        check_vma=False,
    )
```

```python
import functools
import math

import jax
import jax.numpy as jnp
import numpy as np
from jax import lax
from jax.experimental import pallas as pl
from jax.experimental.pallas import tpu as pltpu
from jax.sharding import PartitionSpec as P

G = 128
ITERS = 4

time_step = 0.1
lame_first = 1.5
grain_block = 8
batch = 4
edge_vmem = 63 * 2**20
system_list = (
    ((0, 1, 1), (1, 1, -1)),
    ((0, 1, 1), (1, -1, 1)),
    ((1, 0, 1), (1, 1, -1)),
    ((1, 0, 1), (-1, 1, 1)),
    ((1, 1, 0), (1, -1, 1)),
    ((1, 1, 0), (-1, 1, 1)),
    ((0, 1, -1), (1, 1, 1)),
    ((0, 1, -1), (1, -1, -1)),
    ((1, 0, -1), (1, 1, 1)),
    ((1, 0, -1), (1, -1, 1)),
    ((1, -1, 0), (1, 1, 1)),
    ((1, -1, 0), (1, 1, -1)),
    ((1, 1, 2), (1, 1, -1)),
    ((1, 1, -2), (1, 1, 1)),
    ((1, -1, 2), (1, -1, -1)),
    ((-1, 1, 2), (-1, 1, -1)),
    ((1, 2, 1), (1, -1, 1)),
    ((1, -2, 1), (1, 1, 1)),
    ((-1, 2, 1), (1, 1, -1)),
    ((1, 2, -1), (-1, 1, 1)),
    ((2, 1, 1), (-1, 1, 1)),
    ((-2, 1, 1), (1, 1, 1)),
    ((2, -1, 1), (1, 1, -1)),
    ((2, 1, -1), (1, -1, 1)),
)
upper_pairs = [(i, j) for i in range(5) for j in range(i, 5)]
n_sums = 26


def slip_sums_table():
    table = np.zeros((n_sums, 24))
    for s, (normal, direction) in enumerate(system_list):
        q = np.outer(direction, normal) + np.outer(normal, direction)
        k = np.array([(q[0, 0] - q[1, 1]) / 2, -q[2, 2] / 2, q[1, 2], q[0, 2], q[0, 1]])
        weight = 3 if s < 12 else 1
        for e, (i, j) in enumerate(upper_pairs):
            table[e, s] = weight * k[i] * k[j] * (3 if i == j == 1 else 1)
        first = 15 if s < 12 else 20
        table[first : first + 5, s] = k
        table[25, s] = 1
    columns = np.zeros((n_sums, 24))
    for s in range(24):
        word, bit = divmod(s, 12)
        columns[:, 2 * bit + word] = table[:, s] / 2.0**bit
    return columns


def fill_table(table):
    columns = slip_sums_table()
    lane = lax.broadcasted_iota(jnp.int32, (8, 192), 1)
    own = lane % 8 == lax.broadcasted_iota(jnp.int32, (8, 192), 0)
    system = lane // 8
    for e in range(n_sums):
        entry = jnp.zeros((8, 192), jnp.float32)
        for k in range(24):
            if columns[e, k]:
                entry = jnp.where(system == k, float(columns[e, k]), entry)
        table[8 * e : 8 * e + 8] = jnp.where(own, entry, 0.0)


def fitted(function, degree, top):
    series = np.polynomial.chebyshev.Chebyshev.interpolate(function, degree, domain=[0.0, top])
    return [float(c) for c in series.convert(kind=np.polynomial.Polynomial).coef]


angle_top = 3.1416**2
sin_half = fitted(lambda t: math.sqrt(2) * np.sin(np.sqrt(t) / 2) / np.sqrt(t), 4, angle_top)
cos_half = fitted(lambda t: math.sqrt(2) * np.cos(np.sqrt(t) / 2), 4, angle_top)


def polynomial(t, coefs):
    total = coefs[-1] * t + coefs[-2]
    for c in coefs[-3::-1]:
        total = total * t + c
    return total


def sin_cos(x):
    t = x * x
    s = x * polynomial(t, sin_half)
    c = polynomial(t, cos_half)
    return s * c, 1.0 - s * s


def grain_math(stress, angles, hardness, sums, strain):
    exx, eyy, exy, trace, hydro = strain
    s1, c1 = sin_cos(angles[0])
    sq, cq = sin_cos(angles[1])
    s2, c2 = sin_cos(angles[2])
    c1c2, s1s2, c1s2, s1c2 = c1 * c2, s1 * s2, c1 * s2, s1 * c2
    r00 = c1c2 - s1s2 * cq
    r01 = -(c1s2 + s1c2 * cq)
    r02 = s1 * sq
    r10 = s1c2 + c1s2 * cq
    r11 = c1c2 * cq - s1s2
    r12 = -(c1 * sq)
    a0, b0 = r00 * exx + r10 * exy, r10 * eyy + r00 * exy
    a1, b1 = r01 * exx + r11 * exy, r11 * eyy + r01 * exy
    d00 = r00 * a0 + r10 * b0
    d11 = r01 * a1 + r11 * b1
    t00, t11 = stress[0] + d00, stress[1] + d11
    t22 = stress[2] + (trace - (d00 + d11))
    t_sum = t00 + t11
    v = [
        (t00 - t11) * 0.5,
        t_sum * (1 / math.sqrt(12)) - t22 * (2 / math.sqrt(12)),
        stress[3] + (r02 * a1 + r12 * b1),
        stress[4] + (r02 * a0 + r12 * b0),
        stress[5] + (r01 * a0 + r11 * b0),
    ]
    pressure = (t_sum + t22) * (1.0 / 3.0) + hydro
    step = 1.0 / (1.0 + sums(25))
    h0 = hardness * step * (1 / math.sqrt(2))
    h1 = h0 * (1 / math.sqrt(3))
    h2 = h0 * (1.0 / 3.0)
    bias = []
    for i in range(5):
        first, second = (h0, h1) if i == 1 else (h1, h2)
        bias.append(sums(15 + i) * first + sums(20 + i) * second)
    plain, mixed = step * (1 / 18.0), step * (math.sqrt(3) / 18.0)
    m = {}
    for e, (i, j) in enumerate(upper_pairs):
        entry = sums(e) * (mixed if (i == 1) != (j == 1) else plain)
        m[i, j] = m[j, i] = (1.0 - entry) if i == j else entry
    for _ in range(ITERS):
        fresh = []
        for i in range(5):
            off = None
            for j in range(5):
                if j != i:
                    term = m[i, j] * v[j]
                    off = term if off is None else off + term
            fresh.append((m[i, i] * v[i] + bias[i]) - off)
        v = fresh
    w = v[1] * (1 / math.sqrt(3))
    mid = pressure + w
    x = [mid + v[0], mid - v[0], pressure - 2.0 * w, v[2], v[3], v[4]]
    f0 = x[0] * r00 + x[5] * r01 + x[4] * r02
    f1 = x[5] * r00 + x[1] * r01 + x[3] * r02
    f2 = x[4] * r00 + x[3] * r01 + x[2] * r02
    g0 = x[0] * r10 + x[5] * r11 + x[4] * r12
    g1 = x[5] * r10 + x[1] * r11 + x[3] * r12
    g2 = x[4] * r10 + x[3] * r11 + x[2] * r12
    sample = (
        r00 * f0 + r01 * f1 + r02 * f2,
        r10 * g0 + r11 * g1 + r12 * g2,
        r00 * g0 + r01 * g1 + r02 * g2,
    )
    return x, sample


def bit_rows(words):
    pieces = [jnp.concatenate([w[:8], w[8:]], axis=1) for w in words]
    both = jnp.concatenate(pieces, axis=0).astype(jnp.int16)
    rows = [both & jnp.int16(1 << bit) for bit in range(12)]
    return jnp.concatenate(rows, axis=0).astype(jnp.bfloat16)


def places():
    return lax.axis_index("gx"), lax.axis_index("gy")


def sizes():
    return lax.axis_size("gx"), lax.axis_size("gy")


def whole(*shape):
    return pl.BlockSpec(shape, lambda *i: (0,) * len(shape))


def f32(*shape):
    return jax.ShapeDtypeStruct(shape, jnp.float32)


def lane_ids(rows):
    return lax.broadcasted_iota(jnp.int32, (rows, 128), 1)


def row_ids():
    return lax.broadcasted_iota(jnp.int32, (16, 128), 0)


def edges_kernel(velocity, density, donor_faces, fields, x_even, x_odd, y_sent):
    gx, _ = places()
    odd_x = gx % 2 == 1
    fields[0:2] = velocity[...]
    fields[2] = 1.0 / density[...]
    fields[3:5] = donor_faces[...].astype(jnp.float32)
    lane = lane_ids(16)
    x_even[...] = jnp.zeros_like(x_even)
    x_odd[...] = jnp.zeros_like(x_odd)
    edge = jnp.zeros((16, 128), jnp.float32)
    for k in range(5):
        field = fields[k]
        first, last = field[0:1], field[15:16]
        x_even[k : k + 1] = jnp.where(odd_x, first, last)
        x_odd[k : k + 1] = jnp.where(odd_x, last, first)
        edge = jnp.where((lane == 2 * k) | (lane == 2 * k + 1), pltpu.roll(field, 2 * k + 1, 1), edge)
    y_sent[...] = edge


def edge_fields(velocity, density, donor_faces):
    return pl.pallas_call(
        edges_kernel,
        out_shape=[f32(5, 16, 128), f32(8, 128), f32(8, 128), f32(16, 128)],
        compiler_params=pltpu.CompilerParams(vmem_limit_bytes=edge_vmem),
    )(velocity, density, donor_faces)


def from_sides(got_even, got_odd, index, count):
    odd = index % 2 == 1
    after = jnp.where(odd, got_odd, got_even)
    before = jnp.where(odd, got_even, got_odd)
    return jnp.where(index == count - 1, 0.0, after), jnp.where(index == 0, 0.0, before)


def shifts_x(field, east, west):
    row = row_ids()
    return (
        jnp.where(row == 15, east, pltpu.roll(field, 15, 0)),
        jnp.where(row == 0, west, pltpu.roll(field, 1, 0)),
    )


def shifts_y(field, halo):
    lane = lane_ids(field.shape[0])
    return (
        jnp.where(lane == 127, halo, pltpu.roll(field, 127, 1)),
        jnp.where(lane == 0, halo, pltpu.roll(field, 1, 1)),
    )


def side_columns(after, before, first, last):
    lane = lane_ids(after.shape[0])
    return jnp.where(
        lane == 127,
        pltpu.roll(after, 127 - first, 1),
        jnp.where(lane == 0, pltpu.roll(before, (128 - last) % 128, 1), 0.0),
    )


def solve_kernel(
    counts, fields, x_even, x_odd, y_even, y_odd, stress_in, angles_in, hardness_in, active_in,
    relaxed, zone_sum, rows_even, rows_odd, cols_sent,
    stress, angles, hardness, active, table_wide, table, sums_a, sums_b, strain, rows, sems,
):
    block = pl.program_id(0)
    blocks = hardness.shape[0] // grain_block
    gx, gy = places()

    def copies(i, kinds):
        part = pl.ds(i * grain_block, grain_block)
        every = (
            lambda: (active_in.at[:, part], active.at[:, part]),
            lambda: (stress_in.at[:, part], stress.at[:, part]),
            lambda: (angles_in.at[:, part], angles.at[:, part]),
            lambda: (hardness_in.at[part], hardness.at[part]),
        )
        return [pltpu.make_async_copy(*every[k](), sems.at[k, i]) for k in kinds]

    def count(group, sums):
        first = group * batch
        bits = [bit_rows([active[0, first + k], active[1, first + k]]) for k in range(batch)]
        sums[...] = jnp.dot(
            table[...], jnp.concatenate(bits, axis=1), preferred_element_type=jnp.float32
        )

    def update(group, sums):
        lane = lane_ids(8)
        for half in range(2):
            part = pl.ds(8 * half, 8)
            zone_strain = [strain[i, part] for i in range(5)]
            totals = [zone_sum[k, part] for k in range(3)]
            ends = [cols_sent[c, part] for c in range(6)]
            for k in range(batch):
                g = group * batch + k
                lanes = slice(256 * k + 128 * half, 256 * k + 128 * half + 128)
                x, sample = grain_math(
                    [stress[c, g, part] for c in range(6)],
                    [angles[c, g, part] for c in range(3)],
                    hardness[g, part],
                    lambda e: sums[e * 8 : (e + 1) * 8, lanes],
                    zone_strain,
                )
                here = (lane == 2 * g) | (lane == 2 * g + 1)
                for c in range(6):
                    relaxed[c, g - block * grain_block, part] = x[c]
                    ends[c] = jnp.where(here, pltpu.roll(x[c], 2 * g + 1, 1), ends[c])
                totals = [t + s for t, s in zip(totals, sample)]
            for k in range(3):
                zone_sum[k, part] = totals[k]
            for c in range(6):
                cols_sent[c, part] = ends[c]

    @pl.when(block == 0)
    def _():
        for i in range(blocks):
            for copy in copies(i, range(4)):
                copy.start()
        fill_table(table_wide)
        table[...] = table_wide[...].astype(jnp.bfloat16)
        zone_sum[...] = jnp.zeros_like(zone_sum)
        cols_sent[...] = jnp.zeros_like(cols_sent)
        east, west = from_sides(x_even[...], x_odd[...], gx, counts[0])
        north, south = from_sides(y_even[...], y_odd[...], gy, counts[1])
        grads = []
        for k in range(2):
            u = fields[k]
            u_east, u_west = shifts_x(u, east[k : k + 1], west[k : k + 1])
            u_north, u_south = shifts_y(u, side_columns(north, south, 2 * k + 1, 2 * k))
            grads.append(((u_east - u_west) * 0.5, (u_north - u_south) * 0.5))
        exx, eyy = grads[0][0], grads[1][1]
        exy = 0.5 * (grads[0][1] + grads[1][0])
        strain[0] = 2.0 * time_step * exx
        strain[1] = 2.0 * time_step * eyy
        strain[2] = 2.0 * time_step * exy
        strain[3] = 2.0 * time_step * (exx + eyy)
        strain[4] = lame_first * time_step * (exx + eyy)
        copies(0, [0])[0].wait()
        count(0, sums_a)

    for copy in copies(block, [1, 2, 3]):
        copy.wait()

    @pl.when(block < blocks - 1)
    def _():
        copies(block + 1, [0])[0].wait()

    count(block * 2 + 1, sums_b)
    update(block * 2, sums_a)
    count(jnp.minimum(block * 2 + 2, blocks * 2 - 1), sums_a)
    update(block * 2 + 1, sums_b)

    flat = relaxed.reshape(6 * grain_block * 16, 128)
    grains = pl.ds(pl.multiple_of(block * grain_block, grain_block), grain_block)
    for c in range(6):
        start = c * grain_block * 16
        rows[gx % 2, c, grains] = flat[pl.ds(start + 15, grain_block, stride=16)]
        rows[1 - gx % 2, c, grains] = flat[pl.ds(start, grain_block, stride=16)]

    @pl.when(block == blocks - 1)
    def _():
        rows_even[...] = rows[0]
        rows_odd[...] = rows[1]


def solve_grains(fields, got, stress, angles, hardness, active):
    n = hardness.shape[0]
    in_hbm = pl.BlockSpec(memory_space=pltpu.HBM)
    return pl.pallas_call(
        functools.partial(solve_kernel, sizes()),
        grid=(n // grain_block,),
        in_specs=[
            whole(*fields.shape),
            *[whole(*g.shape) for g in got],
            *[in_hbm] * 4,
        ],
        out_specs=[
            pl.BlockSpec((6, grain_block, 16, 128), lambda i: (0, i, 0, 0)),
            whole(3, 16, 128),
            whole(6, n, 128),
            whole(6, n, 128),
            whole(6, 16, 128),
        ],
        out_shape=[f32(6, n, 16, 128), f32(3, 16, 128), f32(6, n, 128), f32(6, n, 128), f32(6, 16, 128)],
        scratch_shapes=[
            pltpu.VMEM(stress.shape, jnp.float32),
            pltpu.VMEM(angles.shape, jnp.float32),
            pltpu.VMEM(hardness.shape, jnp.float32),
            pltpu.VMEM(active.shape, jnp.int32),
            pltpu.VMEM((8 * n_sums, 192), jnp.float32),
            pltpu.VMEM((8 * n_sums, 192), jnp.bfloat16),
            pltpu.VMEM((8 * n_sums, 256 * batch), jnp.float32),
            pltpu.VMEM((8 * n_sums, 256 * batch), jnp.float32),
            pltpu.VMEM((5, 16, 128), jnp.float32),
            pltpu.VMEM((2, 6, n, 128), jnp.float32),
            pltpu.SemaphoreType.DMA((4, n // grain_block)),
        ],
        compiler_params=pltpu.CompilerParams(vmem_limit_bytes=53 * 2**20),
        cost_estimate=pl.CostEstimate(flops=10**8, bytes_accessed=10**7, transcendentals=0),
    )(fields, *got, stress, angles, hardness, active)


def zone_update(counts, fields, f_got, stress, s_got, tall, moved, velocity_out):
    gx, gy = places()
    fx_even, fx_odd, fy_even, fy_odd = f_got
    sx_even, sx_odd, sy_even, sy_odd = s_got
    f_east, f_west = from_sides(fx_even, fx_odd, gx, counts[0])
    f_north, f_south = from_sides(fy_even, fy_odd, gy, counts[1])
    s_east, s_west = from_sides(sx_even, sx_odd, gx, counts[0])
    s_north, s_south = from_sides(sy_even, sy_odd, gy, counts[1])
    for c in range(3):
        tall[c, 0:2] = s_west[2 * c : 2 * c + 2]
        tall[c, 2:18] = stress[c]
        tall[c, 18:20] = s_east[2 * c : 2 * c + 2]
    near = [side_columns(s_north, s_south, 4 * c + 2, 4 * c + 1) for c in range(3)]
    far = [side_columns(s_north, s_south, 4 * c + 3, 4 * c) for c in range(3)]
    lane = lane_ids(16)
    sign = jnp.where(lane == 127, 0.5, -0.5)

    def x_diff(c):
        return (tall[c, 2:20] - tall[c, 0:18]) * 0.5

    def y_diff(c):
        after, before = shifts_y(tall[c, 1:19], near[c][:18])
        return (after - before) * 0.5

    def rim_x(c):
        return (near[c][2:18] - near[c][0:16]) * 0.5

    def rim_y(c):
        return (far[c][1:17] - stress[c]) * sign

    force = [x_diff(0) + y_diff(2), x_diff(2) + y_diff(1)]
    rim_force = [rim_x(0) + rim_y(2), rim_x(2) + rim_y(1)]
    field_rim = [side_columns(f_north, f_south, 2 * k + 1, 2 * k) for k in range(5)]

    def high(k):
        return jnp.concatenate([f_west[k : k + 1], fields[k], f_east[k : k + 1]], axis=0)

    mass = time_step * high(2)
    rim = []
    for k in range(2):
        moved[k, 0:18] = high(k) + mass * force[k]
        rim.append(field_rim[k] + time_step * field_rim[2] * rim_force[k])
    frac_x = time_step * 0.5 * (moved[0, 0:17] + moved[0, 1:18])
    x_self = frac_x * high(3)[:17]
    x_next = frac_x - x_self
    own = [moved[k, 1:17] for k in range(2)]
    y_sides = [shifts_y(own[k], rim[k]) for k in range(2)]
    frac_y = time_step * 0.5 * (own[1] + y_sides[1][0])
    frac_before = time_step * 0.5 * (own[1] + y_sides[1][1])
    flag = fields[4]
    flag_before = jnp.where(lane == 0, field_rim[4], pltpu.roll(flag, 1, 1))
    y_self, before_self = frac_y * flag, frac_before * flag_before
    y_next, before_next = frac_y - y_self, frac_before - before_self
    centre = 1.0 - x_self[1:17] + x_next[0:16] - y_self + before_next
    coefs = (centre, -x_next[1:17], x_self[0:16], -y_next, before_self)
    for k in range(2):
        velocity_out[k] = (
            centre * own[k]
            + coefs[1] * moved[k, 2:18]
            + coefs[2] * moved[k, 0:16]
            + coefs[3] * y_sides[k][0]
            + coefs[4] * y_sides[k][1]
        )
    return coefs


def remap_kernel(
    counts, fields, fx_even, fx_odd, fy_even, fy_odd, stress, sx_even, sx_odd, y_even, y_odd,
    relaxed, rows_even, rows_odd, out, velocity_out, tall, moved, coefs, rows, cols,
):
    block = pl.program_id(0)
    size = relaxed.shape[1]
    gx, gy = places()
    odd_x = gx % 2 == 1
    rows[0] = jnp.where(odd_x, rows_odd[...], rows_even[...])
    rows[1] = jnp.where(odd_x, rows_even[...], rows_odd[...])
    lane, row = lane_ids(16), row_ids()

    @pl.when(block == 0)
    def _():
        fresh = zone_update(
            counts,
            fields,
            (fx_even[...], fx_odd[...], fy_even[...], fy_odd[...]),
            stress,
            (sx_even[...], sx_odd[...], y_even[96:120], y_odd[96:120]),
            tall,
            moved,
            velocity_out,
        )
        centre, east, west, north, south = fresh
        coefs[0] = centre
        coefs[1] = jnp.where(row == 15, 0.0, east)
        coefs[2] = jnp.where(row == 0, 0.0, west)
        coefs[3] = jnp.where(lane == 127, 0.0, north)
        coefs[4] = jnp.where(lane == 0, 0.0, south)
        coefs[5] = jnp.where((row == 15) & (gx < counts[0] - 1), east, 0.0)
        coefs[6] = jnp.where((row == 0) & (gx > 0), west, 0.0)
        rim = jnp.where((lane == 127) & (gy < counts[1] - 1), north, 0.0)
        coefs[7] = jnp.where((lane == 0) & (gy > 0), south, rim)
        odd_y = gy % 2 == 1
        for c in range(6):
            got_even, got_odd = y_even[16 * c : 16 * c + 16], y_odd[16 * c : 16 * c + 16]
            after = pltpu.roll(jnp.where(odd_y, got_odd, got_even), 127, 1)
            before = pltpu.roll(jnp.where(odd_y, got_even, got_odd), 1, 1)
            cols[c] = jnp.where(lane % 2 == 0, after, before)

    centre, east, west, north, south, _, _, rim = [coefs[i] for i in range(8)]
    high_east, low_west = coefs[5, 8:16], coefs[6, 0:8]

    def one(g):
        for c in range(6):
            q = relaxed[c, g]
            halo = pltpu.roll(cols[c], 127 - 2 * (block * size + g), 1)
            total = centre * q + north * pltpu.roll(q, 127, 1) + south * pltpu.roll(q, 1, 1)
            total = total + rim * halo
            total = total + east * pltpu.roll(q, 15, 0) + west * pltpu.roll(q, 1, 0)
            out[c, g, 0:8] = total[:8] + low_west * rows[1, c, pl.ds(g, 1), :]
            out[c, g, 8:16] = total[8:] + high_east * rows[0, c, pl.ds(g, 1), :]

    def some(i, carry):
        for k in range(16):
            one(i * 16 + k)
        return carry

    lax.fori_loop(0, size // 16, some, 0)


def remap_grains(fields, f_got, stress, s_got, y_got, relaxed, rows_even, rows_odd):
    n = relaxed.shape[1]
    size = 16
    small = (fields, *f_got, stress, *s_got, *y_got)
    return pl.pallas_call(
        functools.partial(remap_kernel, sizes()),
        grid=(n // size,),
        in_specs=[
            *[whole(*a.shape) for a in small],
            pl.BlockSpec((6, size, 16, 128), lambda i: (0, i, 0, 0)),
            pl.BlockSpec((6, size, 128), lambda i: (0, i, 0)),
            pl.BlockSpec((6, size, 128), lambda i: (0, i, 0)),
        ],
        out_specs=[
            pl.BlockSpec((6, size, 16, 128), lambda i: (0, i, 0, 0)),
            whole(2, 16, 128),
        ],
        out_shape=[f32(*relaxed.shape), f32(2, 16, 128)],
        scratch_shapes=[
            pltpu.VMEM((3, 24, 128), jnp.float32),
            pltpu.VMEM((2, 24, 128), jnp.float32),
            pltpu.VMEM((8, 16, 128), jnp.float32),
            pltpu.VMEM((2, 6, size, 128), jnp.float32),
            pltpu.VMEM((6, 16, 128), jnp.float32),
        ],
        compiler_params=pltpu.CompilerParams(vmem_limit_bytes=53 * 2**20),
        cost_estimate=pl.CostEstimate(flops=10**7, bytes_accessed=10**7, transcendentals=0),
    )(*small, relaxed, rows_even, rows_odd)


def swap_even(block, axis):
    return lax.ppermute(block, axis, [(i, i ^ 1) for i in range(lax.axis_size(axis))])


def swap_odd(block, axis):
    count = lax.axis_size(axis)
    pairs = []
    for i in range(1, count, 2):
        pairs += [(i, (i + 1) % count), ((i + 1) % count, i)]
    return lax.ppermute(block, axis, pairs)


def swap_odd_crossed(block):
    count = lax.axis_size("gx")
    pairs = []
    for i in range(1, count, 2):
        for a in range(2):
            left, right = i * 2 + a, ((i + 1) % count) * 2 + 1 - a
            pairs += [(left, right), (right, left)]
    return lax.ppermute(block, ("gx", "ga"), pairs)


def per_device(velocity, density, grain_stress, grain_angles, hardness, active, donor_faces):
    gx = lax.axis_index("gx")
    odd_x = gx % 2 == 1
    fields, x_even, x_odd, y_sent = edge_fields(velocity, density, donor_faces)
    f_got = (
        swap_even(x_even, "gx"),
        swap_odd_crossed(x_odd),
        swap_even(y_sent, "gy"),
        swap_odd(y_sent, "gy"),
    )
    relaxed, part, rows_even, rows_odd, cols = solve_grains(
        fields, f_got, grain_stress, grain_angles, hardness, active
    )
    far_rows_odd = swap_odd(rows_odd, "gx")
    far_rows_even = swap_even(rows_even, "gx")
    zone_stress = (part + swap_even(part, "ga")) * (1.0 / G)
    first, last = zone_stress[:, :2], zone_stress[:, -2:]
    got_even = swap_even(jnp.where(odd_x, first, last).reshape(6, 128), "gx")
    got_odd = swap_odd_crossed(jnp.where(odd_x, last, first).reshape(6, 128))
    east, west = from_sides(got_even, got_odd, gx, lax.axis_size("gx"))
    east, west = east.reshape(3, 2, 128), west.reshape(3, 2, 128)
    tall = jnp.concatenate([west[:, 1:], zone_stress, east[:, :1]], axis=1)
    lane = lax.broadcasted_iota(jnp.int32, (18, 128), 1)
    sides = jnp.zeros((18, 128), jnp.float32)
    for c in range(3):
        sides = jnp.where(lane // 4 == c, jnp.roll(tall[c], 4 * c + 2, axis=1), sides)
    sent = jnp.concatenate([cols.reshape(96, 128), jnp.pad(sides, ((0, 6), (0, 0)))], axis=0)
    y_got = (swap_even(sent, "gy"), swap_odd(sent, "gy"))
    stress_out, velocity_out = remap_grains(
        fields, f_got, zone_stress, (got_even, got_odd), y_got, relaxed, far_rows_even, far_rows_odd
    )
    return (velocity_out, stress_out, zone_stress)


def solution(mesh):
    return jax.shard_map(
        per_device,
        mesh=mesh,
        in_specs=(
            P(None, "gx", "gy"),
            P("gx", "gy"),
            P(None, "ga", "gx", "gy"),
            P(None, "ga", "gx", "gy"),
            P("ga", "gx", "gy"),
            P(None, "ga", "gx", "gy"),
            P(None, "gx", "gy"),
        ),
        out_specs=(P(None, "gx", "gy"), P(None, "ga", "gx", "gy"), P(None, "gx", "gy")),
        check_vma=False,
    )
```

```python
import functools
import math

import jax
import jax.numpy as jnp
import numpy as np
from jax import lax
from jax.experimental import pallas as pl
from jax.experimental.pallas import tpu as pltpu
from jax.sharding import PartitionSpec as P

G = 128
ITERS = 4

time_step = 0.1
lame_first = 1.5
batch = 8
grain_block = 2 * batch
field_room = 640
edge_vmem = 63 * 2**20
system_list = (
    ((0, 1, 1), (1, 1, -1)),
    ((0, 1, 1), (1, -1, 1)),
    ((1, 0, 1), (1, 1, -1)),
    ((1, 0, 1), (-1, 1, 1)),
    ((1, 1, 0), (1, -1, 1)),
    ((1, 1, 0), (-1, 1, 1)),
    ((0, 1, -1), (1, 1, 1)),
    ((0, 1, -1), (1, -1, -1)),
    ((1, 0, -1), (1, 1, 1)),
    ((1, 0, -1), (1, -1, 1)),
    ((1, -1, 0), (1, 1, 1)),
    ((1, -1, 0), (1, 1, -1)),
    ((1, 1, 2), (1, 1, -1)),
    ((1, 1, -2), (1, 1, 1)),
    ((1, -1, 2), (1, -1, -1)),
    ((-1, 1, 2), (-1, 1, -1)),
    ((1, 2, 1), (1, -1, 1)),
    ((1, -2, 1), (1, 1, 1)),
    ((-1, 2, 1), (1, 1, -1)),
    ((1, 2, -1), (-1, 1, 1)),
    ((2, 1, 1), (-1, 1, 1)),
    ((-2, 1, 1), (1, 1, 1)),
    ((2, -1, 1), (1, 1, -1)),
    ((2, 1, -1), (1, -1, 1)),
)
upper_pairs = [(i, j) for i in range(5) for j in range(i, 5)]
n_sums = 26


def slip_sums_table():
    table = np.zeros((n_sums, 24))
    for s, (normal, direction) in enumerate(system_list):
        q = np.outer(direction, normal) + np.outer(normal, direction)
        k = np.array([(q[0, 0] - q[1, 1]) / 2, -q[2, 2] / 2, q[1, 2], q[0, 2], q[0, 1]])
        weight = 3 if s < 12 else 1
        for e, (i, j) in enumerate(upper_pairs):
            table[e, s] = weight * k[i] * k[j] * (3 if i == j == 1 else 1)
        first = 15 if s < 12 else 20
        table[first : first + 5, s] = k
        table[25, s] = 1
    columns = np.zeros((n_sums, 24))
    for s in range(24):
        word, bit = divmod(s, 12)
        columns[:, 2 * bit + word] = table[:, s]
    return columns


def fill_table(table):
    columns = slip_sums_table()
    lane = lax.broadcasted_iota(jnp.int32, (8, 192), 1)
    own = lane % 8 == lax.broadcasted_iota(jnp.int32, (8, 192), 0)
    system = lane // 8
    for e in range(n_sums):
        entry = jnp.zeros((8, 192), jnp.float32)
        for k in range(24):
            if columns[e, k]:
                entry = jnp.where(system == k, float(columns[e, k]), entry)
        table[8 * e : 8 * e + 8] = jnp.where(own, entry, 0.0)


def fitted(function, degree, top):
    series = np.polynomial.chebyshev.Chebyshev.interpolate(function, degree, domain=[0.0, top])
    return [float(c) for c in series.convert(kind=np.polynomial.Polynomial).coef]


angle_top = 3.1416**2
sin_half = fitted(lambda t: math.sqrt(2) * np.sin(np.sqrt(t) / 2) / np.sqrt(t), 4, angle_top)
cos_half = fitted(lambda t: math.sqrt(2) * np.cos(np.sqrt(t) / 2), 4, angle_top)


def polynomial(t, coefs):
    total = coefs[-1] * t + coefs[-2]
    for c in coefs[-3::-1]:
        total = total * t + c
    return total


def sin_cos(x):
    t = x * x
    s = x * polynomial(t, sin_half)
    c = polynomial(t, cos_half)
    return s * c, 1.0 - s * s


def grain_math(stress, angles, hardness, sums, strain):
    exx, eyy, exy, trace, hydro = strain
    s1, c1 = sin_cos(angles[0])
    sq, cq = sin_cos(angles[1])
    s2, c2 = sin_cos(angles[2])
    c1c2, s1s2, c1s2, s1c2 = c1 * c2, s1 * s2, c1 * s2, s1 * c2
    r00 = c1c2 - s1s2 * cq
    r01 = -(c1s2 + s1c2 * cq)
    r02 = s1 * sq
    r10 = s1c2 + c1s2 * cq
    r11 = c1c2 * cq - s1s2
    r12 = -(c1 * sq)
    a0, b0 = r00 * exx + r10 * exy, r10 * eyy + r00 * exy
    a1, b1 = r01 * exx + r11 * exy, r11 * eyy + r01 * exy
    d00 = r00 * a0 + r10 * b0
    d11 = r01 * a1 + r11 * b1
    t00, t11 = stress[0] + d00, stress[1] + d11
    t22 = stress[2] + (trace - (d00 + d11))
    t_sum = t00 + t11
    v = [
        (t00 - t11) * 0.5,
        t_sum * (1 / math.sqrt(12)) - t22 * (2 / math.sqrt(12)),
        stress[3] + (r02 * a1 + r12 * b1),
        stress[4] + (r02 * a0 + r12 * b0),
        stress[5] + (r01 * a0 + r11 * b0),
    ]
    pressure = (t_sum + t22) * (1.0 / 3.0) + hydro
    step = 1.0 / (1.0 + sums(25))
    h0 = hardness * step * (1 / math.sqrt(2))
    h1 = h0 * (1 / math.sqrt(3))
    h2 = h0 * (1.0 / 3.0)
    bias = []
    for i in range(5):
        first, second = (h0, h1) if i == 1 else (h1, h2)
        bias.append(sums(15 + i) * first + sums(20 + i) * second)
    plain, mixed = step * (1 / 18.0), step * (math.sqrt(3) / 18.0)
    m = {}
    for e, (i, j) in enumerate(upper_pairs):
        entry = sums(e) * (mixed if (i == 1) != (j == 1) else plain)
        m[i, j] = m[j, i] = (1.0 - entry) if i == j else entry
    for _ in range(ITERS):
        fresh = []
        for i in range(5):
            off = None
            for j in range(5):
                if j != i:
                    term = m[i, j] * v[j]
                    off = term if off is None else off + term
            fresh.append((m[i, i] * v[i] + bias[i]) - off)
        v = fresh
    w = v[1] * (1 / math.sqrt(3))
    mid = pressure + w
    x = [mid + v[0], mid - v[0], pressure - 2.0 * w, v[2], v[3], v[4]]
    f0 = x[0] * r00 + x[5] * r01 + x[4] * r02
    f1 = x[5] * r00 + x[1] * r01 + x[3] * r02
    f2 = x[4] * r00 + x[3] * r01 + x[2] * r02
    g0 = x[0] * r10 + x[5] * r11 + x[4] * r12
    g1 = x[5] * r10 + x[1] * r11 + x[3] * r12
    g2 = x[4] * r10 + x[3] * r11 + x[2] * r12
    sample = (
        r00 * f0 + r01 * f1 + r02 * f2,
        r10 * g0 + r11 * g1 + r12 * g2,
        r00 * g0 + r01 * g1 + r02 * g2,
    )
    return x, sample


def bit_rows(words):
    pieces = [jnp.concatenate([w[:8], w[8:]], axis=1) for w in words]
    both = jnp.concatenate(pieces, axis=0).astype(jnp.int16)
    one, none = jnp.bfloat16(1.0), jnp.bfloat16(0.0)
    rows = [jnp.where((both & jnp.int16(1 << bit)) != 0, one, none) for bit in range(12)]
    return jnp.concatenate(rows, axis=0)


def places():
    return lax.axis_index("gx"), lax.axis_index("gy")


def sizes():
    return lax.axis_size("gx"), lax.axis_size("gy")


def whole(*shape):
    return pl.BlockSpec(shape, lambda *i: (0,) * len(shape))


def f32(*shape):
    return jax.ShapeDtypeStruct(shape, jnp.float32)


def lane_ids(rows):
    return lax.broadcasted_iota(jnp.int32, (rows, 128), 1)


def row_ids():
    return lax.broadcasted_iota(jnp.int32, (16, 128), 0)


def edges_kernel(velocity, density, donor_faces, fields, x_even, x_odd, y_sent):
    gx, _ = places()
    odd_x = gx % 2 == 1
    fields[0:2] = velocity[...]
    fields[2] = 1.0 / density[...]
    fields[3:5] = donor_faces[...].astype(jnp.float32)
    lane = lane_ids(16)
    x_even[...] = jnp.zeros_like(x_even)
    x_odd[...] = jnp.zeros_like(x_odd)
    edge = jnp.zeros((16, 128), jnp.float32)
    for k in range(5):
        field = fields[k]
        first, last = field[0:1], field[15:16]
        x_even[k : k + 1] = jnp.where(odd_x, first, last)
        x_odd[k : k + 1] = jnp.where(odd_x, last, first)
        edge = jnp.where((lane == 2 * k) | (lane == 2 * k + 1), pltpu.roll(field, 2 * k + 1, 1), edge)
    y_sent[...] = edge


def edge_fields(velocity, density, donor_faces):
    return pl.pallas_call(
        edges_kernel,
        grid=(1,),
        in_specs=[whole(2, 16, 128), whole(16, 128), whole(2, 16, 128)],
        out_specs=[whole(5, 16, 128), whole(8, 128), whole(24, 128), whole(16, 128)],
        out_shape=[f32(field_room, 16, 128), f32(8, 128), f32(24, 128), f32(16, 128)],
        compiler_params=pltpu.CompilerParams(vmem_limit_bytes=edge_vmem),
    )(velocity, density, donor_faces)


def from_sides(got_even, got_odd, index, count):
    odd = index % 2 == 1
    after = jnp.where(odd, got_odd, got_even)
    before = jnp.where(odd, got_even, got_odd)
    return jnp.where(index == count - 1, 0.0, after), jnp.where(index == 0, 0.0, before)


def shifts_x(field, east, west):
    row = row_ids()
    return (
        jnp.where(row == 15, east, pltpu.roll(field, 15, 0)),
        jnp.where(row == 0, west, pltpu.roll(field, 1, 0)),
    )


def shifts_y(field, halo):
    lane = lane_ids(field.shape[0])
    return (
        jnp.where(lane == 127, halo, pltpu.roll(field, 127, 1)),
        jnp.where(lane == 0, halo, pltpu.roll(field, 1, 1)),
    )


def side_columns(after, before, first, last):
    lane = lane_ids(after.shape[0])
    return jnp.where(
        lane == 127,
        pltpu.roll(after, 127 - first, 1),
        jnp.where(lane == 0, pltpu.roll(before, (128 - last) % 128, 1), 0.0),
    )


def solve_kernel(
    counts, fields, x_even, x_odd, y_even, y_odd, stress_in, angles_in, hardness_in, active_in,
    relaxed, zone_sum, rows_even, rows_odd, cols_even, cols_odd,
    stress, angles, hardness, active, table_wide, table, sums_a, sums_b, strain, rows, cols, sems,
):
    block = pl.program_id(0)
    batches = hardness.shape[0] // batch
    gx, gy = places()

    def copies(i, kinds):
        part = pl.ds(i * batch, batch)
        every = (
            lambda: (active_in.at[:, part], active.at[:, part]),
            lambda: (stress_in.at[:, part], stress.at[:, part]),
            lambda: (angles_in.at[:, part], angles.at[:, part]),
            lambda: (hardness_in.at[part], hardness.at[part]),
        )
        return [pltpu.make_async_copy(*every[k](), sems.at[k, i]) for k in kinds]

    def count(group, sums):
        first = group * batch
        bits = [bit_rows([active[0, first + k], active[1, first + k]]) for k in range(batch)]
        sums[...] = jnp.dot(
            table[...], jnp.concatenate(bits, axis=1), preferred_element_type=jnp.float32
        )

    def update(group, sums):
        lane = lane_ids(8)
        for half in range(2):
            part = pl.ds(8 * half, 8)
            zone_strain = [strain[i, part] for i in range(5)]
            totals = [zone_sum[k, part] for k in range(3)]
            ends = [cols[c, part] for c in range(6)]
            for k in range(batch):
                g = group * batch + k
                lanes = slice(256 * k + 128 * half, 256 * k + 128 * half + 128)
                x, sample = grain_math(
                    [stress[c, g, part] for c in range(6)],
                    [angles[c, g, part] for c in range(3)],
                    hardness[g, part],
                    lambda e: sums[e * 8 : (e + 1) * 8, lanes],
                    zone_strain,
                )
                here = (lane == 2 * g) | (lane == 2 * g + 1)
                for c in range(6):
                    relaxed[c, g - block * grain_block, part] = x[c]
                    ends[c] = jnp.where(here, pltpu.roll(x[c], 2 * g + 1, 1), ends[c])
                totals = [t + s for t, s in zip(totals, sample)]
            for k in range(3):
                zone_sum[k, part] = totals[k]
            for c in range(6):
                cols[c, part] = ends[c]

    @pl.when(block == 0)
    def _():
        for i in range(batches):
            for copy in copies(i, range(4)):
                copy.start()
        fill_table(table_wide)
        table[...] = table_wide[...].astype(jnp.bfloat16)
        zone_sum[...] = jnp.zeros_like(zone_sum)
        cols[...] = jnp.zeros_like(cols)
        east, west = from_sides(x_even[...], x_odd[0:8], gx, counts[0])
        north, south = from_sides(y_even[...], y_odd[...], gy, counts[1])
        grads = []
        for k in range(2):
            u = fields[k]
            u_east, u_west = shifts_x(u, east[k : k + 1], west[k : k + 1])
            u_north, u_south = shifts_y(u, side_columns(north, south, 2 * k + 1, 2 * k))
            grads.append(((u_east - u_west) * 0.5, (u_north - u_south) * 0.5))
        exx, eyy = grads[0][0], grads[1][1]
        exy = 0.5 * (grads[0][1] + grads[1][0])
        strain[0] = 2.0 * time_step * exx
        strain[1] = 2.0 * time_step * eyy
        strain[2] = 2.0 * time_step * exy
        strain[3] = 2.0 * time_step * (exx + eyy)
        strain[4] = lame_first * time_step * (exx + eyy)
        copies(0, [0])[0].wait()
        count(0, sums_a)

    group = block * 2
    for copy in copies(group, [1, 2, 3]) + copies(group + 1, [0]):
        copy.wait()
    count(group + 1, sums_b)
    update(group, sums_a)
    for copy in copies(group + 1, [1, 2, 3]):
        copy.wait()

    @pl.when(group + 2 < batches)
    def _():
        copies(group + 2, [0])[0].wait()

    count(jnp.minimum(group + 2, batches - 1), sums_a)
    update(group + 1, sums_b)

    flat = relaxed.reshape(6 * grain_block * 16, 128)
    grains = pl.ds(pl.multiple_of(block * grain_block, grain_block), grain_block)
    for c in range(6):
        start = c * grain_block * 16
        rows[gx % 2, c, grains] = flat[pl.ds(start + 15, grain_block, stride=16)]
        rows[1 - gx % 2, c, grains] = flat[pl.ds(start, grain_block, stride=16)]

    @pl.when(group + 2 == batches)
    def _():
        rows_even[...] = rows[0]
        rows_odd[...] = rows[1]
        low = lane_ids(16) % 2 == 0
        odd_y = gy % 2 == 1
        for c in range(3):
            one, other = cols[c], cols[c + 3]
            last = jnp.where(low, one, pltpu.roll(other, 1, 1))
            first = jnp.where(low, pltpu.roll(one, 127, 1), other)
            cols_even[c] = jnp.where(odd_y, first, last)
            cols_odd[c] = jnp.where(odd_y, last, first)


def solve_grains(fields, got, stress, angles, hardness, active):
    n = hardness.shape[0]
    in_hbm = pl.BlockSpec(memory_space=pltpu.HBM)
    return pl.pallas_call(
        functools.partial(solve_kernel, sizes()),
        grid=(n // grain_block,),
        in_specs=[
            whole(5, 16, 128),
            *[whole(*g.shape) for g in got],
            *[in_hbm] * 4,
        ],
        out_specs=[
            pl.BlockSpec((6, grain_block, 16, 128), lambda i: (0, i, 0, 0)),
            whole(3, 16, 128),
            whole(6, n, 128),
            whole(6, n, 128),
            whole(3, 16, 128),
            whole(3, 16, 128),
        ],
        out_shape=[f32(6, n, 16, 128), f32(3, 16, 128), f32(6, n, 128), f32(6, n, 128)]
        + [f32(3, 16, 128)] * 2,
        scratch_shapes=[
            pltpu.VMEM(stress.shape, jnp.float32),
            pltpu.VMEM(angles.shape, jnp.float32),
            pltpu.VMEM(hardness.shape, jnp.float32),
            pltpu.VMEM(active.shape, jnp.int32),
            pltpu.VMEM((8 * n_sums, 192), jnp.float32),
            pltpu.VMEM((8 * n_sums, 192), jnp.bfloat16),
            pltpu.VMEM((8 * n_sums, 256 * batch), jnp.float32),
            pltpu.VMEM((8 * n_sums, 256 * batch), jnp.float32),
            pltpu.VMEM((5, 16, 128), jnp.float32),
            pltpu.VMEM((2, 6, n, 128), jnp.float32),
            pltpu.VMEM((6, 16, 128), jnp.float32),
            pltpu.SemaphoreType.DMA((4, n // batch)),
        ],
        compiler_params=pltpu.CompilerParams(vmem_limit_bytes=53 * 2**20),
        cost_estimate=pl.CostEstimate(flops=10**8, bytes_accessed=10**7, transcendentals=0),
    )(fields, *got, stress, angles, hardness, active)


def zone_update(counts, fields, f_got, stress, s_got, tall, moved, velocity_out):
    gx, gy = places()
    fx_even, fx_odd, fy_even, fy_odd = f_got
    sx_even, sx_odd, sy_even, sy_odd = s_got
    f_east, f_west = from_sides(fx_even, fx_odd[0:8], gx, counts[0])
    f_north, f_south = from_sides(fy_even, fy_odd, gy, counts[1])
    s_east, s_west = from_sides(sx_even, sx_odd, gx, counts[0])
    s_north, s_south = from_sides(sy_even, sy_odd, gy, counts[1])
    for c in range(3):
        tall[c, 0:2] = s_west[2 * c : 2 * c + 2]
        tall[c, 2:18] = stress[c]
        tall[c, 18:20] = s_east[2 * c : 2 * c + 2]
    near = [side_columns(s_north, s_south, 4 * c + 2, 4 * c + 1) for c in range(3)]
    far = [side_columns(s_north, s_south, 4 * c + 3, 4 * c) for c in range(3)]
    lane = lane_ids(16)
    sign = jnp.where(lane == 127, 0.5, -0.5)

    def x_diff(c):
        return (tall[c, 2:20] - tall[c, 0:18]) * 0.5

    def y_diff(c):
        after, before = shifts_y(tall[c, 1:19], near[c][:18])
        return (after - before) * 0.5

    def rim_x(c):
        return (near[c][2:18] - near[c][0:16]) * 0.5

    def rim_y(c):
        return (far[c][1:17] - stress[c]) * sign

    force = [x_diff(0) + y_diff(2), x_diff(2) + y_diff(1)]
    rim_force = [rim_x(0) + rim_y(2), rim_x(2) + rim_y(1)]
    field_rim = [side_columns(f_north, f_south, 2 * k + 1, 2 * k) for k in range(5)]

    def high(k):
        return jnp.concatenate([f_west[k : k + 1], fields[k], f_east[k : k + 1]], axis=0)

    mass = time_step * high(2)
    rim = []
    for k in range(2):
        moved[k, 0:18] = high(k) + mass * force[k]
        rim.append(field_rim[k] + time_step * field_rim[2] * rim_force[k])
    frac_x = time_step * 0.5 * (moved[0, 0:17] + moved[0, 1:18])
    x_self = frac_x * high(3)[:17]
    x_next = frac_x - x_self
    own = [moved[k, 1:17] for k in range(2)]
    y_sides = [shifts_y(own[k], rim[k]) for k in range(2)]
    frac_y = time_step * 0.5 * (own[1] + y_sides[1][0])
    frac_before = time_step * 0.5 * (own[1] + y_sides[1][1])
    flag = fields[4]
    flag_before = jnp.where(lane == 0, field_rim[4], pltpu.roll(flag, 1, 1))
    y_self, before_self = frac_y * flag, frac_before * flag_before
    y_next, before_next = frac_y - y_self, frac_before - before_self
    centre = 1.0 - x_self[1:17] + x_next[0:16] - y_self + before_next
    coefs = (centre, -x_next[1:17], x_self[0:16], -y_next, before_self)
    for k in range(2):
        velocity_out[k] = (
            centre * own[k]
            + coefs[1] * moved[k, 2:18]
            + coefs[2] * moved[k, 0:16]
            + coefs[3] * y_sides[k][0]
            + coefs[4] * y_sides[k][1]
        )
    return coefs


def remap_kernel(
    counts, fields, fx_even, fx_odd, fy_even, fy_odd, stress, sx_even, sx_odd, y_even, y_odd,
    relaxed_in, rows_even, rows_odd,
    out, velocity_out, relaxed, tall, moved, coefs, rows, cols, sems,
):
    block = pl.program_id(0)
    size = out.shape[1]
    gx, gy = places()
    odd_x = gx % 2 == 1

    def copy(i):
        part = pl.ds(i * size, size)
        return pltpu.make_async_copy(relaxed_in.at[:, part], relaxed.at[:, part], sems.at[i])

    @pl.when(block == 0)
    def _():
        for i in range(relaxed.shape[1] // size):
            copy(i).start()

    rows[0] = jnp.where(odd_x, rows_odd[...], rows_even[...])
    rows[1] = jnp.where(odd_x, rows_even[...], rows_odd[...])
    lane, row = lane_ids(16), row_ids()

    @pl.when(block == 0)
    def _():
        fresh = zone_update(
            counts,
            fields,
            (fx_even[...], fx_odd[...], fy_even[...], fy_odd[...]),
            stress,
            (sx_even[...], sx_odd[0:6], y_even[48:72], y_odd[48:72]),
            tall,
            moved,
            velocity_out,
        )
        centre, east, west, north, south = fresh
        coefs[0] = centre
        coefs[1] = jnp.where(row == 15, 0.0, east)
        coefs[2] = jnp.where(row == 0, 0.0, west)
        coefs[3] = jnp.where(lane == 127, 0.0, north)
        coefs[4] = jnp.where(lane == 0, 0.0, south)
        coefs[5] = jnp.where((row == 15) & (gx < counts[0] - 1), east, 0.0)
        coefs[6] = jnp.where((row == 0) & (gx > 0), west, 0.0)
        rim = jnp.where((lane == 127) & (gy < counts[1] - 1), north, 0.0)
        coefs[7] = jnp.where((lane == 0) & (gy > 0), south, rim)
        odd_y = gy % 2 == 1
        for c in range(3):
            part = slice(16 * c, 16 * c + 16)
            got_even, got_odd = y_even[part], y_odd[part]
            after = jnp.where(odd_y, got_odd, got_even)
            before = jnp.where(odd_y, got_even, got_odd)
            cols[c] = jnp.where(lane % 2 == 0, after, pltpu.roll(before, 1, 1))
            cols[c + 3] = jnp.where(lane % 2 == 0, pltpu.roll(after, 127, 1), before)

    centre, east, west, north, south, _, _, rim = [coefs[i] for i in range(8)]
    high_east, low_west = coefs[5, 8:16], coefs[6, 0:8]
    copy(block).wait()

    def one(g):
        for c in range(6):
            q = relaxed[c, block * size + g]
            halo = pltpu.roll(cols[c], 127 - 2 * (block * size + g), 1)
            total = centre * q + north * pltpu.roll(q, 127, 1) + south * pltpu.roll(q, 1, 1)
            total = total + rim * halo
            total = total + east * pltpu.roll(q, 15, 0) + west * pltpu.roll(q, 1, 0)
            out[c, g, 0:8] = total[:8] + low_west * rows[1, c, pl.ds(g, 1), :]
            out[c, g, 8:16] = total[8:] + high_east * rows[0, c, pl.ds(g, 1), :]

    def some(i, carry):
        for k in range(16):
            one(i * 16 + k)
        return carry

    lax.fori_loop(0, size // 16, some, 0)


def remap_grains(fields, f_got, stress, s_got, y_got, relaxed, rows_even, rows_odd):
    n = relaxed.shape[1]
    size = 16
    small = (*f_got, stress, *s_got, *y_got)
    return pl.pallas_call(
        functools.partial(remap_kernel, sizes()),
        grid=(n // size,),
        in_specs=[
            whole(5, 16, 128),
            *[whole(*a.shape) for a in small],
            pl.BlockSpec(memory_space=pltpu.HBM),
            pl.BlockSpec((6, size, 128), lambda i: (0, i, 0)),
            pl.BlockSpec((6, size, 128), lambda i: (0, i, 0)),
        ],
        out_specs=[
            pl.BlockSpec((6, size, 16, 128), lambda i: (0, i, 0, 0)),
            whole(2, 16, 128),
        ],
        out_shape=[f32(*relaxed.shape), f32(2, 16, 128)],
        scratch_shapes=[
            pltpu.VMEM(relaxed.shape, jnp.float32),
            pltpu.VMEM((3, 24, 128), jnp.float32),
            pltpu.VMEM((2, 24, 128), jnp.float32),
            pltpu.VMEM((8, 16, 128), jnp.float32),
            pltpu.VMEM((2, 6, size, 128), jnp.float32),
            pltpu.VMEM((6, 16, 128), jnp.float32),
            pltpu.SemaphoreType.DMA((n // size,)),
        ],
        compiler_params=pltpu.CompilerParams(vmem_limit_bytes=53 * 2**20),
        cost_estimate=pl.CostEstimate(flops=10**7, bytes_accessed=10**7, transcendentals=0),
    )(fields, *small, relaxed, rows_even, rows_odd)


def swap_even(block, axis):
    return lax.ppermute(block, axis, [(i, i ^ 1) for i in range(lax.axis_size(axis))])


def swap_odd(block, axis):
    count = lax.axis_size(axis)
    pairs = []
    for i in range(1, count, 2):
        pairs += [(i, (i + 1) % count), ((i + 1) % count, i)]
    return lax.ppermute(block, axis, pairs)


def swap_odd_crossed(block):
    count = lax.axis_size("gx")
    pairs = []
    for i in range(1, count, 2):
        for a in range(2):
            left, right = i * 2 + a, ((i + 1) % count) * 2 + 1 - a
            pairs += [(left, right), (right, left)]
    return lax.ppermute(block, ("gx", "ga"), pairs)


def per_device(velocity, density, grain_stress, grain_angles, hardness, active, donor_faces):
    gx = lax.axis_index("gx")
    odd_x = gx % 2 == 1
    fields, x_even, x_odd, y_sent = edge_fields(velocity, density, donor_faces)
    f_got = (
        swap_even(x_even, "gx"),
        swap_odd_crossed(x_odd),
        swap_even(y_sent, "gy"),
        swap_odd(y_sent, "gy"),
    )
    relaxed, part, rows_even, rows_odd, cols_even, cols_odd = solve_grains(
        fields, f_got, grain_stress, grain_angles, hardness, active
    )
    far_rows_odd = swap_odd(rows_odd, "gx")
    far_rows_even = swap_even(rows_even, "gx")
    zone_stress = (part + swap_even(part, "ga")) * (1.0 / G)
    first, last = zone_stress[:, :2], zone_stress[:, -2:]
    got_even = swap_even(jnp.where(odd_x, first, last).reshape(6, 128), "gx")
    to_odd = jnp.pad(jnp.where(odd_x, last, first).reshape(6, 128), ((0, 10), (0, 0)))
    got_odd = swap_odd_crossed(to_odd)
    east, west = from_sides(got_even, got_odd[:6], gx, lax.axis_size("gx"))
    east, west = east.reshape(3, 2, 128), west.reshape(3, 2, 128)
    tall = jnp.concatenate([west[:, 1:], zone_stress, east[:, :1]], axis=1)
    lane = lax.broadcasted_iota(jnp.int32, (18, 128), 1)
    sides = jnp.zeros((18, 128), jnp.float32)
    for c in range(3):
        sides = jnp.where(lane // 4 == c, jnp.roll(tall[c], 4 * c + 2, axis=1), sides)
    sides = jnp.pad(sides, ((0, 6), (0, 0)))
    y_got = (
        swap_even(jnp.concatenate([cols_even.reshape(48, 128), sides], axis=0), "gy"),
        swap_odd(jnp.concatenate([cols_odd.reshape(48, 128), sides], axis=0), "gy"),
    )
    stress_out, velocity_out = remap_grains(
        fields, f_got, zone_stress, (got_even, got_odd), y_got, relaxed, far_rows_even, far_rows_odd
    )
    return (velocity_out, stress_out, zone_stress)


def solution(mesh):
    return jax.shard_map(
        per_device,
        mesh=mesh,
        in_specs=(
            P(None, "gx", "gy"),
            P("gx", "gy"),
            P(None, "ga", "gx", "gy"),
            P(None, "ga", "gx", "gy"),
            P("ga", "gx", "gy"),
            P(None, "ga", "gx", "gy"),
            P(None, "gx", "gy"),
        ),
        out_specs=(P(None, "gx", "gy"), P(None, "ga", "gx", "gy"), P(None, "gx", "gy")),
        check_vma=False,
    )
```

```python
import functools
import math

import jax
import jax.numpy as jnp
import numpy as np
from jax import lax
from jax.experimental import pallas as pl
from jax.experimental.pallas import tpu as pltpu
from jax.sharding import PartitionSpec as P

G = 128
ITERS = 4

time_step = 0.1
lame_first = 1.5
batch = 4
grain_block = 2 * batch
system_list = (
    ((0, 1, 1), (1, 1, -1)),
    ((0, 1, 1), (1, -1, 1)),
    ((1, 0, 1), (1, 1, -1)),
    ((1, 0, 1), (-1, 1, 1)),
    ((1, 1, 0), (1, -1, 1)),
    ((1, 1, 0), (-1, 1, 1)),
    ((0, 1, -1), (1, 1, 1)),
    ((0, 1, -1), (1, -1, -1)),
    ((1, 0, -1), (1, 1, 1)),
    ((1, 0, -1), (1, -1, 1)),
    ((1, -1, 0), (1, 1, 1)),
    ((1, -1, 0), (1, 1, -1)),
    ((1, 1, 2), (1, 1, -1)),
    ((1, 1, -2), (1, 1, 1)),
    ((1, -1, 2), (1, -1, -1)),
    ((-1, 1, 2), (-1, 1, -1)),
    ((1, 2, 1), (1, -1, 1)),
    ((1, -2, 1), (1, 1, 1)),
    ((-1, 2, 1), (1, 1, -1)),
    ((1, 2, -1), (-1, 1, 1)),
    ((2, 1, 1), (-1, 1, 1)),
    ((-2, 1, 1), (1, 1, 1)),
    ((2, -1, 1), (1, 1, -1)),
    ((2, 1, -1), (1, -1, 1)),
)
upper_pairs = [(i, j) for i in range(5) for j in range(i, 5)]
n_sums = 26


def slip_sums_table():
    table = np.zeros((n_sums, 24))
    for s, (normal, direction) in enumerate(system_list):
        q = np.outer(direction, normal) + np.outer(normal, direction)
        k = np.array([(q[0, 0] - q[1, 1]) / 2, -q[2, 2] / 2, q[1, 2], q[0, 2], q[0, 1]])
        weight = 3 if s < 12 else 1
        for e, (i, j) in enumerate(upper_pairs):
            table[e, s] = weight * k[i] * k[j] * (3 if i == j == 1 else 1)
        first = 15 if s < 12 else 20
        table[first : first + 5, s] = k
        table[25, s] = 1
    columns = np.zeros((n_sums, 24))
    for s in range(24):
        word, bit = divmod(s, 12)
        columns[:, 2 * bit + word] = table[:, s]
    return columns


def fill_table(table):
    columns = slip_sums_table()
    lane = lax.broadcasted_iota(jnp.int32, (8, 192), 1)
    own = lane % 8 == lax.broadcasted_iota(jnp.int32, (8, 192), 0)
    system = lane // 8
    for e in range(n_sums):
        entry = jnp.zeros((8, 192), jnp.float32)
        for k in range(24):
            if columns[e, k]:
                entry = jnp.where(system == k, float(columns[e, k]), entry)
        table[8 * e : 8 * e + 8] = jnp.where(own, entry, 0.0)


def fitted(function, degree, top):
    series = np.polynomial.chebyshev.Chebyshev.interpolate(function, degree, domain=[0.0, top])
    return [float(c) for c in series.convert(kind=np.polynomial.Polynomial).coef]


angle_top = 3.1416**2
sin_half = fitted(lambda t: math.sqrt(2) * np.sin(np.sqrt(t) / 2) / np.sqrt(t), 4, angle_top)
cos_half = fitted(lambda t: math.sqrt(2) * np.cos(np.sqrt(t) / 2), 4, angle_top)


def polynomial(t, coefs):
    total = coefs[-1] * t + coefs[-2]
    for c in coefs[-3::-1]:
        total = total * t + c
    return total


def sin_cos(x):
    t = x * x
    s = x * polynomial(t, sin_half)
    c = polynomial(t, cos_half)
    return s * c, 1.0 - s * s


def grain_math(stress, angles, hardness, sums, strain):
    exx, eyy, exy, trace, hydro = strain
    s1, c1 = sin_cos(angles[0])
    sq, cq = sin_cos(angles[1])
    s2, c2 = sin_cos(angles[2])
    c1c2, s1s2, c1s2, s1c2 = c1 * c2, s1 * s2, c1 * s2, s1 * c2
    r00 = c1c2 - s1s2 * cq
    r01 = -(c1s2 + s1c2 * cq)
    r02 = s1 * sq
    r10 = s1c2 + c1s2 * cq
    r11 = c1c2 * cq - s1s2
    r12 = -(c1 * sq)
    a0, b0 = r00 * exx + r10 * exy, r10 * eyy + r00 * exy
    a1, b1 = r01 * exx + r11 * exy, r11 * eyy + r01 * exy
    d00 = r00 * a0 + r10 * b0
    d11 = r01 * a1 + r11 * b1
    t00, t11 = stress[0] + d00, stress[1] + d11
    t22 = stress[2] + (trace - (d00 + d11))
    t_sum = t00 + t11
    v = [
        (t00 - t11) * 0.5,
        t_sum * (1 / math.sqrt(12)) - t22 * (2 / math.sqrt(12)),
        stress[3] + (r02 * a1 + r12 * b1),
        stress[4] + (r02 * a0 + r12 * b0),
        stress[5] + (r01 * a0 + r11 * b0),
    ]
    pressure = (t_sum + t22) * (1.0 / 3.0) + hydro
    step = 1.0 / (1.0 + sums(25))
    h0 = hardness * step * (1 / math.sqrt(2))
    h1 = h0 * (1 / math.sqrt(3))
    h2 = h0 * (1.0 / 3.0)
    bias = []
    for i in range(5):
        first, second = (h0, h1) if i == 1 else (h1, h2)
        bias.append(sums(15 + i) * first + sums(20 + i) * second)
    plain, mixed = step * (1 / 18.0), step * (math.sqrt(3) / 18.0)
    m = {}
    for e, (i, j) in enumerate(upper_pairs):
        entry = sums(e) * (mixed if (i == 1) != (j == 1) else plain)
        m[i, j] = m[j, i] = (1.0 - entry) if i == j else entry
    for _ in range(ITERS):
        fresh = []
        for i in range(5):
            off = None
            for j in range(5):
                if j != i:
                    term = m[i, j] * v[j]
                    off = term if off is None else off + term
            fresh.append((m[i, i] * v[i] + bias[i]) - off)
        v = fresh
    w = v[1] * (1 / math.sqrt(3))
    mid = pressure + w
    x = [mid + v[0], mid - v[0], pressure - 2.0 * w, v[2], v[3], v[4]]
    f0 = x[0] * r00 + x[5] * r01 + x[4] * r02
    f1 = x[5] * r00 + x[1] * r01 + x[3] * r02
    f2 = x[4] * r00 + x[3] * r01 + x[2] * r02
    g0 = x[0] * r10 + x[5] * r11 + x[4] * r12
    g1 = x[5] * r10 + x[1] * r11 + x[3] * r12
    g2 = x[4] * r10 + x[3] * r11 + x[2] * r12
    sample = (
        r00 * f0 + r01 * f1 + r02 * f2,
        r10 * g0 + r11 * g1 + r12 * g2,
        r00 * g0 + r01 * g1 + r02 * g2,
    )
    return x, sample


def bit_rows(words):
    pieces = [jnp.concatenate([w[:8], w[8:]], axis=1) for w in words]
    both = jnp.concatenate(pieces, axis=0).astype(jnp.int16)
    one, none = jnp.bfloat16(1.0), jnp.bfloat16(0.0)
    rows = [jnp.where((both & jnp.int16(1 << bit)) != 0, one, none) for bit in range(12)]
    return jnp.concatenate(rows, axis=0)


def places():
    return lax.axis_index("gx"), lax.axis_index("gy")


def sizes():
    return lax.axis_size("gx"), lax.axis_size("gy")


def whole(*shape):
    return pl.BlockSpec(shape, lambda *i: (0,) * len(shape))


def f32(*shape):
    return jax.ShapeDtypeStruct(shape, jnp.float32)


def lane_ids(rows):
    return lax.broadcasted_iota(jnp.int32, (rows, 128), 1)


def row_ids():
    return lax.broadcasted_iota(jnp.int32, (16, 128), 0)


def from_sides(got_even, got_odd, index, count):
    odd = index % 2 == 1
    after = jnp.where(odd, got_odd, got_even)
    before = jnp.where(odd, got_even, got_odd)
    return jnp.where(index == count - 1, 0.0, after), jnp.where(index == 0, 0.0, before)


def shifts_x(field, east, west):
    row = row_ids()
    return (
        jnp.where(row == 15, east, pltpu.roll(field, 15, 0)),
        jnp.where(row == 0, west, pltpu.roll(field, 1, 0)),
    )


def shifts_y(field, halo):
    lane = lane_ids(field.shape[0])
    return (
        jnp.where(lane == 127, halo, pltpu.roll(field, 127, 1)),
        jnp.where(lane == 0, halo, pltpu.roll(field, 1, 1)),
    )


def side_columns(after, before, first, last):
    lane = lane_ids(after.shape[0])
    return jnp.where(
        lane == 127,
        pltpu.roll(after, 127 - first, 1),
        jnp.where(lane == 0, pltpu.roll(before, (128 - last) % 128, 1), 0.0),
    )


def velocity_halo(counts, got):
    gx, gy = places()
    after_x, before_x = from_sides(got[0], got[1], gx, counts[0])
    after_y, before_y = from_sides(got[2], got[3], gy, counts[1])
    return after_x[0:1], before_x[15:16], side_columns(after_y, before_y, 0, 127)


def solve_kernel(
    counts, half_velocity, x_even, x_odd, y_even, y_odd, stress_in, angles_in, hardness_in, active_in,
    relaxed, zone_sum, rows_even, rows_odd, cols_even, cols_odd,
    stress, angles, hardness, active, table_wide, table, sums_a, sums_b, strain, rows, cols, sems,
):
    block = pl.program_id(0)
    batches = hardness.shape[0] // batch
    gx, gy = places()

    def copies(i, kinds):
        part = pl.ds(i * batch, batch)
        every = (
            lambda: (active_in.at[:, part], active.at[:, part]),
            lambda: (stress_in.at[:, part], stress.at[:, part]),
            lambda: (angles_in.at[:, part], angles.at[:, part]),
            lambda: (hardness_in.at[part], hardness.at[part]),
        )
        return [pltpu.make_async_copy(*every[k](), sems.at[k, i]) for k in kinds]

    def count(group, sums):
        first = group * batch
        bits = [bit_rows([active[0, first + k], active[1, first + k]]) for k in range(batch)]
        sums[...] = jnp.dot(
            table[...], jnp.concatenate(bits, axis=1), preferred_element_type=jnp.float32
        )

    def update(group, sums):
        lane = lane_ids(8)
        for half in range(2):
            part = pl.ds(8 * half, 8)
            zone_strain = [strain[i, part] for i in range(5)]
            totals = [zone_sum[k, part] for k in range(3)]
            ends = [cols[c, part] for c in range(6)]
            for k in range(batch):
                g = group * batch + k
                lanes = slice(256 * k + 128 * half, 256 * k + 128 * half + 128)
                x, sample = grain_math(
                    [stress[c, g, part] for c in range(6)],
                    [angles[c, g, part] for c in range(3)],
                    hardness[g, part],
                    lambda e: sums[e * 8 : (e + 1) * 8, lanes],
                    zone_strain,
                )
                here = (lane == 2 * g) | (lane == 2 * g + 1)
                for c in range(6):
                    relaxed[c, g - block * grain_block, part] = x[c]
                    ends[c] = jnp.where(here, pltpu.roll(x[c], 2 * g + 1, 1), ends[c])
                totals = [t + s for t, s in zip(totals, sample)]
            for k in range(3):
                zone_sum[k, part] = totals[k]
            for c in range(6):
                cols[c, part] = ends[c]

    @pl.when(block == 0)
    def _():
        for i in range(batches):
            for copy in copies(i, range(4)):
                copy.start()
        fill_table(table_wide)
        table[...] = table_wide[...].astype(jnp.bfloat16)
        zone_sum[...] = jnp.zeros_like(zone_sum)
        cols[...] = jnp.zeros_like(cols)
        grads = []
        for k in range(2):
            u = half_velocity[k]
            east, west, halo = velocity_halo(counts, (x_even[k], x_odd[k], y_even[k], y_odd[k]))
            u_east, u_west = shifts_x(u, 0.5 * east, 0.5 * west)
            u_north, u_south = shifts_y(u, 0.5 * halo)
            grads.append((u_east - u_west, u_north - u_south))
        exx, eyy = grads[0][0], grads[1][1]
        exy = 0.5 * (grads[0][1] + grads[1][0])
        strain[0] = 2.0 * time_step * exx
        strain[1] = 2.0 * time_step * eyy
        strain[2] = 2.0 * time_step * exy
        strain[3] = 2.0 * time_step * (exx + eyy)
        strain[4] = lame_first * time_step * (exx + eyy)
        copies(0, [0])[0].wait()
        count(0, sums_a)

    group = block * 2
    for copy in copies(group, [1, 2, 3]) + copies(group + 1, [0]):
        copy.wait()
    count(group + 1, sums_b)
    update(group, sums_a)
    for copy in copies(group + 1, [1, 2, 3]):
        copy.wait()

    @pl.when(group + 2 < batches)
    def _():
        copies(group + 2, [0])[0].wait()

    count(jnp.minimum(group + 2, batches - 1), sums_a)
    update(group + 1, sums_b)

    flat = relaxed.reshape(6 * grain_block * 16, 128)
    grains = pl.ds(pl.multiple_of(block * grain_block, grain_block), grain_block)
    for c in range(6):
        start = c * grain_block * 16
        rows[gx % 2, c, grains] = flat[pl.ds(start + 15, grain_block, stride=16)]
        rows[1 - gx % 2, c, grains] = flat[pl.ds(start, grain_block, stride=16)]

    @pl.when(group + 2 == batches)
    def _():
        rows_even[...] = rows[0]
        rows_odd[...] = rows[1]
        low = lane_ids(16) % 2 == 0
        odd_y = gy % 2 == 1
        for c in range(3):
            one, other = cols[c], cols[c + 3]
            last = jnp.where(low, one, pltpu.roll(other, 1, 1))
            first = jnp.where(low, pltpu.roll(one, 127, 1), other)
            cols_even[c] = jnp.where(odd_y, first, last)
            cols_odd[c] = jnp.where(odd_y, last, first)


def solve_grains(half_velocity, got, stress, angles, hardness, active):
    n = hardness.shape[0]
    in_hbm = pl.BlockSpec(memory_space=pltpu.HBM)
    return pl.pallas_call(
        functools.partial(solve_kernel, sizes()),
        grid=(n // grain_block,),
        in_specs=[
            whole(2, 16, 128),
            *[whole(*g.shape) for g in got],
            *[in_hbm] * 4,
        ],
        out_specs=[
            pl.BlockSpec((6, grain_block, 16, 128), lambda i: (0, i, 0, 0)),
            whole(3, 16, 128),
            whole(6, n, 128),
            whole(6, n, 128),
            whole(3, 16, 128),
            whole(3, 16, 128),
        ],
        out_shape=[f32(6, n, 16, 128), f32(3, 16, 128), f32(6, n, 128), f32(6, n, 128)]
        + [f32(3, 16, 128)] * 2,
        scratch_shapes=[
            pltpu.VMEM(stress.shape, jnp.float32),
            pltpu.VMEM(angles.shape, jnp.float32),
            pltpu.VMEM(hardness.shape, jnp.float32),
            pltpu.VMEM(active.shape, jnp.int32),
            pltpu.VMEM((8 * n_sums, 192), jnp.float32),
            pltpu.VMEM((8 * n_sums, 192), jnp.bfloat16),
            pltpu.VMEM((8 * n_sums, 256 * batch), jnp.float32),
            pltpu.VMEM((8 * n_sums, 256 * batch), jnp.float32),
            pltpu.VMEM((5, 16, 128), jnp.float32),
            pltpu.VMEM((2, 6, n, 128), jnp.float32),
            pltpu.VMEM((6, 16, 128), jnp.float32),
            pltpu.SemaphoreType.DMA((4, n // batch)),
        ],
        compiler_params=pltpu.CompilerParams(vmem_limit_bytes=53 * 2**20),
        cost_estimate=pl.CostEstimate(flops=10**8, bytes_accessed=10**7, transcendentals=0),
    )(half_velocity, *got, stress, angles, hardness, active)


def zone_update(counts, velocity, fields, u_got, stress, s_got, tall, moved, velocity_out):
    gx, gy = places()
    sx_even, sx_odd, sy_even, sy_odd = s_got
    s_east, s_west = from_sides(sx_even, sx_odd, gx, counts[0])
    s_north, s_south = from_sides(sy_even, sy_odd, gy, counts[1])
    for c in range(3):
        tall[c, 0:2] = s_west[2 * c : 2 * c + 2]
        tall[c, 2:18] = stress[c]
        tall[c, 18:20] = s_east[2 * c : 2 * c + 2]
    near = [side_columns(s_north, s_south, 4 * c + 2, 4 * c + 1) for c in range(3)]
    far = [side_columns(s_north, s_south, 4 * c + 3, 4 * c) for c in range(3)]
    lane = lane_ids(16)
    sign = jnp.where(lane == 127, 0.5, -0.5)

    def x_diff(c):
        return (tall[c, 2:20] - tall[c, 0:18]) * 0.5

    def y_diff(c):
        after, before = shifts_y(tall[c, 1:19], near[c][:18])
        return (after - before) * 0.5

    def rim_x(c):
        return (near[c][2:18] - near[c][0:16]) * 0.5

    def rim_y(c):
        return (far[c][1:17] - stress[c]) * sign

    force = [x_diff(0) + y_diff(2), x_diff(2) + y_diff(1)]
    rim_force = [rim_x(0) + rim_y(2), rim_x(2) + rim_y(1)]
    field_rim = [
        side_columns(s_north[:16], s_south[:16], 13 + 2 * k, 12 + 2 * k) for k in range(3)
    ]
    sides = [velocity_halo(counts, [got[k] for got in u_got]) for k in range(2)]

    def high(k):
        return jnp.concatenate([s_west[6 + k : 7 + k], fields[k], s_east[6 + k : 7 + k]], axis=0)

    mass = time_step * high(0)
    rim = []
    for k in range(2):
        east, west, halo = sides[k]
        moved[k, 0:18] = jnp.concatenate([west, velocity[k], east], axis=0) + mass * force[k]
        rim.append(halo + time_step * field_rim[0] * rim_force[k])
    frac_x = time_step * 0.5 * (moved[0, 0:17] + moved[0, 1:18])
    x_self = frac_x * high(1)[:17]
    x_next = frac_x - x_self
    own = [moved[k, 1:17] for k in range(2)]
    y_sides = [shifts_y(own[k], rim[k]) for k in range(2)]
    frac_y = time_step * 0.5 * (own[1] + y_sides[1][0])
    frac_before = time_step * 0.5 * (own[1] + y_sides[1][1])
    flag = fields[2]
    flag_before = jnp.where(lane == 0, field_rim[2], pltpu.roll(flag, 1, 1))
    y_self, before_self = frac_y * flag, frac_before * flag_before
    y_next, before_next = frac_y - y_self, frac_before - before_self
    centre = 1.0 - x_self[1:17] + x_next[0:16] - y_self + before_next
    coefs = (centre, -x_next[1:17], x_self[0:16], -y_next, before_self)
    for k in range(2):
        velocity_out[k] = (
            centre * own[k]
            + coefs[1] * moved[k, 2:18]
            + coefs[2] * moved[k, 0:16]
            + coefs[3] * y_sides[k][0]
            + coefs[4] * y_sides[k][1]
        )
    return coefs


def remap_kernel(
    counts, velocity, fields, ux_even, ux_odd, uy_even, uy_odd, stress, sx_even, sx_odd, y_even, y_odd,
    relaxed_in, rows_even, rows_odd,
    out, velocity_out, relaxed, tall, moved, coefs, rows, cols, sems,
):
    block = pl.program_id(0)
    size = out.shape[1]
    gx, gy = places()
    odd_x = gx % 2 == 1

    def copy(i):
        part = pl.ds(i * size, size)
        return pltpu.make_async_copy(relaxed_in.at[:, part], relaxed.at[:, part], sems.at[i])

    @pl.when(block == 0)
    def _():
        for i in range(relaxed.shape[1] // size):
            copy(i).start()

    rows[0] = jnp.where(odd_x, rows_odd[...], rows_even[...])
    rows[1] = jnp.where(odd_x, rows_even[...], rows_odd[...])
    lane, row = lane_ids(16), row_ids()

    @pl.when(block == 0)
    def _():
        fresh = zone_update(
            counts,
            velocity,
            fields,
            (ux_even, ux_odd, uy_even, uy_odd),
            stress,
            (sx_even[...], sx_odd[...], y_even[48:72], y_odd[48:72]),
            tall,
            moved,
            velocity_out,
        )
        centre, east, west, north, south = fresh
        coefs[0] = centre
        coefs[1] = jnp.where(row == 15, 0.0, east)
        coefs[2] = jnp.where(row == 0, 0.0, west)
        coefs[3] = jnp.where(lane == 127, 0.0, north)
        coefs[4] = jnp.where(lane == 0, 0.0, south)
        coefs[5] = jnp.where((row == 15) & (gx < counts[0] - 1), east, 0.0)
        coefs[6] = jnp.where((row == 0) & (gx > 0), west, 0.0)
        rim = jnp.where((lane == 127) & (gy < counts[1] - 1), north, 0.0)
        coefs[7] = jnp.where((lane == 0) & (gy > 0), south, rim)
        odd_y = gy % 2 == 1
        for c in range(3):
            part = slice(16 * c, 16 * c + 16)
            got_even, got_odd = y_even[part], y_odd[part]
            after = jnp.where(odd_y, got_odd, got_even)
            before = jnp.where(odd_y, got_even, got_odd)
            cols[c] = jnp.where(lane % 2 == 0, after, pltpu.roll(before, 1, 1))
            cols[c + 3] = jnp.where(lane % 2 == 0, pltpu.roll(after, 127, 1), before)

    centre, east, west, north, south, _, _, rim = [coefs[i] for i in range(8)]
    high_east, low_west = coefs[5, 8:16], coefs[6, 0:8]
    copy(block).wait()

    def one(g):
        for c in range(6):
            q = relaxed[c, block * size + g]
            halo = pltpu.roll(cols[c], 127 - 2 * (block * size + g), 1)
            total = centre * q + north * pltpu.roll(q, 127, 1) + south * pltpu.roll(q, 1, 1)
            total = total + rim * halo
            total = total + east * pltpu.roll(q, 15, 0) + west * pltpu.roll(q, 1, 0)
            out[c, g, 0:8] = total[:8] + low_west * rows[1, c, pl.ds(g, 1), :]
            out[c, g, 8:16] = total[8:] + high_east * rows[0, c, pl.ds(g, 1), :]

    def some(i, carry):
        for k in range(16):
            one(i * 16 + k)
        return carry

    lax.fori_loop(0, size // 16, some, 0)


def remap_grains(velocity, fields, u_got, stress, s_got, y_got, relaxed, rows_even, rows_odd):
    n = relaxed.shape[1]
    size = 16
    small = (velocity, fields, *u_got, stress, *s_got, *y_got)
    return pl.pallas_call(
        functools.partial(remap_kernel, sizes()),
        grid=(n // size,),
        in_specs=[
            *[whole(*a.shape) for a in small],
            pl.BlockSpec(memory_space=pltpu.HBM),
            pl.BlockSpec((6, size, 128), lambda i: (0, i, 0)),
            pl.BlockSpec((6, size, 128), lambda i: (0, i, 0)),
        ],
        out_specs=[
            pl.BlockSpec((6, size, 16, 128), lambda i: (0, i, 0, 0)),
            whole(2, 16, 128),
        ],
        out_shape=[f32(*relaxed.shape), f32(2, 16, 128)],
        scratch_shapes=[
            pltpu.VMEM(relaxed.shape, jnp.float32),
            pltpu.VMEM((3, 24, 128), jnp.float32),
            pltpu.VMEM((2, 24, 128), jnp.float32),
            pltpu.VMEM((8, 16, 128), jnp.float32),
            pltpu.VMEM((2, 6, size, 128), jnp.float32),
            pltpu.VMEM((6, 16, 128), jnp.float32),
            pltpu.SemaphoreType.DMA((n // size,)),
        ],
        compiler_params=pltpu.CompilerParams(vmem_limit_bytes=53 * 2**20),
        cost_estimate=pl.CostEstimate(flops=10**7, bytes_accessed=10**7, transcendentals=0),
    )(*small, relaxed, rows_even, rows_odd)


def swap_even(block, axis):
    return lax.ppermute(block, axis, [(i, i ^ 1) for i in range(lax.axis_size(axis))])


def swap_odd(block, axis):
    count = lax.axis_size(axis)
    pairs = []
    for i in range(1, count, 2):
        pairs += [(i, (i + 1) % count), ((i + 1) % count, i)]
    return lax.ppermute(block, axis, pairs)


def swap_odd_crossed(block):
    count = lax.axis_size("gx")
    pairs = []
    for i in range(1, count, 2):
        for a in range(2):
            left, right = i * 2 + a, ((i + 1) % count) * 2 + 1 - a
            pairs += [(left, right), (right, left)]
    return lax.ppermute(block, ("gx", "ga"), pairs)


def per_device(velocity, density, grain_stress, grain_angles, hardness, active, donor_faces):
    gx = lax.axis_index("gx")
    odd_x = gx % 2 == 1
    u_got = (
        swap_even(velocity, "gx"),
        swap_odd_crossed(velocity),
        swap_even(velocity, "gy"),
        swap_odd(velocity, "gy"),
    )
    relaxed, part, rows_even, rows_odd, cols_even, cols_odd = solve_grains(
        0.5 * velocity, u_got, grain_stress, grain_angles, hardness, active
    )
    density, donor_faces, part = lax.optimization_barrier((density, donor_faces, part))
    fields = jnp.concatenate([(1.0 / density)[None], donor_faces.astype(jnp.float32)], axis=0)
    far_rows_odd = swap_odd(rows_odd, "gx")
    far_rows_even = swap_even(rows_even, "gx")
    zone_stress = (part + swap_even(part, "ga")) * (1.0 / G)
    spare = jnp.zeros((7, 128), jnp.float32)
    first = jnp.concatenate([zone_stress[:, :2].reshape(6, 128), fields[:, 0], spare], axis=0)
    last = jnp.concatenate([zone_stress[:, -2:].reshape(6, 128), fields[:, -1], spare], axis=0)
    got_even = swap_even(jnp.where(odd_x, first, last), "gx")
    got_odd = swap_odd_crossed(jnp.where(odd_x, last, first))
    east, west = from_sides(got_even[:6], got_odd[:6], gx, lax.axis_size("gx"))
    east, west = east.reshape(3, 2, 128), west.reshape(3, 2, 128)
    tall = jnp.concatenate([west[:, 1:], zone_stress, east[:, :1]], axis=1)
    lane = lax.broadcasted_iota(jnp.int32, (18, 128), 1)
    sides = jnp.zeros((18, 128), jnp.float32)
    for c in range(3):
        sides = jnp.where(lane // 4 == c, jnp.roll(tall[c], 4 * c + 2, axis=1), sides)
    sides = jnp.pad(sides, ((0, 6), (0, 0)))
    lane = lax.broadcasted_iota(jnp.int32, (16, 128), 1)
    field_sides = jnp.zeros((16, 128), jnp.float32)
    for k in range(3):
        field_sides = jnp.where(lane // 2 == 6 + k, jnp.roll(fields[k], 13 + 2 * k, axis=1), field_sides)
    sides = sides + jnp.pad(field_sides, ((0, 8), (0, 0)))
    y_got = (
        swap_even(jnp.concatenate([cols_even.reshape(48, 128), sides], axis=0), "gy"),
        swap_odd(jnp.concatenate([cols_odd.reshape(48, 128), sides], axis=0), "gy"),
    )
    stress_out, velocity_out = remap_grains(
        velocity, fields, u_got, zone_stress, (got_even, got_odd), y_got, relaxed, far_rows_even, far_rows_odd
    )
    return (velocity_out, stress_out, zone_stress)


def solution(mesh):
    return jax.shard_map(
        per_device,
        mesh=mesh,
        in_specs=(
            P(None, "gx", "gy"),
            P("gx", "gy"),
            P(None, "ga", "gx", "gy"),
            P(None, "ga", "gx", "gy"),
            P("ga", "gx", "gy"),
            P(None, "ga", "gx", "gy"),
            P(None, "gx", "gy"),
        ),
        out_specs=(P(None, "gx", "gy"), P(None, "ga", "gx", "gy"), P(None, "gx", "gy")),
        check_vma=False,
    )
```

```python
import functools
import math

import jax
import jax.numpy as jnp
import numpy as np
from jax import lax
from jax.experimental import pallas as pl
from jax.experimental.pallas import tpu as pltpu
from jax.sharding import PartitionSpec as P

G = 128
ITERS = 4

time_step = 0.1
lame_first = 1.5
batch = 4
grain_block = 2 * batch
system_list = (
    ((0, 1, 1), (1, 1, -1)),
    ((0, 1, 1), (1, -1, 1)),
    ((1, 0, 1), (1, 1, -1)),
    ((1, 0, 1), (-1, 1, 1)),
    ((1, 1, 0), (1, -1, 1)),
    ((1, 1, 0), (-1, 1, 1)),
    ((0, 1, -1), (1, 1, 1)),
    ((0, 1, -1), (1, -1, -1)),
    ((1, 0, -1), (1, 1, 1)),
    ((1, 0, -1), (1, -1, 1)),
    ((1, -1, 0), (1, 1, 1)),
    ((1, -1, 0), (1, 1, -1)),
    ((1, 1, 2), (1, 1, -1)),
    ((1, 1, -2), (1, 1, 1)),
    ((1, -1, 2), (1, -1, -1)),
    ((-1, 1, 2), (-1, 1, -1)),
    ((1, 2, 1), (1, -1, 1)),
    ((1, -2, 1), (1, 1, 1)),
    ((-1, 2, 1), (1, 1, -1)),
    ((1, 2, -1), (-1, 1, 1)),
    ((2, 1, 1), (-1, 1, 1)),
    ((-2, 1, 1), (1, 1, 1)),
    ((2, -1, 1), (1, 1, -1)),
    ((2, 1, -1), (1, -1, 1)),
)
upper_pairs = [(i, j) for i in range(5) for j in range(i, 5)]
n_sums = 26


def slip_sums_table():
    table = np.zeros((n_sums, 24))
    for s, (normal, direction) in enumerate(system_list):
        q = np.outer(direction, normal) + np.outer(normal, direction)
        k = np.array([(q[0, 0] - q[1, 1]) / 2, -q[2, 2] / 2, q[1, 2], q[0, 2], q[0, 1]])
        weight = 3 if s < 12 else 1
        for e, (i, j) in enumerate(upper_pairs):
            table[e, s] = weight * k[i] * k[j] * (3 if i == j == 1 else 1)
        first = 15 if s < 12 else 20
        table[first : first + 5, s] = k
        table[25, s] = 1
    columns = np.zeros((n_sums, 24))
    for s in range(24):
        word, bit = divmod(s, 12)
        columns[:, 2 * bit + word] = table[:, s]
    return columns


def fill_table(table):
    columns = slip_sums_table()
    lane = lax.broadcasted_iota(jnp.int32, (8, 192), 1)
    own = lane % 8 == lax.broadcasted_iota(jnp.int32, (8, 192), 0)
    system = lane // 8
    for e in range(n_sums):
        entry = jnp.zeros((8, 192), jnp.float32)
        for k in range(24):
            if columns[e, k]:
                entry = jnp.where(system == k, float(columns[e, k]), entry)
        table[8 * e : 8 * e + 8] = jnp.where(own, entry, 0.0)


def fitted(function, degree, top):
    series = np.polynomial.chebyshev.Chebyshev.interpolate(function, degree, domain=[0.0, top])
    return [float(c) for c in series.convert(kind=np.polynomial.Polynomial).coef]


angle_top = 3.1416**2
sin_half = fitted(lambda t: math.sqrt(2) * np.sin(np.sqrt(t) / 2) / np.sqrt(t), 4, angle_top)
cos_half = fitted(lambda t: math.sqrt(2) * np.cos(np.sqrt(t) / 2), 4, angle_top)


def polynomial(t, coefs):
    total = coefs[-1] * t + coefs[-2]
    for c in coefs[-3::-1]:
        total = total * t + c
    return total


def sin_cos(x):
    t = x * x
    s = x * polynomial(t, sin_half)
    c = polynomial(t, cos_half)
    return s * c, 1.0 - s * s


def grain_math(stress, angles, hardness, sums, strain):
    exx, eyy, exy, trace, hydro = strain
    s1, c1 = sin_cos(angles[0])
    sq, cq = sin_cos(angles[1])
    s2, c2 = sin_cos(angles[2])
    c1c2, s1s2, c1s2, s1c2 = c1 * c2, s1 * s2, c1 * s2, s1 * c2
    r00 = c1c2 - s1s2 * cq
    r01 = -(c1s2 + s1c2 * cq)
    r02 = s1 * sq
    r10 = s1c2 + c1s2 * cq
    r11 = c1c2 * cq - s1s2
    r12 = -(c1 * sq)
    a0, b0 = r00 * exx + r10 * exy, r10 * eyy + r00 * exy
    a1, b1 = r01 * exx + r11 * exy, r11 * eyy + r01 * exy
    d00 = r00 * a0 + r10 * b0
    d11 = r01 * a1 + r11 * b1
    t00, t11 = stress[0] + d00, stress[1] + d11
    t22 = stress[2] + (trace - (d00 + d11))
    t_sum = t00 + t11
    v = [
        (t00 - t11) * 0.5,
        t_sum * (1 / math.sqrt(12)) - t22 * (2 / math.sqrt(12)),
        stress[3] + (r02 * a1 + r12 * b1),
        stress[4] + (r02 * a0 + r12 * b0),
        stress[5] + (r01 * a0 + r11 * b0),
    ]
    pressure = (t_sum + t22) * (1.0 / 3.0) + hydro
    step = 1.0 / (1.0 + sums(25))
    h0 = hardness * step * (1 / math.sqrt(2))
    h1 = h0 * (1 / math.sqrt(3))
    h2 = h0 * (1.0 / 3.0)
    bias = []
    for i in range(5):
        first, second = (h0, h1) if i == 1 else (h1, h2)
        bias.append(sums(15 + i) * first + sums(20 + i) * second)
    plain, mixed = step * (1 / 18.0), step * (math.sqrt(3) / 18.0)
    m = {}
    for e, (i, j) in enumerate(upper_pairs):
        entry = sums(e) * (mixed if (i == 1) != (j == 1) else plain)
        m[i, j] = m[j, i] = (1.0 - entry) if i == j else entry
    for _ in range(ITERS):
        fresh = []
        for i in range(5):
            off = None
            for j in range(5):
                if j != i:
                    term = m[i, j] * v[j]
                    off = term if off is None else off + term
            fresh.append((m[i, i] * v[i] + bias[i]) - off)
        v = fresh
    w = v[1] * (1 / math.sqrt(3))
    mid = pressure + w
    x = [mid + v[0], mid - v[0], pressure - 2.0 * w, v[2], v[3], v[4]]
    f0 = x[0] * r00 + x[5] * r01 + x[4] * r02
    f1 = x[5] * r00 + x[1] * r01 + x[3] * r02
    f2 = x[4] * r00 + x[3] * r01 + x[2] * r02
    g0 = x[0] * r10 + x[5] * r11 + x[4] * r12
    g1 = x[5] * r10 + x[1] * r11 + x[3] * r12
    g2 = x[4] * r10 + x[3] * r11 + x[2] * r12
    sample = (
        r00 * f0 + r01 * f1 + r02 * f2,
        r10 * g0 + r11 * g1 + r12 * g2,
        r00 * g0 + r01 * g1 + r02 * g2,
    )
    return x, sample


def bit_rows(words):
    pieces = [jnp.concatenate([w[:8], w[8:]], axis=1) for w in words]
    both = jnp.concatenate(pieces, axis=0).astype(jnp.int16)
    one, none = jnp.bfloat16(1.0), jnp.bfloat16(0.0)
    rows = [jnp.where((both & jnp.int16(1 << bit)) != 0, one, none) for bit in range(12)]
    return jnp.concatenate(rows, axis=0)


def places():
    return lax.axis_index("gx"), lax.axis_index("gy")


def sizes():
    return lax.axis_size("gx"), lax.axis_size("gy")


def whole(*shape):
    return pl.BlockSpec(shape, lambda *i: (0,) * len(shape))


def f32(*shape):
    return jax.ShapeDtypeStruct(shape, jnp.float32)


def lane_ids(rows):
    return lax.broadcasted_iota(jnp.int32, (rows, 128), 1)


def row_ids():
    return lax.broadcasted_iota(jnp.int32, (16, 128), 0)


def from_sides(got_even, got_odd, index, count):
    odd = index % 2 == 1
    after = jnp.where(odd, got_odd, got_even)
    before = jnp.where(odd, got_even, got_odd)
    return jnp.where(index == count - 1, 0.0, after), jnp.where(index == 0, 0.0, before)


def shifts_x(field, east, west):
    row = row_ids()
    return (
        jnp.where(row == 15, east, pltpu.roll(field, 15, 0)),
        jnp.where(row == 0, west, pltpu.roll(field, 1, 0)),
    )


def shifts_y(field, halo):
    lane = lane_ids(field.shape[0])
    return (
        jnp.where(lane == 127, halo, pltpu.roll(field, 127, 1)),
        jnp.where(lane == 0, halo, pltpu.roll(field, 1, 1)),
    )


def side_columns(after, before, first, last):
    lane = lane_ids(after.shape[0])
    return jnp.where(
        lane == 127,
        pltpu.roll(after, 127 - first, 1),
        jnp.where(lane == 0, pltpu.roll(before, (128 - last) % 128, 1), 0.0),
    )


def velocity_halo(counts, got):
    gx, gy = places()
    after_x, before_x = from_sides(got[0], got[1], gx, counts[0])
    after_y, before_y = from_sides(got[2], got[3], gy, counts[1])
    return after_x[0:1], before_x[15:16], side_columns(after_y, before_y, 0, 127)


def solve_kernel(
    counts, half_velocity, x_even, x_odd, y_even, y_odd, stress_in, angles_in, hardness_in, active_in,
    relaxed, zone_sum, rows_even, rows_odd, cols_even, cols_odd,
    stress, angles, hardness, active, table_wide, table, sums_a, sums_b, strain, rows, cols, sems,
):
    block = pl.program_id(0)
    blocks = hardness.shape[0] // grain_block
    gx, gy = places()

    def copies(i, kinds):
        part = pl.ds(i * grain_block, grain_block)
        every = (
            lambda: (active_in.at[:, part], active.at[:, part]),
            lambda: (stress_in.at[:, part], stress.at[:, part]),
            lambda: (angles_in.at[:, part], angles.at[:, part]),
            lambda: (hardness_in.at[part], hardness.at[part]),
        )
        return [pltpu.make_async_copy(*every[k](), sems.at[k, i]) for k in kinds]

    def count(group, sums):
        first = group * batch
        bits = [bit_rows([active[0, first + k], active[1, first + k]]) for k in range(batch)]
        sums[...] = jnp.dot(
            table[...], jnp.concatenate(bits, axis=1), preferred_element_type=jnp.float32
        )

    def update(group, sums):
        lane = lane_ids(8)
        for half in range(2):
            part = pl.ds(8 * half, 8)
            zone_strain = [strain[i, part] for i in range(5)]
            totals = [zone_sum[k, part] for k in range(3)]
            ends = [cols[c, part] for c in range(6)]
            for k in range(batch):
                g = group * batch + k
                lanes = slice(256 * k + 128 * half, 256 * k + 128 * half + 128)
                x, sample = grain_math(
                    [stress[c, g, part] for c in range(6)],
                    [angles[c, g, part] for c in range(3)],
                    hardness[g, part],
                    lambda e: sums[e * 8 : (e + 1) * 8, lanes],
                    zone_strain,
                )
                here = (lane == 2 * g) | (lane == 2 * g + 1)
                for c in range(6):
                    relaxed[c, g - block * grain_block, part] = x[c]
                    ends[c] = jnp.where(here, pltpu.roll(x[c], 2 * g + 1, 1), ends[c])
                totals = [t + s for t, s in zip(totals, sample)]
            for k in range(3):
                zone_sum[k, part] = totals[k]
            for c in range(6):
                cols[c, part] = ends[c]

    @pl.when(block == 0)
    def _():
        for i in range(blocks):
            for copy in copies(i, range(4)):
                copy.start()
        fill_table(table_wide)
        table[...] = table_wide[...].astype(jnp.bfloat16)
        zone_sum[...] = jnp.zeros_like(zone_sum)
        cols[...] = jnp.zeros_like(cols)
        grads = []
        for k in range(2):
            u = half_velocity[k]
            east, west, halo = velocity_halo(counts, (x_even[k], x_odd[k], y_even[k], y_odd[k]))
            u_east, u_west = shifts_x(u, 0.5 * east, 0.5 * west)
            u_north, u_south = shifts_y(u, 0.5 * halo)
            grads.append((u_east - u_west, u_north - u_south))
        exx, eyy = grads[0][0], grads[1][1]
        exy = 0.5 * (grads[0][1] + grads[1][0])
        strain[0] = 2.0 * time_step * exx
        strain[1] = 2.0 * time_step * eyy
        strain[2] = 2.0 * time_step * exy
        strain[3] = 2.0 * time_step * (exx + eyy)
        strain[4] = lame_first * time_step * (exx + eyy)
        copies(0, [0])[0].wait()
        count(0, sums_a)

    for copy in copies(block, [1, 2, 3]):
        copy.wait()

    @pl.when(block < blocks - 1)
    def _():
        copies(block + 1, [0])[0].wait()

    group = block * 2
    count(group + 1, sums_b)
    update(group, sums_a)
    count(jnp.minimum(group + 2, blocks * 2 - 1), sums_a)
    update(group + 1, sums_b)

    flat = relaxed.reshape(6 * grain_block * 16, 128)
    grains = pl.ds(pl.multiple_of(block * grain_block, grain_block), grain_block)
    for c in range(6):
        start = c * grain_block * 16
        rows[gx % 2, c, grains] = flat[pl.ds(start + 15, grain_block, stride=16)]
        rows[1 - gx % 2, c, grains] = flat[pl.ds(start, grain_block, stride=16)]

    @pl.when(block == blocks - 1)
    def _():
        rows_even[...] = rows[0]
        rows_odd[...] = rows[1]
        low = lane_ids(16) % 2 == 0
        odd_y = gy % 2 == 1
        for c in range(3):
            one, other = cols[c], cols[c + 3]
            last = jnp.where(low, one, pltpu.roll(other, 1, 1))
            first = jnp.where(low, pltpu.roll(one, 127, 1), other)
            cols_even[c] = jnp.where(odd_y, first, last)
            cols_odd[c] = jnp.where(odd_y, last, first)


def solve_grains(half_velocity, got, stress, angles, hardness, active):
    n = hardness.shape[0]
    in_hbm = pl.BlockSpec(memory_space=pltpu.HBM)
    return pl.pallas_call(
        functools.partial(solve_kernel, sizes()),
        grid=(n // grain_block,),
        in_specs=[
            whole(2, 16, 128),
            *[whole(*g.shape) for g in got],
            *[in_hbm] * 4,
        ],
        out_specs=[
            pl.BlockSpec((6, grain_block, 16, 128), lambda i: (0, i, 0, 0)),
            whole(3, 16, 128),
            whole(6, n, 128),
            whole(6, n, 128),
            whole(3, 16, 128),
            whole(3, 16, 128),
        ],
        out_shape=[f32(6, n, 16, 128), f32(3, 16, 128), f32(6, n, 128), f32(6, n, 128)]
        + [f32(3, 16, 128)] * 2,
        scratch_shapes=[
            pltpu.VMEM(stress.shape, jnp.float32),
            pltpu.VMEM(angles.shape, jnp.float32),
            pltpu.VMEM(hardness.shape, jnp.float32),
            pltpu.VMEM(active.shape, jnp.int32),
            pltpu.VMEM((8 * n_sums, 192), jnp.float32),
            pltpu.VMEM((8 * n_sums, 192), jnp.bfloat16),
            pltpu.VMEM((8 * n_sums, 256 * batch), jnp.float32),
            pltpu.VMEM((8 * n_sums, 256 * batch), jnp.float32),
            pltpu.VMEM((5, 16, 128), jnp.float32),
            pltpu.VMEM((2, 6, n, 128), jnp.float32),
            pltpu.VMEM((6, 16, 128), jnp.float32),
            pltpu.SemaphoreType.DMA((4, n // grain_block)),
        ],
        compiler_params=pltpu.CompilerParams(vmem_limit_bytes=53 * 2**20),
        cost_estimate=pl.CostEstimate(flops=10**8, bytes_accessed=10**7, transcendentals=0),
    )(half_velocity, *got, stress, angles, hardness, active)


def zone_update(counts, velocity, fields, u_got, stress, s_got, tall, moved, velocity_out):
    gx, gy = places()
    sx_even, sx_odd, sy_even, sy_odd = s_got
    s_east, s_west = from_sides(sx_even, sx_odd, gx, counts[0])
    s_north, s_south = from_sides(sy_even, sy_odd, gy, counts[1])
    for c in range(3):
        tall[c, 0:2] = s_west[2 * c : 2 * c + 2]
        tall[c, 2:18] = stress[c]
        tall[c, 18:20] = s_east[2 * c : 2 * c + 2]
    near = [side_columns(s_north, s_south, 4 * c + 2, 4 * c + 1) for c in range(3)]
    far = [side_columns(s_north, s_south, 4 * c + 3, 4 * c) for c in range(3)]
    lane = lane_ids(16)
    sign = jnp.where(lane == 127, 0.5, -0.5)

    def x_diff(c):
        return (tall[c, 2:20] - tall[c, 0:18]) * 0.5

    def y_diff(c):
        after, before = shifts_y(tall[c, 1:19], near[c][:18])
        return (after - before) * 0.5

    def rim_x(c):
        return (near[c][2:18] - near[c][0:16]) * 0.5

    def rim_y(c):
        return (far[c][1:17] - stress[c]) * sign

    force = [x_diff(0) + y_diff(2), x_diff(2) + y_diff(1)]
    rim_force = [rim_x(0) + rim_y(2), rim_x(2) + rim_y(1)]
    field_rim = [
        side_columns(s_north[:16], s_south[:16], 13 + 2 * k, 12 + 2 * k) for k in range(3)
    ]
    sides = [velocity_halo(counts, [got[k] for got in u_got]) for k in range(2)]

    def high(k):
        return jnp.concatenate([s_west[6 + k : 7 + k], fields[k], s_east[6 + k : 7 + k]], axis=0)

    mass = time_step * high(0)
    rim = []
    for k in range(2):
        east, west, halo = sides[k]
        moved[k, 0:18] = jnp.concatenate([west, velocity[k], east], axis=0) + mass * force[k]
        rim.append(halo + time_step * field_rim[0] * rim_force[k])
    frac_x = time_step * 0.5 * (moved[0, 0:17] + moved[0, 1:18])
    x_self = frac_x * high(1)[:17]
    x_next = frac_x - x_self
    own = [moved[k, 1:17] for k in range(2)]
    y_sides = [shifts_y(own[k], rim[k]) for k in range(2)]
    frac_y = time_step * 0.5 * (own[1] + y_sides[1][0])
    frac_before = time_step * 0.5 * (own[1] + y_sides[1][1])
    flag = fields[2]
    flag_before = jnp.where(lane == 0, field_rim[2], pltpu.roll(flag, 1, 1))
    y_self, before_self = frac_y * flag, frac_before * flag_before
    y_next, before_next = frac_y - y_self, frac_before - before_self
    centre = 1.0 - x_self[1:17] + x_next[0:16] - y_self + before_next
    coefs = (centre, -x_next[1:17], x_self[0:16], -y_next, before_self)
    for k in range(2):
        velocity_out[k] = (
            centre * own[k]
            + coefs[1] * moved[k, 2:18]
            + coefs[2] * moved[k, 0:16]
            + coefs[3] * y_sides[k][0]
            + coefs[4] * y_sides[k][1]
        )
    return coefs


def remap_kernel(
    counts, velocity, fields, ux_even, ux_odd, uy_even, uy_odd, stress, sx_even, sx_odd, y_even, y_odd,
    relaxed_in, rows_even, rows_odd,
    out, velocity_out, relaxed, tall, moved, coefs, rows, cols, sems,
):
    block = pl.program_id(0)
    size = out.shape[1]
    gx, gy = places()
    odd_x = gx % 2 == 1

    def copy(i):
        part = pl.ds(i * size, size)
        return pltpu.make_async_copy(relaxed_in.at[:, part], relaxed.at[:, part], sems.at[i])

    @pl.when(block == 0)
    def _():
        for i in range(relaxed.shape[1] // size):
            copy(i).start()

    rows[0] = jnp.where(odd_x, rows_odd[...], rows_even[...])
    rows[1] = jnp.where(odd_x, rows_even[...], rows_odd[...])
    lane, row = lane_ids(16), row_ids()

    @pl.when(block == 0)
    def _():
        fresh = zone_update(
            counts,
            velocity,
            fields,
            (ux_even, ux_odd, uy_even, uy_odd),
            stress,
            (sx_even[...], sx_odd[...], y_even[48:72], y_odd[48:72]),
            tall,
            moved,
            velocity_out,
        )
        centre, east, west, north, south = fresh
        coefs[0] = centre
        coefs[1] = jnp.where(row == 15, 0.0, east)
        coefs[2] = jnp.where(row == 0, 0.0, west)
        coefs[3] = jnp.where(lane == 127, 0.0, north)
        coefs[4] = jnp.where(lane == 0, 0.0, south)
        coefs[5] = jnp.where((row == 15) & (gx < counts[0] - 1), east, 0.0)
        coefs[6] = jnp.where((row == 0) & (gx > 0), west, 0.0)
        rim = jnp.where((lane == 127) & (gy < counts[1] - 1), north, 0.0)
        coefs[7] = jnp.where((lane == 0) & (gy > 0), south, rim)
        odd_y = gy % 2 == 1
        for c in range(3):
            part = slice(16 * c, 16 * c + 16)
            got_even, got_odd = y_even[part], y_odd[part]
            after = jnp.where(odd_y, got_odd, got_even)
            before = jnp.where(odd_y, got_even, got_odd)
            cols[c] = jnp.where(lane % 2 == 0, after, pltpu.roll(before, 1, 1))
            cols[c + 3] = jnp.where(lane % 2 == 0, pltpu.roll(after, 127, 1), before)

    centre, east, west, north, south, _, _, rim = [coefs[i] for i in range(8)]
    high_east, low_west = coefs[5, 8:16], coefs[6, 0:8]
    copy(block).wait()

    def one(g):
        for c in range(6):
            q = relaxed[c, block * size + g]
            halo = pltpu.roll(cols[c], 127 - 2 * (block * size + g), 1)
            total = centre * q + north * pltpu.roll(q, 127, 1) + south * pltpu.roll(q, 1, 1)
            total = total + rim * halo
            total = total + east * pltpu.roll(q, 15, 0) + west * pltpu.roll(q, 1, 0)
            out[c, g, 0:8] = total[:8] + low_west * rows[1, c, pl.ds(g, 1), :]
            out[c, g, 8:16] = total[8:] + high_east * rows[0, c, pl.ds(g, 1), :]

    def some(i, carry):
        for k in range(16):
            one(i * 16 + k)
        return carry

    lax.fori_loop(0, size // 16, some, 0)


def remap_grains(velocity, fields, u_got, stress, s_got, y_got, relaxed, rows_even, rows_odd):
    n = relaxed.shape[1]
    size = 16
    small = (velocity, fields, *u_got, stress, *s_got, *y_got)
    return pl.pallas_call(
        functools.partial(remap_kernel, sizes()),
        grid=(n // size,),
        in_specs=[
            *[whole(*a.shape) for a in small],
            pl.BlockSpec(memory_space=pltpu.HBM),
            pl.BlockSpec((6, size, 128), lambda i: (0, i, 0)),
            pl.BlockSpec((6, size, 128), lambda i: (0, i, 0)),
        ],
        out_specs=[
            pl.BlockSpec((6, size, 16, 128), lambda i: (0, i, 0, 0)),
            whole(2, 16, 128),
        ],
        out_shape=[f32(*relaxed.shape), f32(2, 16, 128)],
        scratch_shapes=[
            pltpu.VMEM(relaxed.shape, jnp.float32),
            pltpu.VMEM((3, 24, 128), jnp.float32),
            pltpu.VMEM((2, 24, 128), jnp.float32),
            pltpu.VMEM((8, 16, 128), jnp.float32),
            pltpu.VMEM((2, 6, size, 128), jnp.float32),
            pltpu.VMEM((6, 16, 128), jnp.float32),
            pltpu.SemaphoreType.DMA((n // size,)),
        ],
        compiler_params=pltpu.CompilerParams(vmem_limit_bytes=53 * 2**20),
        cost_estimate=pl.CostEstimate(flops=10**7, bytes_accessed=10**7, transcendentals=0),
    )(*small, relaxed, rows_even, rows_odd)


def swap_even(block, axis):
    return lax.ppermute(block, axis, [(i, i ^ 1) for i in range(lax.axis_size(axis))])


def swap_odd_y(block):
    count_x, count_y = sizes()
    pairs = []
    for x in range(count_x):
        for y in range(count_y):
            end = y in (0, count_y - 1)
            to_x, to_y = (x ^ 1, y) if end else (x, y + 1 if y % 2 else y - 1)
            pairs.append((x * count_y + y, to_x * count_y + to_y))
    return lax.ppermute(block, ("gx", "gy"), pairs)


def swap_odd_x(block, crossed):
    count = lax.axis_size("gx")
    pairs = []
    for x in range(count):
        for a in range(2):
            end = x in (0, count - 1)
            to_x = x if end else (x + 1 if x % 2 else x - 1)
            to_a = 1 - a if end or crossed else a
            pairs.append((x * 2 + a, to_x * 2 + to_a))
    return lax.ppermute(block, ("gx", "ga"), pairs)


def per_device(velocity, density, grain_stress, grain_angles, hardness, active, donor_faces):
    gx = lax.axis_index("gx")
    odd_x = gx % 2 == 1
    u_got = (
        swap_even(velocity, "gx"),
        swap_odd_x(velocity, True),
        swap_even(velocity, "gy"),
        swap_odd_y(velocity),
    )
    relaxed, part, rows_even, rows_odd, cols_even, cols_odd = solve_grains(
        0.5 * velocity, u_got, grain_stress, grain_angles, hardness, active
    )
    density, donor_faces, part = lax.optimization_barrier((density, donor_faces, part))
    fields = jnp.concatenate([(1.0 / density)[None], donor_faces.astype(jnp.float32)], axis=0)
    zone_stress = (part + swap_even(part, "ga")) * (1.0 / G)
    zone_stress, rows_even, rows_odd = lax.optimization_barrier((zone_stress, rows_even, rows_odd))
    far_rows_odd = swap_odd_x(rows_odd, False)
    far_rows_even = swap_even(rows_even, "gx")
    spare = jnp.zeros((7, 128), jnp.float32)
    first = jnp.concatenate([zone_stress[:, :2].reshape(6, 128), fields[:, 0], spare], axis=0)
    last = jnp.concatenate([zone_stress[:, -2:].reshape(6, 128), fields[:, -1], spare], axis=0)
    got_even = swap_even(jnp.where(odd_x, first, last), "gx")
    got_odd = swap_odd_x(jnp.where(odd_x, last, first), True)
    east, west = from_sides(got_even[:6], got_odd[:6], gx, lax.axis_size("gx"))
    east, west = east.reshape(3, 2, 128), west.reshape(3, 2, 128)
    tall = jnp.concatenate([west[:, 1:], zone_stress, east[:, :1]], axis=1)
    lane = lax.broadcasted_iota(jnp.int32, (18, 128), 1)
    sides = jnp.zeros((18, 128), jnp.float32)
    for c in range(3):
        sides = jnp.where(lane // 4 == c, jnp.roll(tall[c], 4 * c + 2, axis=1), sides)
    sides = jnp.pad(sides, ((0, 6), (0, 0)))
    lane = lax.broadcasted_iota(jnp.int32, (16, 128), 1)
    field_sides = jnp.zeros((16, 128), jnp.float32)
    for k in range(3):
        field_sides = jnp.where(lane // 2 == 6 + k, jnp.roll(fields[k], 13 + 2 * k, axis=1), field_sides)
    sides = sides + jnp.pad(field_sides, ((0, 8), (0, 0)))
    y_got = (
        swap_even(jnp.concatenate([cols_even.reshape(48, 128), sides], axis=0), "gy"),
        swap_odd_y(jnp.concatenate([cols_odd.reshape(48, 128), sides], axis=0)),
    )
    stress_out, velocity_out = remap_grains(
        velocity, fields, u_got, zone_stress, (got_even, got_odd), y_got, relaxed, far_rows_even, far_rows_odd
    )
    return (velocity_out, stress_out, zone_stress)


def solution(mesh):
    return jax.shard_map(
        per_device,
        mesh=mesh,
        in_specs=(
            P(None, "gx", "gy"),
            P("gx", "gy"),
            P(None, "ga", "gx", "gy"),
            P(None, "ga", "gx", "gy"),
            P("ga", "gx", "gy"),
            P(None, "ga", "gx", "gy"),
            P(None, "gx", "gy"),
        ),
        out_specs=(P(None, "gx", "gy"), P(None, "ga", "gx", "gy"), P(None, "gx", "gy")),
        check_vma=False,
    )
```

```python
import functools
import math

import jax
import jax.numpy as jnp
import numpy as np
from jax import lax
from jax.experimental import pallas as pl
from jax.experimental.pallas import tpu as pltpu
from jax.sharding import PartitionSpec as P

G = 128
ITERS = 4

time_step = 0.1
lame_first = 1.5
batch = 4
grain_block = 2 * batch
system_list = (
    ((0, 1, 1), (1, 1, -1)),
    ((0, 1, 1), (1, -1, 1)),
    ((1, 0, 1), (1, 1, -1)),
    ((1, 0, 1), (-1, 1, 1)),
    ((1, 1, 0), (1, -1, 1)),
    ((1, 1, 0), (-1, 1, 1)),
    ((0, 1, -1), (1, 1, 1)),
    ((0, 1, -1), (1, -1, -1)),
    ((1, 0, -1), (1, 1, 1)),
    ((1, 0, -1), (1, -1, 1)),
    ((1, -1, 0), (1, 1, 1)),
    ((1, -1, 0), (1, 1, -1)),
    ((1, 1, 2), (1, 1, -1)),
    ((1, 1, -2), (1, 1, 1)),
    ((1, -1, 2), (1, -1, -1)),
    ((-1, 1, 2), (-1, 1, -1)),
    ((1, 2, 1), (1, -1, 1)),
    ((1, -2, 1), (1, 1, 1)),
    ((-1, 2, 1), (1, 1, -1)),
    ((1, 2, -1), (-1, 1, 1)),
    ((2, 1, 1), (-1, 1, 1)),
    ((-2, 1, 1), (1, 1, 1)),
    ((2, -1, 1), (1, 1, -1)),
    ((2, 1, -1), (1, -1, 1)),
)
upper_pairs = [(i, j) for i in range(5) for j in range(i, 5)]
n_sums = 26


def slip_sums_table():
    table = np.zeros((n_sums, 24))
    for s, (normal, direction) in enumerate(system_list):
        q = np.outer(direction, normal) + np.outer(normal, direction)
        k = np.array([(q[0, 0] - q[1, 1]) / 2, -q[2, 2] / 2, q[1, 2], q[0, 2], q[0, 1]])
        weight = 3 if s < 12 else 1
        for e, (i, j) in enumerate(upper_pairs):
            table[e, s] = weight * k[i] * k[j] * (3 if i == j == 1 else 1)
        first = 15 if s < 12 else 20
        table[first : first + 5, s] = k
        table[25, s] = 1
    columns = np.zeros((n_sums, 24))
    for s in range(24):
        word, bit = divmod(s, 12)
        columns[:, 2 * bit + word] = table[:, s]
    return columns


def fill_table(table):
    columns = slip_sums_table()
    lane = lax.broadcasted_iota(jnp.int32, (8, 192), 1)
    own = lane % 8 == lax.broadcasted_iota(jnp.int32, (8, 192), 0)
    system = lane // 8
    for e in range(n_sums):
        entry = jnp.zeros((8, 192), jnp.float32)
        for k in range(24):
            if columns[e, k]:
                entry = jnp.where(system == k, float(columns[e, k]), entry)
        table[8 * e : 8 * e + 8] = jnp.where(own, entry, 0.0)


def fitted(function, degree, top):
    series = np.polynomial.chebyshev.Chebyshev.interpolate(function, degree, domain=[0.0, top])
    return [float(c) for c in series.convert(kind=np.polynomial.Polynomial).coef]


angle_top = 3.1416**2
sin_half = fitted(lambda t: math.sqrt(2) * np.sin(np.sqrt(t) / 2) / np.sqrt(t), 4, angle_top)
cos_half = fitted(lambda t: math.sqrt(2) * np.cos(np.sqrt(t) / 2), 4, angle_top)


def polynomial(t, coefs):
    total = coefs[-1] * t + coefs[-2]
    for c in coefs[-3::-1]:
        total = total * t + c
    return total


def sin_cos(x):
    t = x * x
    s = x * polynomial(t, sin_half)
    c = polynomial(t, cos_half)
    return s * c, 1.0 - s * s


def grain_math(stress, angles, hardness, sums, strain):
    exx, eyy, exy, trace, hydro = strain
    s1, c1 = sin_cos(angles[0])
    sq, cq = sin_cos(angles[1])
    s2, c2 = sin_cos(angles[2])
    c1c2, s1s2, c1s2, s1c2 = c1 * c2, s1 * s2, c1 * s2, s1 * c2
    r00 = c1c2 - s1s2 * cq
    r01 = -(c1s2 + s1c2 * cq)
    r02 = s1 * sq
    r10 = s1c2 + c1s2 * cq
    r11 = c1c2 * cq - s1s2
    r12 = -(c1 * sq)
    a0, b0 = r00 * exx + r10 * exy, r10 * eyy + r00 * exy
    a1, b1 = r01 * exx + r11 * exy, r11 * eyy + r01 * exy
    d00 = r00 * a0 + r10 * b0
    d11 = r01 * a1 + r11 * b1
    t00, t11 = stress[0] + d00, stress[1] + d11
    t22 = stress[2] + (trace - (d00 + d11))
    t_sum = t00 + t11
    v = [
        (t00 - t11) * 0.5,
        t_sum * (1 / math.sqrt(12)) - t22 * (2 / math.sqrt(12)),
        stress[3] + (r02 * a1 + r12 * b1),
        stress[4] + (r02 * a0 + r12 * b0),
        stress[5] + (r01 * a0 + r11 * b0),
    ]
    pressure = (t_sum + t22) * (1.0 / 3.0) + hydro
    step = 1.0 / (1.0 + sums(25))
    h0 = hardness * step * (1 / math.sqrt(2))
    h1 = h0 * (1 / math.sqrt(3))
    h2 = h0 * (1.0 / 3.0)
    bias = []
    for i in range(5):
        first, second = (h0, h1) if i == 1 else (h1, h2)
        bias.append(sums(15 + i) * first + sums(20 + i) * second)
    plain, mixed = step * (1 / 18.0), step * (math.sqrt(3) / 18.0)
    m = {}
    for e, (i, j) in enumerate(upper_pairs):
        entry = sums(e) * (mixed if (i == 1) != (j == 1) else plain)
        m[i, j] = m[j, i] = (1.0 - entry) if i == j else entry
    for _ in range(ITERS):
        fresh = []
        for i in range(5):
            off = None
            for j in range(5):
                if j != i:
                    term = m[i, j] * v[j]
                    off = term if off is None else off + term
            fresh.append((m[i, i] * v[i] + bias[i]) - off)
        v = fresh
    w = v[1] * (1 / math.sqrt(3))
    mid = pressure + w
    x = [mid + v[0], mid - v[0], pressure - 2.0 * w, v[2], v[3], v[4]]
    f0 = x[0] * r00 + x[5] * r01 + x[4] * r02
    f1 = x[5] * r00 + x[1] * r01 + x[3] * r02
    f2 = x[4] * r00 + x[3] * r01 + x[2] * r02
    g0 = x[0] * r10 + x[5] * r11 + x[4] * r12
    g1 = x[5] * r10 + x[1] * r11 + x[3] * r12
    g2 = x[4] * r10 + x[3] * r11 + x[2] * r12
    sample = (
        r00 * f0 + r01 * f1 + r02 * f2,
        r10 * g0 + r11 * g1 + r12 * g2,
        r00 * g0 + r01 * g1 + r02 * g2,
    )
    return x, sample


def bit_rows(words):
    pieces = [jnp.concatenate([w[:8], w[8:]], axis=1) for w in words]
    both = jnp.concatenate(pieces, axis=0).astype(jnp.int16)
    one, none = jnp.bfloat16(1.0), jnp.bfloat16(0.0)
    rows = [jnp.where((both & jnp.int16(1 << bit)) != 0, one, none) for bit in range(12)]
    return jnp.concatenate(rows, axis=0)


def places():
    return lax.axis_index("gx"), lax.axis_index("gy")


def sizes():
    return lax.axis_size("gx"), lax.axis_size("gy")


def whole(*shape):
    return pl.BlockSpec(shape, lambda *i: (0,) * len(shape))


def f32(*shape):
    return jax.ShapeDtypeStruct(shape, jnp.float32)


def lane_ids(rows):
    return lax.broadcasted_iota(jnp.int32, (rows, 128), 1)


def row_ids():
    return lax.broadcasted_iota(jnp.int32, (16, 128), 0)


def from_sides(got_even, got_odd, index, count):
    odd = index % 2 == 1
    after = jnp.where(odd, got_odd, got_even)
    before = jnp.where(odd, got_even, got_odd)
    return jnp.where(index == count - 1, 0.0, after), jnp.where(index == 0, 0.0, before)


def shifts_x(field, east, west):
    row = row_ids()
    return (
        jnp.where(row == 15, east, pltpu.roll(field, 15, 0)),
        jnp.where(row == 0, west, pltpu.roll(field, 1, 0)),
    )


def shifts_y(field, halo):
    lane = lane_ids(field.shape[0])
    return (
        jnp.where(lane == 127, halo, pltpu.roll(field, 127, 1)),
        jnp.where(lane == 0, halo, pltpu.roll(field, 1, 1)),
    )


def side_columns(after, before, first, last):
    lane = lane_ids(after.shape[0])
    return jnp.where(
        lane == 127,
        pltpu.roll(after, 127 - first, 1),
        jnp.where(lane == 0, pltpu.roll(before, (128 - last) % 128, 1), 0.0),
    )


def velocity_halo(counts, got):
    gx, gy = places()
    after_x, before_x = from_sides(got[0], got[1], gx, counts[0])
    after_y, before_y = from_sides(got[2], got[3], gy, counts[1])
    return after_x[0:1], before_x[15:16], side_columns(after_y, before_y, 0, 127)


def solve_kernel(
    counts, half_velocity, x_even, x_odd, y_even, y_odd, stress_in, angles_in, hardness_in, active_in,
    relaxed_out, zone_sum, rows_even, rows_odd, cols_even, cols_odd,
    relaxed, stress, angles, hardness, active, table_wide, table, sums_a, sums_b, strain, cols, sems, out_sems,
):
    blocks = hardness.shape[0] // grain_block
    gx, gy = places()

    def copies(i, kinds):
        part = pl.ds(i * grain_block, grain_block)
        every = (
            lambda: (active_in.at[:, part], active.at[:, part]),
            lambda: (stress_in.at[:, part], stress.at[:, part]),
            lambda: (angles_in.at[:, part], angles.at[:, part]),
            lambda: (hardness_in.at[part], hardness.at[part]),
        )
        return [pltpu.make_async_copy(*every[k](), sems.at[k, i]) for k in kinds]

    def out_copy(i):
        part = pl.ds(i * grain_block, grain_block)
        return pltpu.make_async_copy(relaxed.at[:, part], relaxed_out.at[:, part], out_sems.at[i])

    def count(group, sums):
        first = group * batch
        bits = [bit_rows([active[0, first + k], active[1, first + k]]) for k in range(batch)]
        sums[...] = jnp.dot(
            table[...], jnp.concatenate(bits, axis=1), preferred_element_type=jnp.float32
        )

    def update(group, sums):
        lane = lane_ids(8)
        for half in range(2):
            part = pl.ds(8 * half, 8)
            zone_strain = [strain[i, part] for i in range(5)]
            totals = [zone_sum[k, part] for k in range(3)]
            ends = [cols[c, part] for c in range(6)]
            for k in range(batch):
                g = group * batch + k
                lanes = slice(256 * k + 128 * half, 256 * k + 128 * half + 128)
                x, sample = grain_math(
                    [stress[c, g, part] for c in range(6)],
                    [angles[c, g, part] for c in range(3)],
                    hardness[g, part],
                    lambda e: sums[e * 8 : (e + 1) * 8, lanes],
                    zone_strain,
                )
                here = (lane == 2 * g) | (lane == 2 * g + 1)
                for c in range(6):
                    relaxed[c, g, part] = x[c]
                    ends[c] = jnp.where(here, pltpu.roll(x[c], 2 * g + 1, 1), ends[c])
                totals = [t + s for t, s in zip(totals, sample)]
            for k in range(3):
                zone_sum[k, part] = totals[k]
            for c in range(6):
                cols[c, part] = ends[c]

    for copy in copies(0, range(4)):
        copy.start()
    for copy in copies(1, range(4)):
        copy.start()
    fill_table(table_wide)
    table[...] = table_wide[...].astype(jnp.bfloat16)
    zone_sum[...] = jnp.zeros_like(zone_sum)
    cols[...] = jnp.zeros_like(cols)
    grads = []
    for k in range(2):
        u = half_velocity[k]
        east, west, halo = velocity_halo(counts, (x_even[k], x_odd[k], y_even[k], y_odd[k]))
        u_east, u_west = shifts_x(u, 0.5 * east, 0.5 * west)
        u_north, u_south = shifts_y(u, 0.5 * halo)
        grads.append((u_east - u_west, u_north - u_south))
    exx, eyy = grads[0][0], grads[1][1]
    exy = 0.5 * (grads[0][1] + grads[1][0])
    strain[0] = 2.0 * time_step * exx
    strain[1] = 2.0 * time_step * eyy
    strain[2] = 2.0 * time_step * exy
    strain[3] = 2.0 * time_step * (exx + eyy)
    strain[4] = lame_first * time_step * (exx + eyy)
    for i in range(2, blocks):
        for copy in copies(i, range(4)):
            copy.start()
    copies(0, [0])[0].wait()
    count(0, sums_a)

    def step(block, carry):
        for copy in copies(block, [1, 2, 3]):
            copy.wait()

        @pl.when(block < blocks - 1)
        def _():
            copies(block + 1, [0])[0].wait()

        group = block * 2
        count(group + 1, sums_b)
        update(group, sums_a)
        count(jnp.minimum(group + 2, blocks * 2 - 1), sums_a)
        update(group + 1, sums_b)
        out_copy(block).start()
        return carry

    lax.fori_loop(0, blocks, step, 0)

    n = relaxed.shape[1]
    flat = relaxed.reshape(6 * n * 16, 128)
    odd_x, odd_y = gx % 2 == 1, gy % 2 == 1
    for c in range(6):
        first = flat[pl.ds(c * n * 16, n, stride=16)]
        last = flat[pl.ds(c * n * 16 + 15, n, stride=16)]
        rows_even[c] = jnp.where(odd_x, first, last)
        rows_odd[c] = jnp.where(odd_x, last, first)
    low = lane_ids(16) % 2 == 0
    for c in range(3):
        one, other = cols[c], cols[c + 3]
        last = jnp.where(low, one, pltpu.roll(other, 1, 1))
        first = jnp.where(low, pltpu.roll(one, 127, 1), other)
        cols_even[c] = jnp.where(odd_y, first, last)
        cols_odd[c] = jnp.where(odd_y, last, first)
    for i in range(blocks):
        out_copy(i).wait()


def solve_grains(half_velocity, got, stress, angles, hardness, active):
    n = hardness.shape[0]
    in_hbm = pl.BlockSpec(memory_space=pltpu.HBM)
    return pl.pallas_call(
        functools.partial(solve_kernel, sizes()),
        grid=(1,),
        in_specs=[
            whole(2, 16, 128),
            *[whole(*g.shape) for g in got],
            *[in_hbm] * 4,
        ],
        out_specs=[
            in_hbm,
            whole(3, 16, 128),
            whole(6, n, 128),
            whole(6, n, 128),
            whole(3, 16, 128),
            whole(3, 16, 128),
        ],
        out_shape=[f32(6, n, 16, 128), f32(3, 16, 128), f32(6, n, 128), f32(6, n, 128)]
        + [f32(3, 16, 128)] * 2,
        scratch_shapes=[
            pltpu.VMEM((6, n, 16, 128), jnp.float32),
            pltpu.VMEM(stress.shape, jnp.float32),
            pltpu.VMEM(angles.shape, jnp.float32),
            pltpu.VMEM(hardness.shape, jnp.float32),
            pltpu.VMEM(active.shape, jnp.int32),
            pltpu.VMEM((8 * n_sums, 192), jnp.float32),
            pltpu.VMEM((8 * n_sums, 192), jnp.bfloat16),
            pltpu.VMEM((8 * n_sums, 256 * batch), jnp.float32),
            pltpu.VMEM((8 * n_sums, 256 * batch), jnp.float32),
            pltpu.VMEM((5, 16, 128), jnp.float32),
            pltpu.VMEM((6, 16, 128), jnp.float32),
            pltpu.SemaphoreType.DMA((4, n // grain_block)),
            pltpu.SemaphoreType.DMA((n // grain_block,)),
        ],
        compiler_params=pltpu.CompilerParams(vmem_limit_bytes=53 * 2**20),
        cost_estimate=pl.CostEstimate(flops=10**8, bytes_accessed=10**7, transcendentals=0),
    )(half_velocity, *got, stress, angles, hardness, active)


def zone_update(counts, velocity, fields, u_got, stress, s_got, tall, moved, velocity_out):
    gx, gy = places()
    sx_even, sx_odd, sy_even, sy_odd = s_got
    s_east, s_west = from_sides(sx_even, sx_odd, gx, counts[0])
    s_north, s_south = from_sides(sy_even, sy_odd, gy, counts[1])
    for c in range(3):
        tall[c, 0:2] = s_west[2 * c : 2 * c + 2]
        tall[c, 2:18] = stress[c]
        tall[c, 18:20] = s_east[2 * c : 2 * c + 2]
    near = [side_columns(s_north, s_south, 4 * c + 2, 4 * c + 1) for c in range(3)]
    far = [side_columns(s_north, s_south, 4 * c + 3, 4 * c) for c in range(3)]
    lane = lane_ids(16)
    sign = jnp.where(lane == 127, 0.5, -0.5)

    def x_diff(c):
        return (tall[c, 2:20] - tall[c, 0:18]) * 0.5

    def y_diff(c):
        after, before = shifts_y(tall[c, 1:19], near[c][:18])
        return (after - before) * 0.5

    def rim_x(c):
        return (near[c][2:18] - near[c][0:16]) * 0.5

    def rim_y(c):
        return (far[c][1:17] - stress[c]) * sign

    force = [x_diff(0) + y_diff(2), x_diff(2) + y_diff(1)]
    rim_force = [rim_x(0) + rim_y(2), rim_x(2) + rim_y(1)]
    field_rim = [
        side_columns(s_north[:16], s_south[:16], 13 + 2 * k, 12 + 2 * k) for k in range(3)
    ]
    sides = [velocity_halo(counts, [got[k] for got in u_got]) for k in range(2)]

    def high(k):
        return jnp.concatenate([s_west[6 + k : 7 + k], fields[k], s_east[6 + k : 7 + k]], axis=0)

    mass = time_step * high(0)
    rim = []
    for k in range(2):
        east, west, halo = sides[k]
        moved[k, 0:18] = jnp.concatenate([west, velocity[k], east], axis=0) + mass * force[k]
        rim.append(halo + time_step * field_rim[0] * rim_force[k])
    frac_x = time_step * 0.5 * (moved[0, 0:17] + moved[0, 1:18])
    x_self = frac_x * high(1)[:17]
    x_next = frac_x - x_self
    own = [moved[k, 1:17] for k in range(2)]
    y_sides = [shifts_y(own[k], rim[k]) for k in range(2)]
    frac_y = time_step * 0.5 * (own[1] + y_sides[1][0])
    frac_before = time_step * 0.5 * (own[1] + y_sides[1][1])
    flag = fields[2]
    flag_before = jnp.where(lane == 0, field_rim[2], pltpu.roll(flag, 1, 1))
    y_self, before_self = frac_y * flag, frac_before * flag_before
    y_next, before_next = frac_y - y_self, frac_before - before_self
    centre = 1.0 - x_self[1:17] + x_next[0:16] - y_self + before_next
    coefs = (centre, -x_next[1:17], x_self[0:16], -y_next, before_self)
    for k in range(2):
        velocity_out[k] = (
            centre * own[k]
            + coefs[1] * moved[k, 2:18]
            + coefs[2] * moved[k, 0:16]
            + coefs[3] * y_sides[k][0]
            + coefs[4] * y_sides[k][1]
        )
    return coefs


def remap_kernel(
    counts, velocity, fields, ux_even, ux_odd, uy_even, uy_odd, stress, sx_even, sx_odd, y_even, y_odd,
    relaxed_in, rows_even, rows_odd,
    out_hbm, velocity_out, relaxed, out, tall, moved, coefs, rows, cols, sems, out_sems,
):
    size = rows.shape[2]
    chunks = relaxed.shape[1] // size
    gx, gy = places()
    odd_x, odd_y = gx % 2 == 1, gy % 2 == 1

    def copy(i):
        part = pl.ds(i * size, size)
        return pltpu.make_async_copy(relaxed_in.at[:, part], relaxed.at[:, part], sems.at[i])

    def out_copy(i):
        part = pl.ds(i * (size // 2), size // 2)
        return pltpu.make_async_copy(out.at[:, part], out_hbm.at[:, part], out_sems.at[i])

    for i in range(chunks):
        copy(i).start()
    lane, row = lane_ids(16), row_ids()

    fresh = zone_update(
        counts,
        velocity,
        fields,
        (ux_even, ux_odd, uy_even, uy_odd),
        stress,
        (sx_even[...], sx_odd[...], y_even[48:72], y_odd[48:72]),
        tall,
        moved,
        velocity_out,
    )
    centre, east, west, north, south = fresh
    coefs[0] = centre
    coefs[1] = jnp.where(row == 15, 0.0, east)
    coefs[2] = jnp.where(row == 0, 0.0, west)
    coefs[3] = jnp.where(lane == 127, 0.0, north)
    coefs[4] = jnp.where(lane == 0, 0.0, south)
    coefs[5] = jnp.where((row == 15) & (gx < counts[0] - 1), east, 0.0)
    coefs[6] = jnp.where((row == 0) & (gx > 0), west, 0.0)
    rim = jnp.where((lane == 127) & (gy < counts[1] - 1), north, 0.0)
    coefs[7] = jnp.where((lane == 0) & (gy > 0), south, rim)
    for c in range(3):
        part = slice(16 * c, 16 * c + 16)
        got_even, got_odd = y_even[part], y_odd[part]
        after = jnp.where(odd_y, got_odd, got_even)
        before = jnp.where(odd_y, got_even, got_odd)
        cols[c] = jnp.where(lane % 2 == 0, after, pltpu.roll(before, 1, 1))
        cols[c + 3] = jnp.where(lane % 2 == 0, pltpu.roll(after, 127, 1), before)

    centre, east, west, north, south, _, _, rim = [coefs[i] for i in range(8)]
    high_east, low_west = coefs[5, 8:16], coefs[6, 0:8]

    def one(g, k):
        for c in range(6):
            q = relaxed[c, g]
            halo = pltpu.roll(cols[c], 127 - 2 * g, 1)
            total = centre * q + north * pltpu.roll(q, 127, 1) + south * pltpu.roll(q, 1, 1)
            total = total + rim * halo
            total = total + east * pltpu.roll(q, 15, 0) + west * pltpu.roll(q, 1, 0)
            out[c, g, 0:8] = total[:8] + low_west * rows[1, c, k : k + 1, :]
            out[c, g, 8:16] = total[8:] + high_east * rows[0, c, k : k + 1, :]

    def chunk(i, carry):
        part = pl.ds(pl.multiple_of(i * size, size), size)
        rows[0] = jnp.where(odd_x, rows_odd[:, part], rows_even[:, part])
        rows[1] = jnp.where(odd_x, rows_even[:, part], rows_odd[:, part])
        copy(i).wait()
        for k in range(size):
            one(i * size + k, k)
            if k == size // 2 - 1:
                out_copy(i * 2).start()
        out_copy(i * 2 + 1).start()
        return carry

    lax.fori_loop(0, chunks, chunk, 0)
    for i in range(2 * chunks):
        out_copy(i).wait()


def remap_grains(velocity, fields, u_got, stress, s_got, y_got, relaxed, rows_even, rows_odd):
    n = relaxed.shape[1]
    size = 16
    small = (velocity, fields, *u_got, stress, *s_got, *y_got)
    return pl.pallas_call(
        functools.partial(remap_kernel, sizes()),
        grid=(1,),
        in_specs=[
            *[whole(*a.shape) for a in small],
            pl.BlockSpec(memory_space=pltpu.HBM),
            whole(*rows_even.shape),
            whole(*rows_odd.shape),
        ],
        out_specs=[
            pl.BlockSpec(memory_space=pltpu.HBM),
            whole(2, 16, 128),
        ],
        out_shape=[f32(*relaxed.shape), f32(2, 16, 128)],
        scratch_shapes=[
            pltpu.VMEM(relaxed.shape, jnp.float32),
            pltpu.VMEM(relaxed.shape, jnp.float32),
            pltpu.VMEM((3, 24, 128), jnp.float32),
            pltpu.VMEM((2, 24, 128), jnp.float32),
            pltpu.VMEM((8, 16, 128), jnp.float32),
            pltpu.VMEM((2, 6, size, 128), jnp.float32),
            pltpu.VMEM((6, 16, 128), jnp.float32),
            pltpu.SemaphoreType.DMA((n // size,)),
            pltpu.SemaphoreType.DMA((2 * n // size,)),
        ],
        compiler_params=pltpu.CompilerParams(vmem_limit_bytes=53 * 2**20),
        cost_estimate=pl.CostEstimate(flops=10**7, bytes_accessed=10**7, transcendentals=0),
    )(*small, relaxed, rows_even, rows_odd)


def swap_even(block, axis):
    return lax.ppermute(block, axis, [(i, i ^ 1) for i in range(lax.axis_size(axis))])


def swap_odd_y(block):
    count_x, count_y = sizes()
    pairs = []
    for x in range(count_x):
        for y in range(count_y):
            end = y in (0, count_y - 1)
            to_x, to_y = (x ^ 1, y) if end else (x, y + 1 if y % 2 else y - 1)
            pairs.append((x * count_y + y, to_x * count_y + to_y))
    return lax.ppermute(block, ("gx", "gy"), pairs)


def swap_odd_x(block, crossed):
    count = lax.axis_size("gx")
    pairs = []
    for x in range(count):
        for a in range(2):
            end = x in (0, count - 1)
            to_x = x if end else (x + 1 if x % 2 else x - 1)
            to_a = 1 - a if end or crossed else a
            pairs.append((x * 2 + a, to_x * 2 + to_a))
    return lax.ppermute(block, ("gx", "ga"), pairs)


def per_device(velocity, density, grain_stress, grain_angles, hardness, active, donor_faces):
    gx = lax.axis_index("gx")
    odd_x = gx % 2 == 1
    u_got = (
        swap_even(velocity, "gx"),
        swap_odd_x(velocity, True),
        swap_even(velocity, "gy"),
        swap_odd_y(velocity),
    )
    relaxed, part, rows_even, rows_odd, cols_even, cols_odd = solve_grains(
        0.5 * velocity, u_got, grain_stress, grain_angles, hardness, active
    )
    density, donor_faces, part = lax.optimization_barrier((density, donor_faces, part))
    fields = jnp.concatenate([(1.0 / density)[None], donor_faces.astype(jnp.float32)], axis=0)
    zone_stress = (part + swap_even(part, "ga")) * (1.0 / G)
    zone_stress, rows_even, rows_odd = lax.optimization_barrier((zone_stress, rows_even, rows_odd))
    far_rows_odd = swap_odd_x(rows_odd, False)
    far_rows_even = swap_even(rows_even, "gx")
    spare = jnp.zeros((7, 128), jnp.float32)
    first = jnp.concatenate([zone_stress[:, :2].reshape(6, 128), fields[:, 0], spare], axis=0)
    last = jnp.concatenate([zone_stress[:, -2:].reshape(6, 128), fields[:, -1], spare], axis=0)
    got_even = swap_even(jnp.where(odd_x, first, last), "gx")
    got_odd = swap_odd_x(jnp.where(odd_x, last, first), True)
    east, west = from_sides(got_even[:6], got_odd[:6], gx, lax.axis_size("gx"))
    east, west = east.reshape(3, 2, 128), west.reshape(3, 2, 128)
    tall = jnp.concatenate([west[:, 1:], zone_stress, east[:, :1]], axis=1)
    lane = lax.broadcasted_iota(jnp.int32, (18, 128), 1)
    sides = jnp.zeros((18, 128), jnp.float32)
    for c in range(3):
        sides = jnp.where(lane // 4 == c, jnp.roll(tall[c], 4 * c + 2, axis=1), sides)
    sides = jnp.pad(sides, ((0, 6), (0, 0)))
    lane = lax.broadcasted_iota(jnp.int32, (16, 128), 1)
    field_sides = jnp.zeros((16, 128), jnp.float32)
    for k in range(3):
        field_sides = jnp.where(lane // 2 == 6 + k, jnp.roll(fields[k], 13 + 2 * k, axis=1), field_sides)
    sides = sides + jnp.pad(field_sides, ((0, 8), (0, 0)))
    y_got = (
        swap_even(jnp.concatenate([cols_even.reshape(48, 128), sides], axis=0), "gy"),
        swap_odd_y(jnp.concatenate([cols_odd.reshape(48, 128), sides], axis=0)),
    )
    stress_out, velocity_out = remap_grains(
        velocity, fields, u_got, zone_stress, (got_even, got_odd), y_got, relaxed, far_rows_even, far_rows_odd
    )
    return (velocity_out, stress_out, zone_stress)


def solution(mesh):
    return jax.shard_map(
        per_device,
        mesh=mesh,
        in_specs=(
            P(None, "gx", "gy"),
            P("gx", "gy"),
            P(None, "ga", "gx", "gy"),
            P(None, "ga", "gx", "gy"),
            P("ga", "gx", "gy"),
            P(None, "ga", "gx", "gy"),
            P(None, "gx", "gy"),
        ),
        out_specs=(P(None, "gx", "gy"), P(None, "ga", "gx", "gy"), P(None, "gx", "gy")),
        check_vma=False,
    )
```

```python
import functools
import math

import jax
import jax.numpy as jnp
import numpy as np
from jax import lax
from jax.experimental import pallas as pl
from jax.experimental.pallas import tpu as pltpu
from jax.sharding import PartitionSpec as P

G = 128
ITERS = 4

time_step = 0.1
lame_first = 1.5
batch = 4
grain_block = 2 * batch
system_list = (
    ((0, 1, 1), (1, 1, -1)),
    ((0, 1, 1), (1, -1, 1)),
    ((1, 0, 1), (1, 1, -1)),
    ((1, 0, 1), (-1, 1, 1)),
    ((1, 1, 0), (1, -1, 1)),
    ((1, 1, 0), (-1, 1, 1)),
    ((0, 1, -1), (1, 1, 1)),
    ((0, 1, -1), (1, -1, -1)),
    ((1, 0, -1), (1, 1, 1)),
    ((1, 0, -1), (1, -1, 1)),
    ((1, -1, 0), (1, 1, 1)),
    ((1, -1, 0), (1, 1, -1)),
    ((1, 1, 2), (1, 1, -1)),
    ((1, 1, -2), (1, 1, 1)),
    ((1, -1, 2), (1, -1, -1)),
    ((-1, 1, 2), (-1, 1, -1)),
    ((1, 2, 1), (1, -1, 1)),
    ((1, -2, 1), (1, 1, 1)),
    ((-1, 2, 1), (1, 1, -1)),
    ((1, 2, -1), (-1, 1, 1)),
    ((2, 1, 1), (-1, 1, 1)),
    ((-2, 1, 1), (1, 1, 1)),
    ((2, -1, 1), (1, 1, -1)),
    ((2, 1, -1), (1, -1, 1)),
)
upper_pairs = [(i, j) for i in range(5) for j in range(i, 5)]
n_sums = 26


def slip_sums_table():
    table = np.zeros((n_sums, 24))
    for s, (normal, direction) in enumerate(system_list):
        q = np.outer(direction, normal) + np.outer(normal, direction)
        k = np.array([(q[0, 0] - q[1, 1]) / 2, -q[2, 2] / 2, q[1, 2], q[0, 2], q[0, 1]])
        weight = 3 if s < 12 else 1
        for e, (i, j) in enumerate(upper_pairs):
            table[e, s] = weight * k[i] * k[j] * (3 if i == j == 1 else 1)
        first = 15 if s < 12 else 20
        table[first : first + 5, s] = k
        table[25, s] = 1
    columns = np.zeros((n_sums, 24))
    for s in range(24):
        word, bit = divmod(s, 12)
        columns[:, 2 * bit + word] = table[:, s]
    return columns


def fill_table(table):
    columns = slip_sums_table()
    lane = lax.broadcasted_iota(jnp.int32, (8, 192), 1)
    own = lane % 8 == lax.broadcasted_iota(jnp.int32, (8, 192), 0)
    system = lane // 8
    for e in range(n_sums):
        entry = jnp.zeros((8, 192), jnp.float32)
        for k in range(24):
            if columns[e, k]:
                entry = jnp.where(system == k, float(columns[e, k]), entry)
        table[8 * e : 8 * e + 8] = jnp.where(own, entry, 0.0)


def fitted(function, degree, top):
    series = np.polynomial.chebyshev.Chebyshev.interpolate(function, degree, domain=[0.0, top])
    return [float(c) for c in series.convert(kind=np.polynomial.Polynomial).coef]


angle_top = 3.1416**2
sin_half = fitted(lambda t: math.sqrt(2) * np.sin(np.sqrt(t) / 2) / np.sqrt(t), 4, angle_top)
cos_half = fitted(lambda t: math.sqrt(2) * np.cos(np.sqrt(t) / 2), 4, angle_top)


def polynomial(t, coefs):
    total = coefs[-1] * t + coefs[-2]
    for c in coefs[-3::-1]:
        total = total * t + c
    return total


def sin_cos(x):
    t = x * x
    s = x * polynomial(t, sin_half)
    c = polynomial(t, cos_half)
    return s * c, 1.0 - s * s


def grain_math(stress, angles, hardness, sums, strain):
    exx, eyy, exy, trace, hydro = strain
    s1, c1 = sin_cos(angles[0])
    sq, cq = sin_cos(angles[1])
    s2, c2 = sin_cos(angles[2])
    c1c2, s1s2, c1s2, s1c2 = c1 * c2, s1 * s2, c1 * s2, s1 * c2
    r00 = c1c2 - s1s2 * cq
    r01 = -(c1s2 + s1c2 * cq)
    r02 = s1 * sq
    r10 = s1c2 + c1s2 * cq
    r11 = c1c2 * cq - s1s2
    r12 = -(c1 * sq)
    a0, b0 = r00 * exx + r10 * exy, r10 * eyy + r00 * exy
    a1, b1 = r01 * exx + r11 * exy, r11 * eyy + r01 * exy
    d00 = r00 * a0 + r10 * b0
    d11 = r01 * a1 + r11 * b1
    t00, t11 = stress[0] + d00, stress[1] + d11
    t22 = stress[2] + (trace - (d00 + d11))
    t_sum = t00 + t11
    v = [
        (t00 - t11) * 0.5,
        t_sum * (1 / math.sqrt(12)) - t22 * (2 / math.sqrt(12)),
        stress[3] + (r02 * a1 + r12 * b1),
        stress[4] + (r02 * a0 + r12 * b0),
        stress[5] + (r01 * a0 + r11 * b0),
    ]
    pressure = (t_sum + t22) * (1.0 / 3.0) + hydro
    step = 1.0 / (1.0 + sums(25))
    h0 = hardness * step * (1 / math.sqrt(2))
    h1 = h0 * (1 / math.sqrt(3))
    h2 = h0 * (1.0 / 3.0)
    bias = []
    for i in range(5):
        first, second = (h0, h1) if i == 1 else (h1, h2)
        bias.append(sums(15 + i) * first + sums(20 + i) * second)
    plain, mixed = step * (1 / 18.0), step * (math.sqrt(3) / 18.0)
    m = {}
    for e, (i, j) in enumerate(upper_pairs):
        entry = sums(e) * (mixed if (i == 1) != (j == 1) else plain)
        m[i, j] = m[j, i] = (1.0 - entry) if i == j else entry
    for _ in range(ITERS):
        fresh = []
        for i in range(5):
            off = None
            for j in range(5):
                if j != i:
                    term = m[i, j] * v[j]
                    off = term if off is None else off + term
            fresh.append((m[i, i] * v[i] + bias[i]) - off)
        v = fresh
    w = v[1] * (1 / math.sqrt(3))
    mid = pressure + w
    x = [mid + v[0], mid - v[0], pressure - 2.0 * w, v[2], v[3], v[4]]
    f0 = x[0] * r00 + x[5] * r01 + x[4] * r02
    f1 = x[5] * r00 + x[1] * r01 + x[3] * r02
    f2 = x[4] * r00 + x[3] * r01 + x[2] * r02
    g0 = x[0] * r10 + x[5] * r11 + x[4] * r12
    g1 = x[5] * r10 + x[1] * r11 + x[3] * r12
    g2 = x[4] * r10 + x[3] * r11 + x[2] * r12
    sample = (
        r00 * f0 + r01 * f1 + r02 * f2,
        r10 * g0 + r11 * g1 + r12 * g2,
        r00 * g0 + r01 * g1 + r02 * g2,
    )
    return x, sample


def bit_rows(words):
    pieces = [jnp.concatenate([w[:8], w[8:]], axis=1) for w in words]
    both = jnp.concatenate(pieces, axis=0).astype(jnp.int16)
    one, none = jnp.bfloat16(1.0), jnp.bfloat16(0.0)
    rows = [jnp.where((both & jnp.int16(1 << bit)) != 0, one, none) for bit in range(12)]
    return jnp.concatenate(rows, axis=0)


def places():
    return lax.axis_index("gx"), lax.axis_index("gy")


def sizes():
    return lax.axis_size("gx"), lax.axis_size("gy")


def whole(*shape):
    return pl.BlockSpec(shape, lambda *i: (0,) * len(shape))


def f32(*shape):
    return jax.ShapeDtypeStruct(shape, jnp.float32)


def lane_ids(rows):
    return lax.broadcasted_iota(jnp.int32, (rows, 128), 1)


def row_ids():
    return lax.broadcasted_iota(jnp.int32, (16, 128), 0)


def from_sides(got_even, got_odd, index, count):
    odd = index % 2 == 1
    after = jnp.where(odd, got_odd, got_even)
    before = jnp.where(odd, got_even, got_odd)
    return jnp.where(index == count - 1, 0.0, after), jnp.where(index == 0, 0.0, before)


def shifts_x(field, east, west):
    row = row_ids()
    return (
        jnp.where(row == 15, east, pltpu.roll(field, 15, 0)),
        jnp.where(row == 0, west, pltpu.roll(field, 1, 0)),
    )


def shifts_y(field, halo):
    lane = lane_ids(field.shape[0])
    return (
        jnp.where(lane == 127, halo, pltpu.roll(field, 127, 1)),
        jnp.where(lane == 0, halo, pltpu.roll(field, 1, 1)),
    )


def side_columns(after, before, first, last):
    lane = lane_ids(after.shape[0])
    return jnp.where(
        lane == 127,
        pltpu.roll(after, 127 - first, 1),
        jnp.where(lane == 0, pltpu.roll(before, (128 - last) % 128, 1), 0.0),
    )


def velocity_halo(counts, got):
    gx, gy = places()
    after_x, before_x = from_sides(got[0], got[1], gx, counts[0])
    after_y, before_y = from_sides(got[2], got[3], gy, counts[1])
    return after_x[0:1], before_x[15:16], side_columns(after_y, before_y, 0, 127)


def solve_kernel(
    counts, half_velocity, x_even, x_odd, y_even, y_odd, stress_in, angles_in, hardness_in, active_in,
    relaxed_out, zone_sum, rows_even, rows_odd, cols_even, cols_odd,
    relaxed, stress, angles, hardness, active, table_wide, table, sums_a, sums_b, strain, cols, sems, out_sems,
):
    blocks = hardness.shape[0] // grain_block
    gx, gy = places()

    def copies(i, kinds):
        part = pl.ds(i * grain_block, grain_block)
        every = (
            lambda: (active_in.at[:, part], active.at[:, part]),
            lambda: (stress_in.at[:, part], stress.at[:, part]),
            lambda: (angles_in.at[:, part], angles.at[:, part]),
            lambda: (hardness_in.at[part], hardness.at[part]),
        )
        return [pltpu.make_async_copy(*every[k](), sems.at[k, i]) for k in kinds]

    def out_copy(i):
        part = pl.ds(i * grain_block, grain_block)
        return pltpu.make_async_copy(relaxed.at[:, part], relaxed_out.at[:, part], out_sems.at[i])

    def count(group, sums):
        first = group * batch
        bits = [bit_rows([active[0, first + k], active[1, first + k]]) for k in range(batch)]
        sums[...] = jnp.dot(
            table[...], jnp.concatenate(bits, axis=1), preferred_element_type=jnp.float32
        )

    def update(group, sums):
        lane = lane_ids(8)
        for half in range(2):
            part = pl.ds(8 * half, 8)
            zone_strain = [strain[i, part] for i in range(5)]
            totals = [zone_sum[k, part] for k in range(3)]
            ends = [cols[c, part] for c in range(6)]
            for k in range(batch):
                g = group * batch + k
                lanes = slice(256 * k + 128 * half, 256 * k + 128 * half + 128)
                x, sample = grain_math(
                    [stress[c, g, part] for c in range(6)],
                    [angles[c, g, part] for c in range(3)],
                    hardness[g, part],
                    lambda e: sums[e * 8 : (e + 1) * 8, lanes],
                    zone_strain,
                )
                here = (lane == 2 * g) | (lane == 2 * g + 1)
                for c in range(6):
                    relaxed[c, g, part] = x[c]
                    ends[c] = jnp.where(here, pltpu.roll(x[c], 2 * g + 1, 1), ends[c])
                totals = [t + s for t, s in zip(totals, sample)]
            for k in range(3):
                zone_sum[k, part] = totals[k]
            for c in range(6):
                cols[c, part] = ends[c]

    for copy in copies(0, range(4)):
        copy.start()
    for copy in copies(1, range(4)):
        copy.start()
    fill_table(table_wide)
    table[...] = table_wide[...].astype(jnp.bfloat16)
    zone_sum[...] = jnp.zeros_like(zone_sum)
    cols[...] = jnp.zeros_like(cols)
    grads = []
    for k in range(2):
        u = half_velocity[k]
        east, west, halo = velocity_halo(counts, (x_even[k], x_odd[k], y_even[k], y_odd[k]))
        u_east, u_west = shifts_x(u, 0.5 * east, 0.5 * west)
        u_north, u_south = shifts_y(u, 0.5 * halo)
        grads.append((u_east - u_west, u_north - u_south))
    exx, eyy = grads[0][0], grads[1][1]
    exy = 0.5 * (grads[0][1] + grads[1][0])
    strain[0] = 2.0 * time_step * exx
    strain[1] = 2.0 * time_step * eyy
    strain[2] = 2.0 * time_step * exy
    strain[3] = 2.0 * time_step * (exx + eyy)
    strain[4] = lame_first * time_step * (exx + eyy)
    for i in range(2, blocks):
        for copy in copies(i, range(4)):
            copy.start()
    copies(0, [0])[0].wait()
    count(0, sums_a)

    def step(block, carry):
        for copy in copies(block, [1, 2, 3]):
            copy.wait()

        @pl.when(block < blocks - 1)
        def _():
            copies(block + 1, [0])[0].wait()

        group = block * 2
        count(group + 1, sums_b)
        update(group, sums_a)
        count(jnp.minimum(group + 2, blocks * 2 - 1), sums_a)
        update(group + 1, sums_b)
        out_copy(block).start()
        return carry

    lax.fori_loop(0, blocks, step, 0)

    n = relaxed.shape[1]
    flat = relaxed.reshape(6 * n * 16, 128)
    odd_x, odd_y = gx % 2 == 1, gy % 2 == 1
    for c in range(6):
        first = flat[pl.ds(c * n * 16, n, stride=16)]
        last = flat[pl.ds(c * n * 16 + 15, n, stride=16)]
        rows_even[c] = jnp.where(odd_x, first, last)
        rows_odd[c] = jnp.where(odd_x, last, first)
    low = lane_ids(16) % 2 == 0
    for c in range(3):
        one, other = cols[c], cols[c + 3]
        last = jnp.where(low, one, pltpu.roll(other, 1, 1))
        first = jnp.where(low, pltpu.roll(one, 127, 1), other)
        cols_even[c] = jnp.where(odd_y, first, last)
        cols_odd[c] = jnp.where(odd_y, last, first)
    for i in range(blocks):
        out_copy(i).wait()


def solve_grains(half_velocity, got, stress, angles, hardness, active):
    n = hardness.shape[0]
    in_hbm = pl.BlockSpec(memory_space=pltpu.HBM)
    return pl.pallas_call(
        functools.partial(solve_kernel, sizes()),
        grid=(1,),
        in_specs=[
            whole(2, 16, 128),
            *[whole(*g.shape) for g in got],
            *[in_hbm] * 4,
        ],
        out_specs=[
            in_hbm,
            whole(3, 16, 128),
            whole(6, n, 128),
            whole(6, n, 128),
            whole(3, 16, 128),
            whole(3, 16, 128),
        ],
        out_shape=[f32(6, n, 16, 128), f32(3, 16, 128), f32(6, n, 128), f32(6, n, 128)]
        + [f32(3, 16, 128)] * 2,
        scratch_shapes=[
            pltpu.VMEM((6, n, 16, 128), jnp.float32),
            pltpu.VMEM(stress.shape, jnp.float32),
            pltpu.VMEM(angles.shape, jnp.float32),
            pltpu.VMEM(hardness.shape, jnp.float32),
            pltpu.VMEM(active.shape, jnp.int32),
            pltpu.VMEM((8 * n_sums, 192), jnp.float32),
            pltpu.VMEM((8 * n_sums, 192), jnp.bfloat16),
            pltpu.VMEM((8 * n_sums, 256 * batch), jnp.float32),
            pltpu.VMEM((8 * n_sums, 256 * batch), jnp.float32),
            pltpu.VMEM((5, 16, 128), jnp.float32),
            pltpu.VMEM((6, 16, 128), jnp.float32),
            pltpu.SemaphoreType.DMA((4, n // grain_block)),
            pltpu.SemaphoreType.DMA((n // grain_block,)),
        ],
        compiler_params=pltpu.CompilerParams(vmem_limit_bytes=53 * 2**20),
        cost_estimate=pl.CostEstimate(flops=10**8, bytes_accessed=10**7, transcendentals=0),
    )(half_velocity, *got, stress, angles, hardness, active)


def zone_update(counts, velocity, fields, u_got, stress, s_got, tall, moved, velocity_out):
    gx, gy = places()
    sx_even, sx_odd, sy_even, sy_odd = s_got
    s_east, s_west = from_sides(sx_even, sx_odd, gx, counts[0])
    s_north, s_south = from_sides(sy_even, sy_odd, gy, counts[1])
    for c in range(3):
        tall[c, 0:2] = s_west[2 * c : 2 * c + 2]
        tall[c, 2:18] = stress[c]
        tall[c, 18:20] = s_east[2 * c : 2 * c + 2]
    near = [side_columns(s_north, s_south, 4 * c + 2, 4 * c + 1) for c in range(3)]
    far = [side_columns(s_north, s_south, 4 * c + 3, 4 * c) for c in range(3)]
    lane = lane_ids(16)
    sign = jnp.where(lane == 127, 0.5, -0.5)

    def x_diff(c):
        return (tall[c, 2:20] - tall[c, 0:18]) * 0.5

    def y_diff(c):
        after, before = shifts_y(tall[c, 1:19], near[c][:18])
        return (after - before) * 0.5

    def rim_x(c):
        return (near[c][2:18] - near[c][0:16]) * 0.5

    def rim_y(c):
        return (far[c][1:17] - stress[c]) * sign

    force = [x_diff(0) + y_diff(2), x_diff(2) + y_diff(1)]
    rim_force = [rim_x(0) + rim_y(2), rim_x(2) + rim_y(1)]
    field_rim = [
        side_columns(s_north[:16], s_south[:16], 13 + 2 * k, 12 + 2 * k) for k in range(3)
    ]
    sides = [velocity_halo(counts, [got[k] for got in u_got]) for k in range(2)]

    def high(k):
        return jnp.concatenate([s_west[6 + k : 7 + k], fields[k], s_east[6 + k : 7 + k]], axis=0)

    mass = time_step * high(0)
    rim = []
    for k in range(2):
        east, west, halo = sides[k]
        moved[k, 0:18] = jnp.concatenate([west, velocity[k], east], axis=0) + mass * force[k]
        rim.append(halo + time_step * field_rim[0] * rim_force[k])
    frac_x = time_step * 0.5 * (moved[0, 0:17] + moved[0, 1:18])
    x_self = frac_x * high(1)[:17]
    x_next = frac_x - x_self
    own = [moved[k, 1:17] for k in range(2)]
    y_sides = [shifts_y(own[k], rim[k]) for k in range(2)]
    frac_y = time_step * 0.5 * (own[1] + y_sides[1][0])
    frac_before = time_step * 0.5 * (own[1] + y_sides[1][1])
    flag = fields[2]
    flag_before = jnp.where(lane == 0, field_rim[2], pltpu.roll(flag, 1, 1))
    y_self, before_self = frac_y * flag, frac_before * flag_before
    y_next, before_next = frac_y - y_self, frac_before - before_self
    centre = 1.0 - x_self[1:17] + x_next[0:16] - y_self + before_next
    coefs = (centre, -x_next[1:17], x_self[0:16], -y_next, before_self)
    for k in range(2):
        velocity_out[k] = (
            centre * own[k]
            + coefs[1] * moved[k, 2:18]
            + coefs[2] * moved[k, 0:16]
            + coefs[3] * y_sides[k][0]
            + coefs[4] * y_sides[k][1]
        )
    return coefs


def remap_kernel(
    counts, velocity, fields, ux_even, ux_odd, uy_even, uy_odd, stress, sx_even, sx_odd, y_even, y_odd,
    relaxed_in, rows_even, rows_odd,
    out, velocity_out, relaxed, tall, moved, coefs, rows, cols, sems,
):
    block = pl.program_id(0)
    size = out.shape[1]
    gx, gy = places()
    odd_x = gx % 2 == 1

    def copy(i):
        part = pl.ds(i * size, size)
        return pltpu.make_async_copy(relaxed_in.at[:, part], relaxed.at[:, part], sems.at[i])

    @pl.when(block == 0)
    def _():
        for i in range(relaxed.shape[1] // size):
            copy(i).start()

    rows[0] = jnp.where(odd_x, rows_odd[...], rows_even[...])
    rows[1] = jnp.where(odd_x, rows_even[...], rows_odd[...])
    lane, row = lane_ids(16), row_ids()

    @pl.when(block == 0)
    def _():
        fresh = zone_update(
            counts,
            velocity,
            fields,
            (ux_even, ux_odd, uy_even, uy_odd),
            stress,
            (sx_even[...], sx_odd[...], y_even[48:72], y_odd[48:72]),
            tall,
            moved,
            velocity_out,
        )
        centre, east, west, north, south = fresh
        coefs[0] = centre
        coefs[1] = jnp.where(row == 15, 0.0, east)
        coefs[2] = jnp.where(row == 0, 0.0, west)
        coefs[3] = jnp.where(lane == 127, 0.0, north)
        coefs[4] = jnp.where(lane == 0, 0.0, south)
        coefs[5] = jnp.where((row == 15) & (gx < counts[0] - 1), east, 0.0)
        coefs[6] = jnp.where((row == 0) & (gx > 0), west, 0.0)
        rim = jnp.where((lane == 127) & (gy < counts[1] - 1), north, 0.0)
        coefs[7] = jnp.where((lane == 0) & (gy > 0), south, rim)
        odd_y = gy % 2 == 1
        for c in range(3):
            part = slice(16 * c, 16 * c + 16)
            got_even, got_odd = y_even[part], y_odd[part]
            after = jnp.where(odd_y, got_odd, got_even)
            before = jnp.where(odd_y, got_even, got_odd)
            cols[c] = jnp.where(lane % 2 == 0, after, pltpu.roll(before, 1, 1))
            cols[c + 3] = jnp.where(lane % 2 == 0, pltpu.roll(after, 127, 1), before)

    centre, east, west, north, south, _, _, rim = [coefs[i] for i in range(8)]
    high_east, low_west = coefs[5, 8:16], coefs[6, 0:8]
    copy(block).wait()

    def one(g):
        for c in range(6):
            q = relaxed[c, block * size + g]
            halo = pltpu.roll(cols[c], 127 - 2 * (block * size + g), 1)
            total = centre * q + north * pltpu.roll(q, 127, 1) + south * pltpu.roll(q, 1, 1)
            total = total + rim * halo
            total = total + east * pltpu.roll(q, 15, 0) + west * pltpu.roll(q, 1, 0)
            out[c, g, 0:8] = total[:8] + low_west * rows[1, c, pl.ds(g, 1), :]
            out[c, g, 8:16] = total[8:] + high_east * rows[0, c, pl.ds(g, 1), :]

    def some(i, carry):
        for k in range(16):
            one(i * 16 + k)
        return carry

    lax.fori_loop(0, size // 16, some, 0)


def remap_grains(velocity, fields, u_got, stress, s_got, y_got, relaxed, rows_even, rows_odd):
    n = relaxed.shape[1]
    size = 16
    small = (velocity, fields, *u_got, stress, *s_got, *y_got)
    return pl.pallas_call(
        functools.partial(remap_kernel, sizes()),
        grid=(n // size,),
        in_specs=[
            *[whole(*a.shape) for a in small],
            pl.BlockSpec(memory_space=pltpu.HBM),
            pl.BlockSpec((6, size, 128), lambda i: (0, i, 0)),
            pl.BlockSpec((6, size, 128), lambda i: (0, i, 0)),
        ],
        out_specs=[
            pl.BlockSpec((6, size, 16, 128), lambda i: (0, i, 0, 0)),
            whole(2, 16, 128),
        ],
        out_shape=[f32(*relaxed.shape), f32(2, 16, 128)],
        scratch_shapes=[
            pltpu.VMEM(relaxed.shape, jnp.float32),
            pltpu.VMEM((3, 24, 128), jnp.float32),
            pltpu.VMEM((2, 24, 128), jnp.float32),
            pltpu.VMEM((8, 16, 128), jnp.float32),
            pltpu.VMEM((2, 6, size, 128), jnp.float32),
            pltpu.VMEM((6, 16, 128), jnp.float32),
            pltpu.SemaphoreType.DMA((n // size,)),
        ],
        compiler_params=pltpu.CompilerParams(vmem_limit_bytes=53 * 2**20),
        cost_estimate=pl.CostEstimate(flops=10**7, bytes_accessed=10**7, transcendentals=0),
    )(*small, relaxed, rows_even, rows_odd)


def swap_even(block, axis):
    return lax.ppermute(block, axis, [(i, i ^ 1) for i in range(lax.axis_size(axis))])


def swap_odd_y(block):
    count_x, count_y = sizes()
    pairs = []
    for x in range(count_x):
        for y in range(count_y):
            end = y in (0, count_y - 1)
            to_x, to_y = (x ^ 1, y) if end else (x, y + 1 if y % 2 else y - 1)
            pairs.append((x * count_y + y, to_x * count_y + to_y))
    return lax.ppermute(block, ("gx", "gy"), pairs)


def swap_odd_x(block, crossed):
    count = lax.axis_size("gx")
    pairs = []
    for x in range(count):
        for a in range(2):
            end = x in (0, count - 1)
            to_x = x if end else (x + 1 if x % 2 else x - 1)
            to_a = 1 - a if end or crossed else a
            pairs.append((x * 2 + a, to_x * 2 + to_a))
    return lax.ppermute(block, ("gx", "ga"), pairs)


def per_device(velocity, density, grain_stress, grain_angles, hardness, active, donor_faces):
    gx = lax.axis_index("gx")
    odd_x = gx % 2 == 1
    u_got = (
        swap_even(velocity, "gx"),
        swap_odd_x(velocity, True),
        swap_even(velocity, "gy"),
        swap_odd_y(velocity),
    )
    relaxed, part, rows_even, rows_odd, cols_even, cols_odd = solve_grains(
        0.5 * velocity, u_got, grain_stress, grain_angles, hardness, active
    )
    density, donor_faces, part = lax.optimization_barrier((density, donor_faces, part))
    fields = jnp.concatenate([(1.0 / density)[None], donor_faces.astype(jnp.float32)], axis=0)
    zone_stress = (part + swap_even(part, "ga")) * (1.0 / G)
    zone_stress, rows_even, rows_odd = lax.optimization_barrier((zone_stress, rows_even, rows_odd))
    far_rows_odd = swap_odd_x(rows_odd, False)
    far_rows_even = swap_even(rows_even, "gx")
    spare = jnp.zeros((7, 128), jnp.float32)
    first = jnp.concatenate([zone_stress[:, :2].reshape(6, 128), fields[:, 0], spare], axis=0)
    last = jnp.concatenate([zone_stress[:, -2:].reshape(6, 128), fields[:, -1], spare], axis=0)
    got_even = swap_even(jnp.where(odd_x, first, last), "gx")
    got_odd = swap_odd_x(jnp.where(odd_x, last, first), True)
    east, west = from_sides(got_even[:6], got_odd[:6], gx, lax.axis_size("gx"))
    east, west = east.reshape(3, 2, 128), west.reshape(3, 2, 128)
    tall = jnp.concatenate([west[:, 1:], zone_stress, east[:, :1]], axis=1)
    lane = lax.broadcasted_iota(jnp.int32, (18, 128), 1)
    sides = jnp.zeros((18, 128), jnp.float32)
    for c in range(3):
        sides = jnp.where(lane // 4 == c, jnp.roll(tall[c], 4 * c + 2, axis=1), sides)
    sides = jnp.pad(sides, ((0, 6), (0, 0)))
    lane = lax.broadcasted_iota(jnp.int32, (16, 128), 1)
    field_sides = jnp.zeros((16, 128), jnp.float32)
    for k in range(3):
        field_sides = jnp.where(lane // 2 == 6 + k, jnp.roll(fields[k], 13 + 2 * k, axis=1), field_sides)
    sides = sides + jnp.pad(field_sides, ((0, 8), (0, 0)))
    y_got = (
        swap_even(jnp.concatenate([cols_even.reshape(48, 128), sides], axis=0), "gy"),
        swap_odd_y(jnp.concatenate([cols_odd.reshape(48, 128), sides], axis=0)),
    )
    stress_out, velocity_out = remap_grains(
        velocity, fields, u_got, zone_stress, (got_even, got_odd), y_got, relaxed, far_rows_even, far_rows_odd
    )
    return (velocity_out, stress_out, zone_stress)


def solution(mesh):
    return jax.shard_map(
        per_device,
        mesh=mesh,
        in_specs=(
            P(None, "gx", "gy"),
            P("gx", "gy"),
            P(None, "ga", "gx", "gy"),
            P(None, "ga", "gx", "gy"),
            P("ga", "gx", "gy"),
            P(None, "ga", "gx", "gy"),
            P(None, "gx", "gy"),
        ),
        out_specs=(P(None, "gx", "gy"), P(None, "ga", "gx", "gy"), P(None, "gx", "gy")),
        check_vma=False,
    )
```

```python
import functools
import math

import jax
import jax.numpy as jnp
import numpy as np
from jax import lax
from jax.experimental import pallas as pl
from jax.experimental.pallas import tpu as pltpu
from jax.sharding import PartitionSpec as P

G = 128
ITERS = 4

time_step = 0.1
lame_first = 1.5
batch = 4
grain_block = 2 * batch
system_list = (
    ((0, 1, 1), (1, 1, -1)),
    ((0, 1, 1), (1, -1, 1)),
    ((1, 0, 1), (1, 1, -1)),
    ((1, 0, 1), (-1, 1, 1)),
    ((1, 1, 0), (1, -1, 1)),
    ((1, 1, 0), (-1, 1, 1)),
    ((0, 1, -1), (1, 1, 1)),
    ((0, 1, -1), (1, -1, -1)),
    ((1, 0, -1), (1, 1, 1)),
    ((1, 0, -1), (1, -1, 1)),
    ((1, -1, 0), (1, 1, 1)),
    ((1, -1, 0), (1, 1, -1)),
    ((1, 1, 2), (1, 1, -1)),
    ((1, 1, -2), (1, 1, 1)),
    ((1, -1, 2), (1, -1, -1)),
    ((-1, 1, 2), (-1, 1, -1)),
    ((1, 2, 1), (1, -1, 1)),
    ((1, -2, 1), (1, 1, 1)),
    ((-1, 2, 1), (1, 1, -1)),
    ((1, 2, -1), (-1, 1, 1)),
    ((2, 1, 1), (-1, 1, 1)),
    ((-2, 1, 1), (1, 1, 1)),
    ((2, -1, 1), (1, 1, -1)),
    ((2, 1, -1), (1, -1, 1)),
)
upper_pairs = [(i, j) for i in range(5) for j in range(i, 5)]
n_sums = 26


def slip_sums_table():
    table = np.zeros((n_sums, 24))
    for s, (normal, direction) in enumerate(system_list):
        q = np.outer(direction, normal) + np.outer(normal, direction)
        k = np.array([(q[0, 0] - q[1, 1]) / 2, -q[2, 2] / 2, q[1, 2], q[0, 2], q[0, 1]])
        weight = 3 if s < 12 else 1
        for e, (i, j) in enumerate(upper_pairs):
            table[e, s] = weight * k[i] * k[j] * (3 if i == j == 1 else 1)
        first = 15 if s < 12 else 20
        table[first : first + 5, s] = k
        table[25, s] = 1
    columns = np.zeros((n_sums, 24))
    for s in range(24):
        word, bit = divmod(s, 12)
        columns[:, 2 * bit + word] = table[:, s]
    return columns


def fill_table(table):
    columns = slip_sums_table()
    lane = lax.broadcasted_iota(jnp.int32, (8, 192), 1)
    own = lane % 8 == lax.broadcasted_iota(jnp.int32, (8, 192), 0)
    system = lane // 8
    for e in range(n_sums):
        entry = jnp.zeros((8, 192), jnp.float32)
        for k in range(24):
            if columns[e, k]:
                entry = jnp.where(system == k, float(columns[e, k]), entry)
        table[8 * e : 8 * e + 8] = jnp.where(own, entry, 0.0)


def fitted(function, degree, top):
    series = np.polynomial.chebyshev.Chebyshev.interpolate(function, degree, domain=[0.0, top])
    return [float(c) for c in series.convert(kind=np.polynomial.Polynomial).coef]


angle_top = 3.1416**2
sin_half = fitted(lambda t: math.sqrt(2) * np.sin(np.sqrt(t) / 2) / np.sqrt(t), 4, angle_top)
cos_half = fitted(lambda t: math.sqrt(2) * np.cos(np.sqrt(t) / 2), 4, angle_top)


def polynomial(t, coefs):
    total = coefs[-1] * t + coefs[-2]
    for c in coefs[-3::-1]:
        total = total * t + c
    return total


def sin_cos(x):
    t = x * x
    s = x * polynomial(t, sin_half)
    c = polynomial(t, cos_half)
    return s * c, 1.0 - s * s


def grain_math(stress, angles, hardness, sums, strain):
    exx, eyy, exy, trace, hydro = strain
    s1, c1 = sin_cos(angles[0])
    sq, cq = sin_cos(angles[1])
    s2, c2 = sin_cos(angles[2])
    c1c2, s1s2, c1s2, s1c2 = c1 * c2, s1 * s2, c1 * s2, s1 * c2
    r00 = c1c2 - s1s2 * cq
    r01 = -(c1s2 + s1c2 * cq)
    r02 = s1 * sq
    r10 = s1c2 + c1s2 * cq
    r11 = c1c2 * cq - s1s2
    r12 = -(c1 * sq)
    a0, b0 = r00 * exx + r10 * exy, r10 * eyy + r00 * exy
    a1, b1 = r01 * exx + r11 * exy, r11 * eyy + r01 * exy
    d00 = r00 * a0 + r10 * b0
    d11 = r01 * a1 + r11 * b1
    t00, t11 = stress[0] + d00, stress[1] + d11
    t22 = stress[2] + (trace - (d00 + d11))
    t_sum = t00 + t11
    v = [
        (t00 - t11) * 0.5,
        t_sum * (1 / math.sqrt(12)) - t22 * (2 / math.sqrt(12)),
        stress[3] + (r02 * a1 + r12 * b1),
        stress[4] + (r02 * a0 + r12 * b0),
        stress[5] + (r01 * a0 + r11 * b0),
    ]
    pressure = (t_sum + t22) * (1.0 / 3.0) + hydro
    step = 1.0 / (1.0 + sums(25))
    h0 = hardness * step * (1 / math.sqrt(2))
    h1 = h0 * (1 / math.sqrt(3))
    h2 = h0 * (1.0 / 3.0)
    bias = []
    for i in range(5):
        first, second = (h0, h1) if i == 1 else (h1, h2)
        bias.append(sums(15 + i) * first + sums(20 + i) * second)
    plain, mixed = step * (1 / 18.0), step * (math.sqrt(3) / 18.0)
    m = {}
    for e, (i, j) in enumerate(upper_pairs):
        entry = sums(e) * (mixed if (i == 1) != (j == 1) else plain)
        m[i, j] = m[j, i] = (1.0 - entry) if i == j else entry
    for _ in range(ITERS):
        fresh = []
        for i in range(5):
            off = None
            for j in range(5):
                if j != i:
                    term = m[i, j] * v[j]
                    off = term if off is None else off + term
            fresh.append((m[i, i] * v[i] + bias[i]) - off)
        v = fresh
    w = v[1] * (1 / math.sqrt(3))
    mid = pressure + w
    x = [mid + v[0], mid - v[0], pressure - 2.0 * w, v[2], v[3], v[4]]
    f0 = x[0] * r00 + x[5] * r01 + x[4] * r02
    f1 = x[5] * r00 + x[1] * r01 + x[3] * r02
    f2 = x[4] * r00 + x[3] * r01 + x[2] * r02
    g0 = x[0] * r10 + x[5] * r11 + x[4] * r12
    g1 = x[5] * r10 + x[1] * r11 + x[3] * r12
    g2 = x[4] * r10 + x[3] * r11 + x[2] * r12
    sample = (
        r00 * f0 + r01 * f1 + r02 * f2,
        r10 * g0 + r11 * g1 + r12 * g2,
        r00 * g0 + r01 * g1 + r02 * g2,
    )
    return x, sample


def bit_rows(words):
    pieces = [jnp.concatenate([w[:8], w[8:]], axis=1) for w in words]
    both = jnp.concatenate(pieces, axis=0).astype(jnp.int16)
    one, none = jnp.bfloat16(1.0), jnp.bfloat16(0.0)
    rows = [jnp.where((both & jnp.int16(1 << bit)) != 0, one, none) for bit in range(12)]
    return jnp.concatenate(rows, axis=0)


def places():
    return lax.axis_index("gx"), lax.axis_index("gy")


def sizes():
    return lax.axis_size("gx"), lax.axis_size("gy")


def whole(*shape):
    return pl.BlockSpec(shape, lambda *i: (0,) * len(shape))


def f32(*shape):
    return jax.ShapeDtypeStruct(shape, jnp.float32)


def lane_ids(rows):
    return lax.broadcasted_iota(jnp.int32, (rows, 128), 1)


def row_ids():
    return lax.broadcasted_iota(jnp.int32, (16, 128), 0)


def from_sides(got_even, got_odd, index, count):
    odd = index % 2 == 1
    after = jnp.where(odd, got_odd, got_even)
    before = jnp.where(odd, got_even, got_odd)
    return jnp.where(index == count - 1, 0.0, after), jnp.where(index == 0, 0.0, before)


def shifts_x(field, east, west):
    row = row_ids()
    return (
        jnp.where(row == 15, east, pltpu.roll(field, 15, 0)),
        jnp.where(row == 0, west, pltpu.roll(field, 1, 0)),
    )


def shifts_y(field, halo):
    lane = lane_ids(field.shape[0])
    return (
        jnp.where(lane == 127, halo, pltpu.roll(field, 127, 1)),
        jnp.where(lane == 0, halo, pltpu.roll(field, 1, 1)),
    )


def side_columns(after, before, first, last):
    lane = lane_ids(after.shape[0])
    return jnp.where(
        lane == 127,
        pltpu.roll(after, 127 - first, 1),
        jnp.where(lane == 0, pltpu.roll(before, (128 - last) % 128, 1), 0.0),
    )


def velocity_halo(counts, got):
    gx, gy = places()
    after_x, before_x = from_sides(got[0], got[1], gx, counts[0])
    after_y, before_y = from_sides(got[2], got[3], gy, counts[1])
    return after_x[0:1], before_x[15:16], side_columns(after_y, before_y, 0, 127)


def solve_kernel(
    counts, half_velocity, x_even, x_odd, y_even, y_odd, stress_in, angles_in, hardness_in, active_in,
    relaxed_out, zone_sum, rows_even, rows_odd, cols_even, cols_odd,
    relaxed, stress, angles, hardness, active, table_wide, table, sums_a, sums_b, strain, cols, sems, out_sems,
):
    blocks = hardness.shape[0] // grain_block
    gx, gy = places()

    def copies(i, kinds):
        part = pl.ds(i * grain_block, grain_block)
        every = (
            lambda: (active_in.at[:, part], active.at[:, part]),
            lambda: (stress_in.at[:, part], stress.at[:, part]),
            lambda: (angles_in.at[:, part], angles.at[:, part]),
            lambda: (hardness_in.at[part], hardness.at[part]),
        )
        return [pltpu.make_async_copy(*every[k](), sems.at[k, i]) for k in kinds]

    def out_copy(i):
        part = pl.ds(i * grain_block, grain_block)
        return pltpu.make_async_copy(relaxed.at[0:6, part], relaxed_out.at[:, part], out_sems.at[i])

    def count(group, sums):
        first = group * batch
        bits = [bit_rows([active[0, first + k], active[1, first + k]]) for k in range(batch)]
        sums[...] = jnp.dot(
            table[...], jnp.concatenate(bits, axis=1), preferred_element_type=jnp.float32
        )

    def update(group, sums):
        lane = lane_ids(8)
        for half in range(2):
            part = pl.ds(8 * half, 8)
            zone_strain = [strain[i, part] for i in range(5)]
            totals = [zone_sum[k, part] for k in range(3)]
            ends = [cols[c, part] for c in range(6)]
            for k in range(batch):
                g = group * batch + k
                lanes = slice(256 * k + 128 * half, 256 * k + 128 * half + 128)
                x, sample = grain_math(
                    [stress[c, g, part] for c in range(6)],
                    [angles[c, g, part] for c in range(3)],
                    hardness[g, part],
                    lambda e: sums[e * 8 : (e + 1) * 8, lanes],
                    zone_strain,
                )
                here = (lane == 2 * g) | (lane == 2 * g + 1)
                for c in range(6):
                    relaxed[c, g, part] = x[c]
                    ends[c] = jnp.where(here, pltpu.roll(x[c], 2 * g + 1, 1), ends[c])
                totals = [t + s for t, s in zip(totals, sample)]
            for k in range(3):
                zone_sum[k, part] = totals[k]
            for c in range(6):
                cols[c, part] = ends[c]

    for copy in copies(0, range(4)):
        copy.start()
    for copy in copies(1, range(4)):
        copy.start()
    fill_table(table_wide)
    table[...] = table_wide[...].astype(jnp.bfloat16)
    zone_sum[...] = jnp.zeros_like(zone_sum)
    cols[...] = jnp.zeros_like(cols)
    grads = []
    for k in range(2):
        u = half_velocity[k]
        east, west, halo = velocity_halo(counts, (x_even[k], x_odd[k], y_even[k], y_odd[k]))
        u_east, u_west = shifts_x(u, 0.5 * east, 0.5 * west)
        u_north, u_south = shifts_y(u, 0.5 * halo)
        grads.append((u_east - u_west, u_north - u_south))
    exx, eyy = grads[0][0], grads[1][1]
    exy = 0.5 * (grads[0][1] + grads[1][0])
    strain[0] = 2.0 * time_step * exx
    strain[1] = 2.0 * time_step * eyy
    strain[2] = 2.0 * time_step * exy
    strain[3] = 2.0 * time_step * (exx + eyy)
    strain[4] = lame_first * time_step * (exx + eyy)
    for i in range(2, blocks):
        for copy in copies(i, range(4)):
            copy.start()
    copies(0, [0])[0].wait()
    count(0, sums_a)

    def step(block, carry):
        for copy in copies(block, [1, 2, 3]):
            copy.wait()

        @pl.when(block < blocks - 1)
        def _():
            copies(block + 1, [0])[0].wait()

        group = block * 2
        count(group + 1, sums_b)
        update(group, sums_a)
        count(jnp.minimum(group + 2, blocks * 2 - 1), sums_a)
        update(group + 1, sums_b)
        out_copy(block).start()
        return carry

    lax.fori_loop(0, blocks, step, 0)

    n = relaxed.shape[1]
    flat = relaxed.reshape(7 * n * 16, 128)
    odd_x, odd_y = gx % 2 == 1, gy % 2 == 1
    for c in range(6):
        first = flat[pl.ds(c * n * 16, n, stride=16)]
        last = flat[pl.ds(c * n * 16 + 15, n, stride=16)]
        rows_even[c] = jnp.where(odd_x, first, last)
        rows_odd[c] = jnp.where(odd_x, last, first)
    low = lane_ids(16) % 2 == 0
    for c in range(3):
        one, other = cols[c], cols[c + 3]
        last = jnp.where(low, one, pltpu.roll(other, 1, 1))
        first = jnp.where(low, pltpu.roll(one, 127, 1), other)
        cols_even[c] = jnp.where(odd_y, first, last)
        cols_odd[c] = jnp.where(odd_y, last, first)
    for i in range(blocks):
        out_copy(i).wait()


def solve_grains(half_velocity, got, stress, angles, hardness, active):
    n = hardness.shape[0]
    in_hbm = pl.BlockSpec(memory_space=pltpu.HBM)
    return pl.pallas_call(
        functools.partial(solve_kernel, sizes()),
        grid=(1,),
        in_specs=[
            whole(2, 16, 128),
            *[whole(*g.shape) for g in got],
            *[in_hbm] * 4,
        ],
        out_specs=[
            in_hbm,
            whole(3, 16, 128),
            whole(6, n, 128),
            whole(6, n, 128),
            whole(3, 16, 128),
            whole(3, 16, 128),
        ],
        out_shape=[f32(6, n, 16, 128), f32(3, 16, 128), f32(6, n, 128), f32(6, n, 128)]
        + [f32(3, 16, 128)] * 2,
        scratch_shapes=[
            pltpu.VMEM((7, n, 16, 128), jnp.float32),
            pltpu.VMEM(stress.shape, jnp.float32),
            pltpu.VMEM(angles.shape, jnp.float32),
            pltpu.VMEM(hardness.shape, jnp.float32),
            pltpu.VMEM(active.shape, jnp.int32),
            pltpu.VMEM((8 * n_sums, 192), jnp.float32),
            pltpu.VMEM((8 * n_sums, 192), jnp.bfloat16),
            pltpu.VMEM((8 * n_sums, 256 * batch), jnp.float32),
            pltpu.VMEM((8 * n_sums, 256 * batch), jnp.float32),
            pltpu.VMEM((5, 16, 128), jnp.float32),
            pltpu.VMEM((6, 16, 128), jnp.float32),
            pltpu.SemaphoreType.DMA((4, n // grain_block)),
            pltpu.SemaphoreType.DMA((n // grain_block,)),
        ],
        compiler_params=pltpu.CompilerParams(vmem_limit_bytes=53 * 2**20),
        cost_estimate=pl.CostEstimate(flops=10**8, bytes_accessed=10**7, transcendentals=0),
    )(half_velocity, *got, stress, angles, hardness, active)


def zone_update(counts, velocity, fields, u_got, stress, s_got, tall, moved, velocity_out):
    gx, gy = places()
    sx_even, sx_odd, sy_even, sy_odd = s_got
    s_east, s_west = from_sides(sx_even, sx_odd, gx, counts[0])
    s_north, s_south = from_sides(sy_even, sy_odd, gy, counts[1])
    for c in range(3):
        tall[c, 0:2] = s_west[2 * c : 2 * c + 2]
        tall[c, 2:18] = stress[c]
        tall[c, 18:20] = s_east[2 * c : 2 * c + 2]
    near = [side_columns(s_north, s_south, 4 * c + 2, 4 * c + 1) for c in range(3)]
    far = [side_columns(s_north, s_south, 4 * c + 3, 4 * c) for c in range(3)]
    lane = lane_ids(16)
    sign = jnp.where(lane == 127, 0.5, -0.5)

    def x_diff(c):
        return (tall[c, 2:20] - tall[c, 0:18]) * 0.5

    def y_diff(c):
        after, before = shifts_y(tall[c, 1:19], near[c][:18])
        return (after - before) * 0.5

    def rim_x(c):
        return (near[c][2:18] - near[c][0:16]) * 0.5

    def rim_y(c):
        return (far[c][1:17] - stress[c]) * sign

    force = [x_diff(0) + y_diff(2), x_diff(2) + y_diff(1)]
    rim_force = [rim_x(0) + rim_y(2), rim_x(2) + rim_y(1)]
    field_rim = [
        side_columns(s_north[:16], s_south[:16], 13 + 2 * k, 12 + 2 * k) for k in range(3)
    ]
    sides = [velocity_halo(counts, [got[k] for got in u_got]) for k in range(2)]

    def high(k):
        return jnp.concatenate([s_west[6 + k : 7 + k], fields[k], s_east[6 + k : 7 + k]], axis=0)

    mass = time_step * high(0)
    rim = []
    for k in range(2):
        east, west, halo = sides[k]
        moved[k, 0:18] = jnp.concatenate([west, velocity[k], east], axis=0) + mass * force[k]
        rim.append(halo + time_step * field_rim[0] * rim_force[k])
    frac_x = time_step * 0.5 * (moved[0, 0:17] + moved[0, 1:18])
    x_self = frac_x * high(1)[:17]
    x_next = frac_x - x_self
    own = [moved[k, 1:17] for k in range(2)]
    y_sides = [shifts_y(own[k], rim[k]) for k in range(2)]
    frac_y = time_step * 0.5 * (own[1] + y_sides[1][0])
    frac_before = time_step * 0.5 * (own[1] + y_sides[1][1])
    flag = fields[2]
    flag_before = jnp.where(lane == 0, field_rim[2], pltpu.roll(flag, 1, 1))
    y_self, before_self = frac_y * flag, frac_before * flag_before
    y_next, before_next = frac_y - y_self, frac_before - before_self
    centre = 1.0 - x_self[1:17] + x_next[0:16] - y_self + before_next
    coefs = (centre, -x_next[1:17], x_self[0:16], -y_next, before_self)
    for k in range(2):
        velocity_out[k] = (
            centre * own[k]
            + coefs[1] * moved[k, 2:18]
            + coefs[2] * moved[k, 0:16]
            + coefs[3] * y_sides[k][0]
            + coefs[4] * y_sides[k][1]
        )
    return coefs


def remap_kernel(
    counts, velocity, fields, ux_even, ux_odd, uy_even, uy_odd, stress, sx_even, sx_odd, y_even, y_odd,
    relaxed_in, rows_even, rows_odd,
    out, velocity_out, relaxed, tall, moved, coefs, rows, cols, sems,
):
    block = pl.program_id(0)
    size = out.shape[1]
    gx, gy = places()
    odd_x = gx % 2 == 1

    def copy(i):
        part = pl.ds(i * size, size)
        return pltpu.make_async_copy(relaxed_in.at[:, part], relaxed.at[:, part], sems.at[i])

    @pl.when(block == 0)
    def _():
        for i in range(relaxed.shape[1] // size):
            copy(i).start()

    rows[0, :, :size] = jnp.where(odd_x, rows_odd[...], rows_even[...])
    rows[1, :, :size] = jnp.where(odd_x, rows_even[...], rows_odd[...])
    lane, row = lane_ids(16), row_ids()

    @pl.when(block == 0)
    def _():
        fresh = zone_update(
            counts,
            velocity,
            fields,
            (ux_even, ux_odd, uy_even, uy_odd),
            stress,
            (sx_even[...], sx_odd[...], y_even[48:72], y_odd[48:72]),
            tall,
            moved,
            velocity_out,
        )
        centre, east, west, north, south = fresh
        coefs[0] = centre
        coefs[1] = jnp.where(row == 15, 0.0, east)
        coefs[2] = jnp.where(row == 0, 0.0, west)
        coefs[3] = jnp.where(lane == 127, 0.0, north)
        coefs[4] = jnp.where(lane == 0, 0.0, south)
        coefs[5] = jnp.where((row == 15) & (gx < counts[0] - 1), east, 0.0)
        coefs[6] = jnp.where((row == 0) & (gx > 0), west, 0.0)
        rim = jnp.where((lane == 127) & (gy < counts[1] - 1), north, 0.0)
        coefs[7] = jnp.where((lane == 0) & (gy > 0), south, rim)
        odd_y = gy % 2 == 1
        for c in range(3):
            part = slice(16 * c, 16 * c + 16)
            got_even, got_odd = y_even[part], y_odd[part]
            after = jnp.where(odd_y, got_odd, got_even)
            before = jnp.where(odd_y, got_even, got_odd)
            cols[c] = jnp.where(lane % 2 == 0, after, pltpu.roll(before, 1, 1))
            cols[c + 3] = jnp.where(lane % 2 == 0, pltpu.roll(after, 127, 1), before)

    centre, east, west, north, south, _, _, rim = [coefs[i] for i in range(8)]
    high_east, low_west = coefs[5, 8:16], coefs[6, 0:8]
    copy(block).wait()

    def one(g):
        for c in range(6):
            q = relaxed[c, block * size + g]
            halo = pltpu.roll(cols[c], 127 - 2 * (block * size + g), 1)
            total = centre * q + north * pltpu.roll(q, 127, 1) + south * pltpu.roll(q, 1, 1)
            total = total + rim * halo
            total = total + east * pltpu.roll(q, 15, 0) + west * pltpu.roll(q, 1, 0)
            out[c, g, 0:8] = total[:8] + low_west * rows[1, c, pl.ds(g, 1), :]
            out[c, g, 8:16] = total[8:] + high_east * rows[0, c, pl.ds(g, 1), :]

    def some(i, carry):
        for k in range(16):
            one(i * 16 + k)
        return carry

    lax.fori_loop(0, size // 16, some, 0)


def remap_grains(velocity, fields, u_got, stress, s_got, y_got, relaxed, rows_even, rows_odd):
    n = relaxed.shape[1]
    size = 16
    small = (velocity, fields, *u_got, stress, *s_got, *y_got)
    return pl.pallas_call(
        functools.partial(remap_kernel, sizes()),
        grid=(n // size,),
        in_specs=[
            *[whole(*a.shape) for a in small],
            pl.BlockSpec(memory_space=pltpu.HBM),
            pl.BlockSpec((6, size, 128), lambda i: (0, i, 0)),
            pl.BlockSpec((6, size, 128), lambda i: (0, i, 0)),
        ],
        out_specs=[
            pl.BlockSpec((6, size, 16, 128), lambda i: (0, i, 0, 0)),
            whole(2, 16, 128),
        ],
        out_shape=[f32(*relaxed.shape), f32(2, 16, 128)],
        scratch_shapes=[
            pltpu.VMEM(relaxed.shape, jnp.float32),
            pltpu.VMEM((3, 32, 128), jnp.float32),
            pltpu.VMEM((2, 32, 128), jnp.float32),
            pltpu.VMEM((8, 16, 128), jnp.float32),
            pltpu.VMEM((2, 6, size + 8, 128), jnp.float32),
            pltpu.VMEM((6, 16, 128), jnp.float32),
            pltpu.SemaphoreType.DMA((n // size,)),
        ],
        compiler_params=pltpu.CompilerParams(vmem_limit_bytes=53 * 2**20),
        cost_estimate=pl.CostEstimate(flops=10**7, bytes_accessed=10**7, transcendentals=0),
    )(*small, relaxed, rows_even, rows_odd)


def swap_even(block, axis):
    return lax.ppermute(block, axis, [(i, i ^ 1) for i in range(lax.axis_size(axis))])


def swap_odd_y(block):
    count_x, count_y = sizes()
    pairs = []
    for x in range(count_x):
        for y in range(count_y):
            end = y in (0, count_y - 1)
            to_x, to_y = (x ^ 1, y) if end else (x, y + 1 if y % 2 else y - 1)
            pairs.append((x * count_y + y, to_x * count_y + to_y))
    return lax.ppermute(block, ("gx", "gy"), pairs)


def swap_odd_x(block, crossed):
    count = lax.axis_size("gx")
    pairs = []
    for x in range(count):
        for a in range(2):
            end = x in (0, count - 1)
            to_x = x if end else (x + 1 if x % 2 else x - 1)
            to_a = 1 - a if end or crossed else a
            pairs.append((x * 2 + a, to_x * 2 + to_a))
    return lax.ppermute(block, ("gx", "ga"), pairs)


def per_device(velocity, density, grain_stress, grain_angles, hardness, active, donor_faces):
    gx = lax.axis_index("gx")
    odd_x = gx % 2 == 1
    u_got = (
        swap_even(velocity, "gx"),
        swap_odd_x(velocity, True),
        swap_even(velocity, "gy"),
        swap_odd_y(velocity),
    )
    relaxed, part, rows_even, rows_odd, cols_even, cols_odd = solve_grains(
        0.5 * velocity, u_got, grain_stress, grain_angles, hardness, active
    )
    density, donor_faces, part = lax.optimization_barrier((density, donor_faces, part))
    fields = jnp.concatenate([(1.0 / density)[None], donor_faces.astype(jnp.float32)], axis=0)
    zone_stress = (part + swap_even(part, "ga")) * (1.0 / G)
    zone_stress, rows_even, rows_odd = lax.optimization_barrier((zone_stress, rows_even, rows_odd))
    far_rows_odd = swap_odd_x(rows_odd, False)
    far_rows_even = swap_even(rows_even, "gx")
    spare = jnp.zeros((7, 128), jnp.float32)
    first = jnp.concatenate([zone_stress[:, :2].reshape(6, 128), fields[:, 0], spare], axis=0)
    last = jnp.concatenate([zone_stress[:, -2:].reshape(6, 128), fields[:, -1], spare], axis=0)
    got_even = swap_even(jnp.where(odd_x, first, last), "gx")
    got_odd = swap_odd_x(jnp.where(odd_x, last, first), True)
    east, west = from_sides(got_even[:6], got_odd[:6], gx, lax.axis_size("gx"))
    east, west = east.reshape(3, 2, 128), west.reshape(3, 2, 128)
    tall = jnp.concatenate([west[:, 1:], zone_stress, east[:, :1]], axis=1)
    lane = lax.broadcasted_iota(jnp.int32, (18, 128), 1)
    sides = jnp.zeros((18, 128), jnp.float32)
    for c in range(3):
        sides = jnp.where(lane // 4 == c, jnp.roll(tall[c], 4 * c + 2, axis=1), sides)
    sides = jnp.pad(sides, ((0, 6), (0, 0)))
    lane = lax.broadcasted_iota(jnp.int32, (16, 128), 1)
    field_sides = jnp.zeros((16, 128), jnp.float32)
    for k in range(3):
        field_sides = jnp.where(lane // 2 == 6 + k, jnp.roll(fields[k], 13 + 2 * k, axis=1), field_sides)
    sides = sides + jnp.pad(field_sides, ((0, 8), (0, 0)))
    y_got = (
        swap_even(jnp.concatenate([cols_even.reshape(48, 128), sides], axis=0), "gy"),
        swap_odd_y(jnp.concatenate([cols_odd.reshape(48, 128), sides], axis=0)),
    )
    stress_out, velocity_out = remap_grains(
        velocity, fields, u_got, zone_stress, (got_even, got_odd), y_got, relaxed, far_rows_even, far_rows_odd
    )
    return (velocity_out, stress_out, zone_stress)


def solution(mesh):
    return jax.shard_map(
        per_device,
        mesh=mesh,
        in_specs=(
            P(None, "gx", "gy"),
            P("gx", "gy"),
            P(None, "ga", "gx", "gy"),
            P(None, "ga", "gx", "gy"),
            P("ga", "gx", "gy"),
            P(None, "ga", "gx", "gy"),
            P(None, "gx", "gy"),
        ),
        out_specs=(P(None, "gx", "gy"), P(None, "ga", "gx", "gy"), P(None, "gx", "gy")),
        check_vma=False,
    )
```

```python
import functools
import math

import jax
import jax.numpy as jnp
import numpy as np
from jax import lax
from jax.experimental import pallas as pl
from jax.experimental.pallas import tpu as pltpu
from jax.sharding import PartitionSpec as P

G = 128
ITERS = 4

time_step = 0.1
lame_first = 1.5
batch = 4
grain_block = 2 * batch
system_list = (
    ((0, 1, 1), (1, 1, -1)),
    ((0, 1, 1), (1, -1, 1)),
    ((1, 0, 1), (1, 1, -1)),
    ((1, 0, 1), (-1, 1, 1)),
    ((1, 1, 0), (1, -1, 1)),
    ((1, 1, 0), (-1, 1, 1)),
    ((0, 1, -1), (1, 1, 1)),
    ((0, 1, -1), (1, -1, -1)),
    ((1, 0, -1), (1, 1, 1)),
    ((1, 0, -1), (1, -1, 1)),
    ((1, -1, 0), (1, 1, 1)),
    ((1, -1, 0), (1, 1, -1)),
    ((1, 1, 2), (1, 1, -1)),
    ((1, 1, -2), (1, 1, 1)),
    ((1, -1, 2), (1, -1, -1)),
    ((-1, 1, 2), (-1, 1, -1)),
    ((1, 2, 1), (1, -1, 1)),
    ((1, -2, 1), (1, 1, 1)),
    ((-1, 2, 1), (1, 1, -1)),
    ((1, 2, -1), (-1, 1, 1)),
    ((2, 1, 1), (-1, 1, 1)),
    ((-2, 1, 1), (1, 1, 1)),
    ((2, -1, 1), (1, 1, -1)),
    ((2, 1, -1), (1, -1, 1)),
)
upper_pairs = [(i, j) for i in range(5) for j in range(i, 5)]
n_sums = 26


def slip_sums_table():
    table = np.zeros((n_sums, 24))
    for s, (normal, direction) in enumerate(system_list):
        q = np.outer(direction, normal) + np.outer(normal, direction)
        k = np.array([(q[0, 0] - q[1, 1]) / 2, -q[2, 2] / 2, q[1, 2], q[0, 2], q[0, 1]])
        weight = 3 if s < 12 else 1
        for e, (i, j) in enumerate(upper_pairs):
            table[e, s] = weight * k[i] * k[j] * (3 if i == j == 1 else 1)
        first = 15 if s < 12 else 20
        table[first : first + 5, s] = k
        table[25, s] = 1
    columns = np.zeros((n_sums, 24))
    for s in range(24):
        word, bit = divmod(s, 12)
        columns[:, 2 * bit + word] = table[:, s]
    return columns


def fill_table(table):
    columns = slip_sums_table()
    lane = lax.broadcasted_iota(jnp.int32, (8, 192), 1)
    own = lane % 8 == lax.broadcasted_iota(jnp.int32, (8, 192), 0)
    system = lane // 8
    for e in range(n_sums):
        entry = jnp.zeros((8, 192), jnp.float32)
        for k in range(24):
            if columns[e, k]:
                entry = jnp.where(system == k, float(columns[e, k]), entry)
        table[8 * e : 8 * e + 8] = jnp.where(own, entry, 0.0)


def fitted(function, degree, top):
    series = np.polynomial.chebyshev.Chebyshev.interpolate(function, degree, domain=[0.0, top])
    return [float(c) for c in series.convert(kind=np.polynomial.Polynomial).coef]


angle_top = 3.1416**2
sin_half = fitted(lambda t: math.sqrt(2) * np.sin(np.sqrt(t) / 2) / np.sqrt(t), 4, angle_top)
cos_half = fitted(lambda t: math.sqrt(2) * np.cos(np.sqrt(t) / 2), 4, angle_top)


def polynomial(t, coefs):
    total = coefs[-1] * t + coefs[-2]
    for c in coefs[-3::-1]:
        total = total * t + c
    return total


def sin_cos(x):
    t = x * x
    s = x * polynomial(t, sin_half)
    c = polynomial(t, cos_half)
    return s * c, 1.0 - s * s


def grain_math(stress, angles, hardness, sums, strain):
    exx, eyy, exy, trace, hydro = strain
    s1, c1 = sin_cos(angles[0])
    sq, cq = sin_cos(angles[1])
    s2, c2 = sin_cos(angles[2])
    c1c2, s1s2, c1s2, s1c2 = c1 * c2, s1 * s2, c1 * s2, s1 * c2
    r00 = c1c2 - s1s2 * cq
    r01 = -(c1s2 + s1c2 * cq)
    r02 = s1 * sq
    r10 = s1c2 + c1s2 * cq
    r11 = c1c2 * cq - s1s2
    r12 = -(c1 * sq)
    a0, b0 = r00 * exx + r10 * exy, r10 * eyy + r00 * exy
    a1, b1 = r01 * exx + r11 * exy, r11 * eyy + r01 * exy
    d00 = r00 * a0 + r10 * b0
    d11 = r01 * a1 + r11 * b1
    t00, t11 = stress[0] + d00, stress[1] + d11
    t22 = stress[2] + (trace - (d00 + d11))
    t_sum = t00 + t11
    v = [
        (t00 - t11) * 0.5,
        t_sum * (1 / math.sqrt(12)) - t22 * (2 / math.sqrt(12)),
        stress[3] + (r02 * a1 + r12 * b1),
        stress[4] + (r02 * a0 + r12 * b0),
        stress[5] + (r01 * a0 + r11 * b0),
    ]
    pressure = (t_sum + t22) * (1.0 / 3.0) + hydro
    step = 1.0 / (1.0 + sums(25))
    h0 = hardness * step * (1 / math.sqrt(2))
    h1 = h0 * (1 / math.sqrt(3))
    h2 = h0 * (1.0 / 3.0)
    bias = []
    for i in range(5):
        first, second = (h0, h1) if i == 1 else (h1, h2)
        bias.append(sums(15 + i) * first + sums(20 + i) * second)
    plain, mixed = step * (1 / 18.0), step * (math.sqrt(3) / 18.0)
    m = {}
    for e, (i, j) in enumerate(upper_pairs):
        entry = sums(e) * (mixed if (i == 1) != (j == 1) else plain)
        m[i, j] = m[j, i] = (1.0 - entry) if i == j else entry
    for _ in range(ITERS):
        fresh = []
        for i in range(5):
            off = None
            for j in range(5):
                if j != i:
                    term = m[i, j] * v[j]
                    off = term if off is None else off + term
            fresh.append((m[i, i] * v[i] + bias[i]) - off)
        v = fresh
    w = v[1] * (1 / math.sqrt(3))
    mid = pressure + w
    x = [mid + v[0], mid - v[0], pressure - 2.0 * w, v[2], v[3], v[4]]
    f0 = x[0] * r00 + x[5] * r01 + x[4] * r02
    f1 = x[5] * r00 + x[1] * r01 + x[3] * r02
    f2 = x[4] * r00 + x[3] * r01 + x[2] * r02
    g0 = x[0] * r10 + x[5] * r11 + x[4] * r12
    g1 = x[5] * r10 + x[1] * r11 + x[3] * r12
    g2 = x[4] * r10 + x[3] * r11 + x[2] * r12
    sample = (
        r00 * f0 + r01 * f1 + r02 * f2,
        r10 * g0 + r11 * g1 + r12 * g2,
        r00 * g0 + r01 * g1 + r02 * g2,
    )
    return x, sample


def bit_rows(words):
    pieces = [jnp.concatenate([w[:8], w[8:]], axis=1) for w in words]
    both = jnp.concatenate(pieces, axis=0).astype(jnp.int16)
    one, none = jnp.bfloat16(1.0), jnp.bfloat16(0.0)
    rows = [jnp.where((both & jnp.int16(1 << bit)) != 0, one, none) for bit in range(12)]
    return jnp.concatenate(rows, axis=0)


def places():
    return lax.axis_index("gx"), lax.axis_index("gy")


def sizes():
    return lax.axis_size("gx"), lax.axis_size("gy")


def whole(*shape):
    return pl.BlockSpec(shape, lambda *i: (0,) * len(shape))


def f32(*shape):
    return jax.ShapeDtypeStruct(shape, jnp.float32)


def lane_ids(rows):
    return lax.broadcasted_iota(jnp.int32, (rows, 128), 1)


def row_ids():
    return lax.broadcasted_iota(jnp.int32, (16, 128), 0)


def from_sides(got_even, got_odd, index, count):
    odd = index % 2 == 1
    after = jnp.where(odd, got_odd, got_even)
    before = jnp.where(odd, got_even, got_odd)
    return jnp.where(index == count - 1, 0.0, after), jnp.where(index == 0, 0.0, before)


def shifts_x(field, east, west):
    row = row_ids()
    return (
        jnp.where(row == 15, east, pltpu.roll(field, 15, 0)),
        jnp.where(row == 0, west, pltpu.roll(field, 1, 0)),
    )


def shifts_y(field, halo):
    lane = lane_ids(field.shape[0])
    return (
        jnp.where(lane == 127, halo, pltpu.roll(field, 127, 1)),
        jnp.where(lane == 0, halo, pltpu.roll(field, 1, 1)),
    )


def side_columns(after, before, first, last):
    lane = lane_ids(after.shape[0])
    return jnp.where(
        lane == 127,
        pltpu.roll(after, 127 - first, 1),
        jnp.where(lane == 0, pltpu.roll(before, (128 - last) % 128, 1), 0.0),
    )


def velocity_halo(counts, got):
    gx, gy = places()
    after_x, before_x = from_sides(got[0], got[1], gx, counts[0])
    after_y, before_y = from_sides(got[2], got[3], gy, counts[1])
    return after_x[0:1], before_x[15:16], side_columns(after_y, before_y, 0, 127)


def solve_kernel(
    counts, half_velocity, x_even, x_odd, y_even, y_odd, stress_in, angles_in, hardness_in, active_in,
    relaxed_out, zone_sum, rows_even, rows_odd, cols_even, cols_odd,
    relaxed, stress, angles, hardness, active, table_wide, table, sums_a, sums_b, strain, cols, sems, out_sems,
):
    blocks = hardness.shape[0] // grain_block
    gx, gy = places()

    def copies(i, kinds):
        part = pl.ds(i * grain_block, grain_block)
        every = (
            lambda: (active_in.at[:, part], active.at[:, part]),
            lambda: (stress_in.at[:, part], stress.at[:, part]),
            lambda: (angles_in.at[:, part], angles.at[:, part]),
            lambda: (hardness_in.at[part], hardness.at[part]),
        )
        return [pltpu.make_async_copy(*every[k](), sems.at[k, i]) for k in kinds]

    def out_copy(i):
        part = pl.ds(i * grain_block, grain_block)
        return pltpu.make_async_copy(relaxed.at[0:6, part], relaxed_out.at[:, part], out_sems.at[i])

    def count(group, sums):
        first = group * batch
        bits = [bit_rows([active[0, first + k], active[1, first + k]]) for k in range(batch)]
        sums[...] = jnp.dot(
            table[...], jnp.concatenate(bits, axis=1), preferred_element_type=jnp.float32
        )

    def update(group, sums):
        lane = lane_ids(8)
        for half in range(2):
            part = pl.ds(8 * half, 8)
            zone_strain = [strain[i, part] for i in range(5)]
            totals = [zone_sum[k, part] for k in range(3)]
            ends = [cols[c, part] for c in range(6)]
            for k in range(batch):
                g = group * batch + k
                lanes = slice(256 * k + 128 * half, 256 * k + 128 * half + 128)
                x, sample = grain_math(
                    [stress[c, g, part] for c in range(6)],
                    [angles[c, g, part] for c in range(3)],
                    hardness[g, part],
                    lambda e: sums[e * 8 : (e + 1) * 8, lanes],
                    zone_strain,
                )
                here = (lane == 2 * g) | (lane == 2 * g + 1)
                for c in range(6):
                    relaxed[c, g, part] = x[c]
                    ends[c] = jnp.where(here, pltpu.roll(x[c], 2 * g + 1, 1), ends[c])
                totals = [t + s for t, s in zip(totals, sample)]
            for k in range(3):
                zone_sum[k, part] = totals[k]
            for c in range(6):
                cols[c, part] = ends[c]

    for copy in copies(0, range(4)):
        copy.start()
    for copy in copies(1, range(4)):
        copy.start()
    fill_table(table_wide)
    table[...] = table_wide[...].astype(jnp.bfloat16)
    zone_sum[...] = jnp.zeros_like(zone_sum)
    cols[...] = jnp.zeros_like(cols)
    grads = []
    for k in range(2):
        u = half_velocity[k]
        east, west, halo = velocity_halo(counts, (x_even[k], x_odd[k], y_even[k], y_odd[k]))
        u_east, u_west = shifts_x(u, 0.5 * east, 0.5 * west)
        u_north, u_south = shifts_y(u, 0.5 * halo)
        grads.append((u_east - u_west, u_north - u_south))
    exx, eyy = grads[0][0], grads[1][1]
    exy = 0.5 * (grads[0][1] + grads[1][0])
    strain[0] = 2.0 * time_step * exx
    strain[1] = 2.0 * time_step * eyy
    strain[2] = 2.0 * time_step * exy
    strain[3] = 2.0 * time_step * (exx + eyy)
    strain[4] = lame_first * time_step * (exx + eyy)
    for i in range(2, blocks):
        for copy in copies(i, range(4)):
            copy.start()
    copies(0, [0])[0].wait()
    count(0, sums_a)

    def step(block, carry):
        for copy in copies(block, [1, 2, 3]):
            copy.wait()

        @pl.when(block < blocks - 1)
        def _():
            copies(block + 1, [0])[0].wait()

        group = block * 2
        count(group + 1, sums_b)
        update(group, sums_a)
        count(jnp.minimum(group + 2, blocks * 2 - 1), sums_a)
        update(group + 1, sums_b)
        out_copy(block).start()
        return carry

    lax.fori_loop(0, blocks, step, 0)

    n = relaxed.shape[1]
    flat = relaxed.reshape(7 * n * 16, 128)
    odd_x, odd_y = gx % 2 == 1, gy % 2 == 1
    for c in range(6):
        first = flat[pl.ds(c * n * 16, n, stride=16)]
        last = flat[pl.ds(c * n * 16 + 15, n, stride=16)]
        rows_even[c] = jnp.where(odd_x, first, last)
        rows_odd[c] = jnp.where(odd_x, last, first)
    low = lane_ids(16) % 2 == 0
    for c in range(3):
        one, other = cols[c], cols[c + 3]
        last = jnp.where(low, one, pltpu.roll(other, 1, 1))
        first = jnp.where(low, pltpu.roll(one, 127, 1), other)
        cols_even[c] = jnp.where(odd_y, first, last)
        cols_odd[c] = jnp.where(odd_y, last, first)
    for i in range(blocks):
        out_copy(i).wait()


def solve_grains(half_velocity, got, stress, angles, hardness, active):
    n = hardness.shape[0]
    in_hbm = pl.BlockSpec(memory_space=pltpu.HBM)
    return pl.pallas_call(
        functools.partial(solve_kernel, sizes()),
        grid=(1,),
        in_specs=[
            whole(2, 16, 128),
            *[whole(*g.shape) for g in got],
            *[in_hbm] * 4,
        ],
        out_specs=[
            in_hbm,
            whole(3, 16, 128),
            whole(6, n, 128),
            whole(6, n, 128),
            whole(3, 16, 128),
            whole(3, 16, 128),
        ],
        out_shape=[f32(6, n, 16, 128), f32(3, 16, 128), f32(6, n, 128), f32(6, n, 128)]
        + [f32(3, 16, 128)] * 2,
        scratch_shapes=[
            pltpu.VMEM((7, n, 16, 128), jnp.float32),
            pltpu.VMEM(stress.shape, jnp.float32),
            pltpu.VMEM(angles.shape, jnp.float32),
            pltpu.VMEM(hardness.shape, jnp.float32),
            pltpu.VMEM(active.shape, jnp.int32),
            pltpu.VMEM((8 * n_sums, 192), jnp.float32),
            pltpu.VMEM((8 * n_sums, 192), jnp.bfloat16),
            pltpu.VMEM((8 * n_sums, 256 * batch), jnp.float32),
            pltpu.VMEM((8 * n_sums, 256 * batch), jnp.float32),
            pltpu.VMEM((5, 16, 128), jnp.float32),
            pltpu.VMEM((6, 16, 128), jnp.float32),
            pltpu.SemaphoreType.DMA((4, n // grain_block)),
            pltpu.SemaphoreType.DMA((n // grain_block,)),
        ],
        compiler_params=pltpu.CompilerParams(vmem_limit_bytes=53 * 2**20),
        cost_estimate=pl.CostEstimate(flops=10**8, bytes_accessed=10**7, transcendentals=0),
    )(half_velocity, *got, stress, angles, hardness, active)


def zone_update(counts, velocity, fields, u_got, stress, s_got, tall, moved, velocity_out):
    gx, gy = places()
    sx_even, sx_odd, sy_even, sy_odd = s_got
    s_east, s_west = from_sides(sx_even, sx_odd, gx, counts[0])
    s_north, s_south = from_sides(sy_even, sy_odd, gy, counts[1])
    for c in range(3):
        tall[c, 0:2] = s_west[2 * c : 2 * c + 2]
        tall[c, 2:18] = stress[c]
        tall[c, 18:20] = s_east[2 * c : 2 * c + 2]
    near = [side_columns(s_north, s_south, 4 * c + 2, 4 * c + 1) for c in range(3)]
    far = [side_columns(s_north, s_south, 4 * c + 3, 4 * c) for c in range(3)]
    lane = lane_ids(16)
    sign = jnp.where(lane == 127, 0.5, -0.5)

    def x_diff(c):
        return (tall[c, 2:20] - tall[c, 0:18]) * 0.5

    def y_diff(c):
        after, before = shifts_y(tall[c, 1:19], near[c][:18])
        return (after - before) * 0.5

    def rim_x(c):
        return (near[c][2:18] - near[c][0:16]) * 0.5

    def rim_y(c):
        return (far[c][1:17] - stress[c]) * sign

    force = [x_diff(0) + y_diff(2), x_diff(2) + y_diff(1)]
    rim_force = [rim_x(0) + rim_y(2), rim_x(2) + rim_y(1)]
    field_rim = [
        side_columns(s_north[:16], s_south[:16], 13 + 2 * k, 12 + 2 * k) for k in range(3)
    ]
    sides = [velocity_halo(counts, [got[k] for got in u_got]) for k in range(2)]

    def high(k):
        return jnp.concatenate([s_west[6 + k : 7 + k], fields[k], s_east[6 + k : 7 + k]], axis=0)

    mass = time_step * high(0)
    rim = []
    for k in range(2):
        east, west, halo = sides[k]
        moved[k, 0:18] = jnp.concatenate([west, velocity[k], east], axis=0) + mass * force[k]
        rim.append(halo + time_step * field_rim[0] * rim_force[k])
    frac_x = time_step * 0.5 * (moved[0, 0:17] + moved[0, 1:18])
    x_self = frac_x * high(1)[:17]
    x_next = frac_x - x_self
    own = [moved[k, 1:17] for k in range(2)]
    y_sides = [shifts_y(own[k], rim[k]) for k in range(2)]
    frac_y = time_step * 0.5 * (own[1] + y_sides[1][0])
    frac_before = time_step * 0.5 * (own[1] + y_sides[1][1])
    flag = fields[2]
    flag_before = jnp.where(lane == 0, field_rim[2], pltpu.roll(flag, 1, 1))
    y_self, before_self = frac_y * flag, frac_before * flag_before
    y_next, before_next = frac_y - y_self, frac_before - before_self
    centre = 1.0 - x_self[1:17] + x_next[0:16] - y_self + before_next
    coefs = (centre, -x_next[1:17], x_self[0:16], -y_next, before_self)
    for k in range(2):
        velocity_out[k] = (
            centre * own[k]
            + coefs[1] * moved[k, 2:18]
            + coefs[2] * moved[k, 0:16]
            + coefs[3] * y_sides[k][0]
            + coefs[4] * y_sides[k][1]
        )
    return coefs


def remap_kernel(
    counts, velocity, fields, ux_even, ux_odd, uy_even, uy_odd, stress, sx_even, sx_odd, y_odd, y_even,
    relaxed_in, rows_even, rows_odd,
    out, velocity_out, relaxed, tall, moved, coefs, rows, cols, sems,
):
    block = pl.program_id(0)
    size = out.shape[1]
    gx, gy = places()
    odd_x = gx % 2 == 1

    def copy(i):
        part = pl.ds(i * size, size)
        return pltpu.make_async_copy(relaxed_in.at[:, part], relaxed.at[:, part], sems.at[i])

    @pl.when(block == 0)
    def _():
        for i in range(relaxed.shape[1] // size):
            copy(i).start()

    rows[0, :, :size] = jnp.where(odd_x, rows_odd[...], rows_even[...])
    rows[1, :, :size] = jnp.where(odd_x, rows_even[...], rows_odd[...])
    lane, row = lane_ids(16), row_ids()

    @pl.when(block == 0)
    def _():
        fresh = zone_update(
            counts,
            velocity,
            fields,
            (ux_even, ux_odd, uy_even, uy_odd),
            stress,
            (sx_even[...], sx_odd[...], y_even[48:72], y_odd[48:72]),
            tall,
            moved,
            velocity_out,
        )
        centre, east, west, north, south = fresh
        coefs[0] = centre
        coefs[1] = jnp.where(row == 15, 0.0, east)
        coefs[2] = jnp.where(row == 0, 0.0, west)
        coefs[3] = jnp.where(lane == 127, 0.0, north)
        coefs[4] = jnp.where(lane == 0, 0.0, south)
        coefs[5] = jnp.where((row == 15) & (gx < counts[0] - 1), east, 0.0)
        coefs[6] = jnp.where((row == 0) & (gx > 0), west, 0.0)
        rim = jnp.where((lane == 127) & (gy < counts[1] - 1), north, 0.0)
        coefs[7] = jnp.where((lane == 0) & (gy > 0), south, rim)
        odd_y = gy % 2 == 1
        for c in range(3):
            part = slice(16 * c, 16 * c + 16)
            got_even, got_odd = y_even[part], y_odd[part]
            after = jnp.where(odd_y, got_odd, got_even)
            before = jnp.where(odd_y, got_even, got_odd)
            cols[c] = jnp.where(lane % 2 == 0, after, pltpu.roll(before, 1, 1))
            cols[c + 3] = jnp.where(lane % 2 == 0, pltpu.roll(after, 127, 1), before)

    centre, east, west, north, south, _, _, rim = [coefs[i] for i in range(8)]
    high_east, low_west = coefs[5, 8:16], coefs[6, 0:8]
    copy(block).wait()

    def one(g):
        for c in range(6):
            q = relaxed[c, block * size + g]
            halo = pltpu.roll(cols[c], 127 - 2 * (block * size + g), 1)
            total = centre * q + north * pltpu.roll(q, 127, 1) + south * pltpu.roll(q, 1, 1)
            total = total + rim * halo
            total = total + east * pltpu.roll(q, 15, 0) + west * pltpu.roll(q, 1, 0)
            out[c, g, 0:8] = total[:8] + low_west * rows[1, c, pl.ds(g, 1), :]
            out[c, g, 8:16] = total[8:] + high_east * rows[0, c, pl.ds(g, 1), :]

    def some(i, carry):
        for k in range(16):
            one(i * 16 + k)
        return carry

    lax.fori_loop(0, size // 16, some, 0)


def remap_grains(velocity, fields, u_got, stress, s_got, y_got, relaxed, rows_even, rows_odd):
    n = relaxed.shape[1]
    size = 16
    small = (velocity, fields, *u_got, stress, *s_got, *y_got)
    return pl.pallas_call(
        functools.partial(remap_kernel, sizes()),
        grid=(n // size,),
        in_specs=[
            *[whole(*a.shape) for a in small],
            pl.BlockSpec(memory_space=pltpu.HBM),
            pl.BlockSpec((6, size, 128), lambda i: (0, i, 0)),
            pl.BlockSpec((6, size, 128), lambda i: (0, i, 0)),
        ],
        out_specs=[
            pl.BlockSpec((6, size, 16, 128), lambda i: (0, i, 0, 0)),
            whole(2, 16, 128),
        ],
        out_shape=[f32(*relaxed.shape), f32(2, 16, 128)],
        scratch_shapes=[
            pltpu.VMEM(relaxed.shape, jnp.float32),
            pltpu.VMEM((3, 32, 128), jnp.float32),
            pltpu.VMEM((2, 32, 128), jnp.float32),
            pltpu.VMEM((8, 16, 128), jnp.float32),
            pltpu.VMEM((2, 6, size + 8, 128), jnp.float32),
            pltpu.VMEM((6, 16, 128), jnp.float32),
            pltpu.SemaphoreType.DMA((n // size,)),
        ],
        compiler_params=pltpu.CompilerParams(vmem_limit_bytes=53 * 2**20),
        cost_estimate=pl.CostEstimate(flops=10**7, bytes_accessed=10**7, transcendentals=0),
    )(*small, relaxed, rows_even, rows_odd)


def swap_even(block, axis):
    return lax.ppermute(block, axis, [(i, i ^ 1) for i in range(lax.axis_size(axis))])


def swap_odd_y(block):
    count_x, count_y = sizes()
    pairs = []
    for x in range(count_x):
        for y in range(count_y):
            end = y in (0, count_y - 1)
            to_x, to_y = (x ^ 1, y) if end else (x, y + 1 if y % 2 else y - 1)
            pairs.append((x * count_y + y, to_x * count_y + to_y))
    return lax.ppermute(block, ("gx", "gy"), pairs)


def swap_odd_x(block, crossed):
    count = lax.axis_size("gx")
    pairs = []
    for x in range(count):
        for a in range(2):
            end = x in (0, count - 1)
            to_x = x if end else (x + 1 if x % 2 else x - 1)
            to_a = 1 - a if end or crossed else a
            pairs.append((x * 2 + a, to_x * 2 + to_a))
    return lax.ppermute(block, ("gx", "ga"), pairs)


def per_device(velocity, density, grain_stress, grain_angles, hardness, active, donor_faces):
    gx = lax.axis_index("gx")
    odd_x = gx % 2 == 1
    u_got = (
        swap_even(velocity, "gx"),
        swap_odd_x(velocity, True),
        swap_even(velocity, "gy"),
        swap_odd_y(velocity),
    )
    relaxed, part, rows_even, rows_odd, cols_even, cols_odd = solve_grains(
        0.5 * velocity, u_got, grain_stress, grain_angles, hardness, active
    )
    density, donor_faces, part = lax.optimization_barrier((density, donor_faces, part))
    fields = jnp.concatenate([(1.0 / density)[None], donor_faces.astype(jnp.float32)], axis=0)
    zone_stress = (part + swap_even(part, "ga")) * (1.0 / G)
    zone_stress, rows_even, rows_odd = lax.optimization_barrier((zone_stress, rows_even, rows_odd))
    far_rows_odd = swap_odd_x(rows_odd, False)
    far_rows_even = swap_even(rows_even, "gx")
    spare = jnp.zeros((7, 128), jnp.float32)
    first = jnp.concatenate([zone_stress[:, :2].reshape(6, 128), fields[:, 0], spare], axis=0)
    last = jnp.concatenate([zone_stress[:, -2:].reshape(6, 128), fields[:, -1], spare], axis=0)
    got_even = swap_even(jnp.where(odd_x, first, last), "gx")
    got_odd = swap_odd_x(jnp.where(odd_x, last, first), True)
    east, west = from_sides(got_even[:6], got_odd[:6], gx, lax.axis_size("gx"))
    east, west = east.reshape(3, 2, 128), west.reshape(3, 2, 128)
    tall = jnp.concatenate([west[:, 1:], zone_stress, east[:, :1]], axis=1)
    lane = lax.broadcasted_iota(jnp.int32, (18, 128), 1)
    sides = jnp.zeros((18, 128), jnp.float32)
    for c in range(3):
        sides = jnp.where(lane // 4 == c, jnp.roll(tall[c], 4 * c + 2, axis=1), sides)
    sides = jnp.pad(sides, ((0, 6), (0, 0)))
    lane = lax.broadcasted_iota(jnp.int32, (16, 128), 1)
    field_sides = jnp.zeros((16, 128), jnp.float32)
    for k in range(3):
        field_sides = jnp.where(lane // 2 == 6 + k, jnp.roll(fields[k], 13 + 2 * k, axis=1), field_sides)
    sides = sides + jnp.pad(field_sides, ((0, 8), (0, 0)))
    y_odd = swap_odd_y(jnp.concatenate([cols_odd.reshape(48, 128), sides], axis=0))
    y_even = swap_even(jnp.concatenate([cols_even.reshape(48, 128), sides], axis=0), "gy")
    y_got = (y_odd, y_even)
    stress_out, velocity_out = remap_grains(
        velocity, fields, u_got, zone_stress, (got_even, got_odd), y_got, relaxed, far_rows_even, far_rows_odd
    )
    return (velocity_out, stress_out, zone_stress)


def solution(mesh):
    return jax.shard_map(
        per_device,
        mesh=mesh,
        in_specs=(
            P(None, "gx", "gy"),
            P("gx", "gy"),
            P(None, "ga", "gx", "gy"),
            P(None, "ga", "gx", "gy"),
            P("ga", "gx", "gy"),
            P(None, "ga", "gx", "gy"),
            P(None, "gx", "gy"),
        ),
        out_specs=(P(None, "gx", "gy"), P(None, "ga", "gx", "gy"), P(None, "gx", "gy")),
        check_vma=False,
    )
```
